256 devices in a mesh: patch: 64 (over y, z, core), grp: 4 (over x).
Axes of the slice: x: 4, y: 4, z: 8, core: 2. Of those that a mesh axis runs over, the one named last changes fastest.
Arguments:
- sky: bfloat16 [131072, 1024], P(('patch', 'grp')), may hold values from -24 to 24
- send_index: int32 [64, 4, 64, 32], P('patch', 'grp'), may hold values from 0 to 511, as said below
- send_count: int32 [64, 4, 64], P('patch', 'grp'), may hold values from 0 to 32, as said below
- taper: float32 [64, 4, 64, 32], P('patch', 'grp'), may hold values from 0.1 to 1
- start_basis: float32 [1024, 12], replicated, may hold values from -0.1875 to 0.1875
Outputs:
- cleaned_sky: float32 [131072, 1024], P(('patch', 'grp'))
The draws below stay inside these ranges and needn't reach their ends.
Inputs may be any that keep to these rules, and one draw needn't show every extreme that they name: `send_index`: within one list the first send_count entries are distinct. `send_count`: in every draw some patch receives 32 rows from every device.
All inputs are finite; a program needn't handle non-finite values.
Results may differ from the reference program's by a relative error of at most 0.0055.
Values may be sent and summed in bfloat16 or wider, within the bound.
A program may use at most 64 MiB of HBM per device.

```python
import math
import jax
import jax.numpy as jnp
from jax import lax

F = 1024
MODES = 12
ITERS = 6
STRIPE_DEV = 512
CAP = 32
PIX = 131072
N_PATCH = 64
N_GRP = 4


def layout(key):
    key_sizes, key_big, key_jitter, key_order = jax.random.split(key, 4)
    patch_sizes = jax.random.randint(key_sizes, (N_PATCH,), 1, 9)
    biggest = jax.random.randint(key_big, (), 0, N_PATCH)
    patch_sizes = jnp.where(jnp.arange(N_PATCH) == biggest, 8, patch_sizes)
    jitter = jax.random.randint(key_jitter, (N_PATCH, N_GRP, N_PATCH), 0, max(CAP // 4, 1))
    counts = jnp.minimum(CAP, patch_sizes[None, None, :] * CAP // 8 + jitter)
    scores = jax.random.randint(key_order, (N_PATCH, N_GRP, N_PATCH, STRIPE_DEV), 0, 2 ** 30 // STRIPE_DEV)
    scores = scores * STRIPE_DEV + jnp.arange(STRIPE_DEV)[None, None, None, :]
    ordering = jnp.argsort(scores, axis=-1, stable=True)
    return (ordering[..., :CAP].astype(jnp.int32), counts.astype(jnp.int32))


def draw_send_index(key, part):
    return layout(key)[0]


def draw_send_count(key, part):
    return layout(key)[1]


def draw_sky(key, part):
    key = jax.random.fold_in(key, 7)
    key_rows, key_chan, key_vals, key_amps = jax.random.split(key, 4)
    components = 16
    order = jnp.arange(components).astype(jnp.float32)
    strength = 3.2 * jnp.power(0.8, order)
    channel_pos = (jnp.arange(F).astype(jnp.float32) + 0.5) / F
    shapes = jnp.cos(math.pi * order[:, None] * channel_pos[None, :])
    row_scale = jnp.exp(jax.random.uniform(key_rows, (PIX, 1), jnp.float32, math.log(0.3), math.log(1.5)))
    channel_scale = jnp.exp(jax.random.uniform(key_chan, (1, F), jnp.float32, math.log(0.7), math.log(1.4)))
    noise = jnp.clip(jax.random.normal(key_vals, (PIX, F), jnp.float32), -3.0, 3.0)
    amps = jnp.clip(jax.random.normal(key_amps, (PIX, components), jnp.float32) * 0.58, -1.0, 1.0)
    foreground = jnp.zeros((PIX, F), jnp.float32)
    for index in range(components):
        foreground = foreground + amps[:, index:index + 1] * strength[index] * shapes[index][None, :]
    return (foreground + noise * row_scale * channel_scale).astype(jnp.bfloat16)


def levels(rng, shape, cuts, least, high):
    level = 1.0
    for axis_at, parts in cuts:
        draws = jax.random.uniform(jax.random.fold_in(jax.random.fold_in(rng, 6), axis_at), (parts,), jnp.float32, least / len(cuts), high / len(cuts))
        level = level * jnp.repeat(jnp.exp(draws), shape[axis_at] // parts).reshape((-1,) + (1,) * (len(shape) - 1 - axis_at))
    return level


def scatter_about(own_key, dims, deviation, limit, held_as=jnp.bfloat16):
    return jnp.clip(deviation * jax.random.normal(own_key, dims, jnp.float32), -limit, limit).astype(held_as)


def setup_inputs(seed: int = 0) -> dict:
    streams_of = jax.random.split(jax.random.key(seed), 6)
    return {
        "sky": draw_sky(jax.random.fold_in(streams_of[5], 71), 0),
        "send_index": draw_send_index(jax.random.fold_in(streams_of[5], 71), 0),
        "send_count": draw_send_count(jax.random.fold_in(streams_of[5], 71), 0),
        "taper": jnp.clip(0.1 + 0.9 * jax.random.uniform(streams_of[3], (N_PATCH, N_GRP, N_PATCH, CAP), jnp.float32) ** levels(streams_of[3], (N_PATCH, N_GRP, N_PATCH, CAP), ((0, 64), (1, 4)), -0.2, 0.2), 0.1, 1.0),
        "start_basis": scatter_about(streams_of[4], (F, MODES), F ** -0.5, 0.1875, jnp.float32),
    }


def orthonormal(matrix):
    columns = []
    for column_index in range(matrix.shape[1]):
        vector = matrix[:, column_index]
        for earlier in columns:
            vector = vector - jnp.sum(earlier * vector) * earlier
        vector = vector / jnp.sqrt(jnp.sum(vector * vector) + 1e-12)
        columns.append(vector)
    return jnp.stack(columns, axis=1)

def reference(sky, send_index, send_count, taper, start_basis):
    highest = lax.Precision.HIGHEST
    owners = ((jnp.arange(N_PATCH)[:, None] * N_GRP + jnp.arange(N_GRP)[None, :]) * STRIPE_DEV).astype(jnp.int32)
    slot_index = jnp.arange(CAP).astype(jnp.int32)

    def accumulate(carry, patch_index):
        numerator, weight_total = carry
        local_rows = send_index[:, :, patch_index, :].astype(jnp.int32)
        pixel_rows = (owners[:, :, None] + local_rows).reshape(-1)
        live_slots = (slot_index[None, None, :] < send_count[:, :, patch_index][:, :, None]).reshape(-1)
        gathered = jnp.where(live_slots[:, None], sky[pixel_rows], jnp.zeros((), sky.dtype))
        wide = gathered.astype(jnp.float32)
        gram_matrix = jnp.einsum('rf,rg->fg', wide, wide, precision=highest)
        subspace = start_basis
        for sweep in range(ITERS):
            subspace = orthonormal(jnp.dot(gram_matrix, subspace, precision=highest))
        basis_low = subspace.astype(jnp.bfloat16)
        coefficients = jnp.dot(gathered, basis_low, preferred_element_type=jnp.float32)
        cleaned = (wide - jnp.dot(coefficients, basis_low.astype(jnp.float32).T, precision=highest)).astype(jnp.bfloat16)
        weights = jnp.where(live_slots, taper[:, :, patch_index, :].reshape(-1), jnp.zeros((), taper.dtype))
        numerator = numerator.at[pixel_rows].add(weights[:, None] * cleaned.astype(jnp.float32))
        weight_total = weight_total.at[pixel_rows].add(weights)
        return ((numerator, weight_total), None)
    start = (jnp.zeros((PIX, F), jnp.float32), jnp.zeros((PIX,), jnp.float32))
    (numerator, weight_total), _ = lax.scan(accumulate, start, jnp.arange(N_PATCH).astype(jnp.int32))
    covered = weight_total > 0
    safe_total = jnp.where(covered, weight_total, jnp.ones((), jnp.float32))
    return jnp.where(covered[:, None], numerator / safe_total[:, None], sky.astype(jnp.float32))
```

```python
import jax
import jax.numpy as jnp
from jax import lax
from jax.experimental import pallas as pl
from jax.experimental.pallas import tpu as pltpu
from jax.sharding import Mesh, PartitionSpec as P

ITERS = 6
MODES = 12
SHARERS = 4
PAD = 16
CELL = ("y", "core", "x", "zl")
MESH = pl.DeviceIdType.MESH
MIB = 1 << 20


def two_pieces(value):
    high = value.astype(jnp.bfloat16).astype(jnp.float32)
    return jnp.concatenate([high, value - high], axis=0).astype(jnp.bfloat16)


def gather_kernel(index_ref, count_ref, sky_ref, out_ref, column_ref):
    capacity, patches = index_ref.shape
    step = pl.program_id(0)

    @pl.when(step == 0)
    def _():
        slot = lax.broadcasted_iota(jnp.int32, (capacity, patches), 0)
        index = jnp.where(slot < count_ref[...], index_ref[...], -1)
        for d in range(patches):
            column_ref[capacity * d : capacity * (d + 1), :] = jnp.broadcast_to(index[:, d : d + 1], (capacity, 128))

    column = column_ref[pl.ds(pl.multiple_of(step * 128, 128), 128), :]
    lane = lax.broadcasted_iota(jnp.int32, (128, 128), 1)
    pieces = [(column == lane + 128 * t) for t in range(sky_ref.shape[0] // 128)]
    pick = jnp.concatenate([jnp.where(p, 1.0, 0.0) for p in pieces], axis=1).astype(jnp.bfloat16)
    out_ref[...] = jnp.dot(pick, sky_ref[...], preferred_element_type=jnp.float32).astype(jnp.bfloat16)


def gather_rows(index, count, sky):
    slots = index.shape[0] * index.shape[1]
    channels = sky.shape[1]
    whole = lambda a: pl.BlockSpec(a.shape, lambda i: (0, 0))
    return pl.pallas_call(
        gather_kernel,
        grid=(slots // 128,),
        out_shape=jax.ShapeDtypeStruct((slots, channels), jnp.bfloat16),
        in_specs=[whole(index), whole(count), whole(sky)],
        out_specs=pl.BlockSpec((128, channels), lambda i: (i, 0)),
        scratch_shapes=[pltpu.VMEM((slots, 128), jnp.int32)],
        compiler_params=pltpu.CompilerParams(vmem_limit_bytes=24 * MIB),
    )(index, count, sky)


def gram_kernel(x_ref, out_ref):
    width = out_ref.shape[1]
    start = pl.multiple_of(pl.program_id(0) * width, width)
    gram = lax.dot_general(
        x_ref[:, pl.ds(start, width)], x_ref[...], (((0,), (0,)), ((), ())), preferred_element_type=jnp.float32
    )
    high = gram.astype(jnp.bfloat16)
    out_ref[0] = high
    out_ref[1] = (gram - high.astype(jnp.float32)).astype(jnp.bfloat16)


def grams(x):
    rows, channels = x.shape
    width = 256
    return pl.pallas_call(
        gram_kernel,
        grid=(channels // width,),
        out_shape=jax.ShapeDtypeStruct((2, channels, channels), jnp.bfloat16),
        in_specs=[pl.BlockSpec((rows, channels), lambda t: (0, 0))],
        out_specs=pl.BlockSpec((2, width, channels), lambda t: (0, t, 0)),
        compiler_params=pltpu.CompilerParams(vmem_limit_bytes=32 * MIB),
    )(x)


def orthonormal_rows(v):
    row = lax.broadcasted_iota(jnp.int32, (MODES, 1), 0)
    norms = jnp.zeros((MODES, 1), jnp.float32)
    for k in range(MODES):
        lead = v[k : k + 1]
        dots = jnp.sum(v * lead, axis=1, keepdims=True)
        norms = jnp.where(row == k, dots, norms)
        if k + 1 < MODES:
            v = v - jnp.where(row > k, dots / (dots[k : k + 1] + 1e-12), 0.0) * lead
    return v / jnp.sqrt(norms + 1e-12)


def stacked(z, folds):
    width = z.shape[1] // folds
    return jnp.concatenate([z[:, width * f : width * (f + 1)] for f in range(folds)], axis=0)


def unstacked(z, folds):
    return jnp.concatenate([z[MODES * f : MODES * (f + 1)] for f in range(folds)], axis=1)


def sweep_kernel(gram_ref, q0_ref, out_ref, q_ref, exact, short, x_send, x_recv, s_send, s_recv):
    me = lax.axis_index("zp")
    barrier = pltpu.get_barrier_semaphore()
    for o in range(1, SHARERS):
        pl.semaphore_signal(barrier, inc=1, device_id={"zp": lax.rem(me + o, SHARERS)}, device_id_type=MESH)
    pl.semaphore_wait(barrier, SHARERS - 1)

    q_ref[...] = q0_ref[...]

    def partial():
        lhs = two_pieces(q_ref[...])
        z = jnp.dot(jnp.concatenate([lhs, lhs], axis=1), gram_ref[...], preferred_element_type=jnp.float32)
        return z[:MODES] + z[MODES:]

    def exchange(box, send_sem, recv_sem):
        copies = [
            pltpu.make_async_remote_copy(
                src_ref=box.at[me],
                dst_ref=box.at[me],
                send_sem=send_sem.at[o],
                recv_sem=recv_sem.at[o],
                device_id={"zp": lax.rem(me + o, SHARERS)},
                device_id_type=MESH,
            )
            for o in range(1, SHARERS)
        ]
        for each in copies:
            each.start()
        for each in copies:
            each.wait()
        total = box[0].astype(jnp.float32)
        for k in range(1, SHARERS):
            total = total + box[k].astype(jnp.float32)
        return total

    def sweep(step, wide):
        folds, box, sems = (2, exact, (x_send, x_recv)) if wide else (4, short, (s_send, s_recv))
        slot = lax.rem(step, 2)
        box = box.at[slot]
        box[me] = stacked(partial(), folds).astype(box.dtype)
        total = exchange(box, sems[0].at[slot], sems[1].at[slot])
        q_ref[...] = orthonormal_rows(unstacked(total, folds))

    def loop(first, last, wide):
        def body(step, carry):
            sweep(step, wide)
            return carry

        lax.fori_loop(first, last, body, 0)

    loop(0, 2, True)
    loop(2, ITERS - 1, False)
    loop(ITERS - 1, ITERS, True)
    q = q_ref[...]
    channels = q.shape[1]
    q = jnp.concatenate([q, jnp.zeros((PAD - MODES, channels), jnp.float32)], axis=0).astype(jnp.bfloat16)
    out_ref[0] = q[:, : channels // 2]
    out_ref[1] = q[:, channels // 2 :]


def sweeps(gram, q0):
    channels = q0.shape[1]
    vmem = pl.BlockSpec(memory_space=pltpu.VMEM)
    return pl.pallas_call(
        sweep_kernel,
        out_shape=jax.ShapeDtypeStruct((2, PAD, channels // 2), jnp.bfloat16),
        in_specs=[vmem, vmem],
        out_specs=vmem,
        scratch_shapes=[
            pltpu.VMEM((MODES, channels), jnp.float32),
            pltpu.VMEM((2, SHARERS, 2 * MODES, channels // 2), jnp.float32),
            pltpu.VMEM((2, SHARERS, 4 * MODES, channels // 4), jnp.bfloat16),
            pltpu.SemaphoreType.DMA((2, SHARERS)),
            pltpu.SemaphoreType.DMA((2, SHARERS)),
            pltpu.SemaphoreType.DMA((2, SHARERS)),
            pltpu.SemaphoreType.DMA((2, SHARERS)),
        ],
        compiler_params=pltpu.CompilerParams(
            collective_id=0, has_side_effects=True, vmem_limit_bytes=40 * MIB
        ),
    )(gram, q0)


def share_kernel(b_ref, out_ref, a_send, a_recv, r_send, r_recv, s_send, s_recv):
    y, c, x, zl = (lax.axis_index(name) for name in CELL)
    barrier = pltpu.get_barrier_semaphore()
    ring = lambda at, o: lax.rem(at + o, 4)
    for o in range(1, 4):
        pl.semaphore_signal(barrier, inc=1, device_id={"x": ring(x, o)}, device_id_type=MESH)
        pl.semaphore_signal(barrier, inc=1, device_id={"y": ring(y, o)}, device_id_type=MESH)
    pl.semaphore_signal(barrier, inc=1, device_id={"core": 1 - c}, device_id_type=MESH)
    pl.semaphore_signal(barrier, inc=1, device_id={"zl": 1 - zl}, device_id_type=MESH)
    pl.semaphore_wait(barrier, 8)

    def copy(src, dst, sems, at, to):
        return pltpu.make_async_remote_copy(
            src_ref=src, dst_ref=dst, send_sem=sems[0].at[at], recv_sem=sems[1].at[at],
            device_id=to, device_id_type=MESH,
        )

    near, far, across = (a_send, a_recv), (r_send, r_recv), (s_send, s_recv)
    pair = []
    for h in range(2):
        pair.append(copy(b_ref.at[h], out_ref.at[h, y, c, x, zl], near, 6 + h, {"zl": 1 - zl}))
        pair[h].start()
        out_ref[h, y, c, x, zl] = b_ref[h]
    blocks = [out_ref.at[h, y, c, x] for h in range(2)]
    own = [
        [copy(blocks[0], blocks[0], near, o - 1, {"x": ring(x, o)}) for o in range(1, 4)],
        [copy(blocks[1], blocks[1], near, 2 + o, {"y": ring(y, o)}) for o in range(1, 4)],
    ]
    for h in range(2):
        pair[h].wait_recv()
        for each in own[h]:
            each.start()
    lines = [out_ref.at[0, y, c], out_ref.at[1, :, c, x]]
    sibling = {"core": 1 - c}
    started = pair + own[0] + own[1]
    passed = [[], []]
    crossed = []
    for h, axis in ((0, "y"), (1, "x")):
        at = y if h == 0 else x
        for o in range(3):
            own[h][o].wait_recv()
        for o in range(1, 4):
            passed[h].append(copy(lines[h], lines[h], far, 3 * h + o, {axis: ring(at, o)}))
            passed[h][-1].start()
        crossed.append(copy(lines[h], lines[h], across, 4 * h, sibling))
        crossed[-1].start()
    for o in range(1, 4):
        for h in range(2):
            passed[h][o - 1].wait_recv()
            line = out_ref.at[0, ring(y, 4 - o), c] if h == 0 else out_ref.at[1, :, c, ring(x, 4 - o)]
            crossed.append(copy(line, line, across, 4 * h + o, sibling))
            crossed[-1].start()
    for each in crossed:
        each.wait_recv()
    for each in started + passed[0] + passed[1] + crossed:
        each.wait_send()


def share(basis):
    halves, rows, width = basis.shape
    vmem = pl.BlockSpec(memory_space=pltpu.VMEM)
    return pl.pallas_call(
        share_kernel,
        out_shape=jax.ShapeDtypeStruct((halves, 4, 2, 4, 2, rows, width), jnp.bfloat16),
        in_specs=[vmem],
        out_specs=vmem,
        scratch_shapes=[pltpu.SemaphoreType.DMA((8,))] * 6,
        compiler_params=pltpu.CompilerParams(
            collective_id=1, has_side_effects=True, vmem_limit_bytes=24 * MIB
        ),
    )(basis)


def blend_kernel(index_ref, count_ref, taper_ref, sky_ref, basis_ref, out_ref):
    rows = sky_ref.shape[0]
    capacity, patches = index_ref.shape
    halves, columns, width = basis_ref.shape
    slot = lax.broadcasted_iota(jnp.int32, (capacity, patches), 0)
    index = jnp.where(slot < count_ref[...], index_ref[...], -1)
    pixel = pl.program_id(0) * rows + lax.broadcasted_iota(jnp.int32, (rows, patches), 0)
    weights = jnp.zeros((rows, patches), jnp.float32)
    for j in range(capacity):
        weights = weights + jnp.where(index[j : j + 1, :] == pixel, taper_ref[j : j + 1, :], 0.0)
    total = jnp.sum(weights, axis=1, keepdims=True)
    weights = weights / jnp.where(total > 0, total, 1.0)
    high = weights.astype(jnp.bfloat16).astype(jnp.float32)
    pieces = jnp.concatenate([high, weights - high], axis=1).astype(jnp.bfloat16)
    patch = lax.broadcasted_iota(jnp.int32, (2 * patches, columns), 0)
    offset = lax.broadcasted_iota(jnp.int32, (2 * patches, columns), 1) - PAD * jnp.where(
        patch < patches, patch, patch - patches
    )
    spread = jnp.where((offset >= 0) & (offset < PAD), 1.0, 0.0).astype(jnp.bfloat16)
    spread = jnp.dot(pieces, spread, preferred_element_type=jnp.float32)
    coefficients = sum(
        lax.dot_general(
            sky_ref[:, width * h : width * (h + 1)],
            basis_ref[h],
            (((1,), (1,)), ((), ())),
            preferred_element_type=jnp.float32,
        )
        for h in range(halves)
    )
    amounts = two_pieces(spread * coefficients)
    for h in range(halves):
        taken = jnp.dot(amounts, basis_ref[h], preferred_element_type=jnp.float32)
        part = slice(width * h, width * (h + 1))
        out_ref[:, part] = sky_ref[:, part].astype(jnp.float32) - (taken[:rows] + taken[rows:])


def blend(index, count, taper, sky, basis):
    pixels, channels = sky.shape
    rows = 128
    whole = lambda a: pl.BlockSpec(a.shape, lambda i: (0,) * a.ndim)
    return pl.pallas_call(
        blend_kernel,
        grid=(pixels // rows,),
        out_shape=jax.ShapeDtypeStruct((pixels, channels), jnp.float32),
        in_specs=[
            whole(index),
            whole(count),
            whole(taper),
            pl.BlockSpec((rows, channels), lambda i: (i, 0)),
            whole(basis),
        ],
        out_specs=pl.BlockSpec((rows, channels), lambda i: (i, 0)),
        compiler_params=pltpu.CompilerParams(vmem_limit_bytes=32 * MIB),
    )(index, count, taper, sky, basis)


def local(sky, send_index, send_count, taper, start_basis):
    patches, capacity = send_index.shape[2:]
    channels = sky.shape[1]
    index = send_index.reshape(patches, capacity).T
    count = send_count.reshape(1, patches)
    weight = taper.reshape(patches, capacity).T
    outgoing = gather_rows(index, count, sky)
    x = lax.all_to_all(outgoing.reshape(patches, capacity, channels), CELL, 0, 0, tiled=True)
    basis = sweeps(grams(x.reshape(-1, channels)).reshape(2 * channels, channels), start_basis.T)
    bases = share(basis)
    return blend(index, count, weight, sky, bases.reshape(2, patches * PAD, channels // 2))


def solution(mesh):
    fine = Mesh(mesh.devices.reshape(4, SHARERS, 2, 2, 4), ("y", "zp", "zl", "core", "x"))
    patch = ("y", "zp", "zl", "core")
    rows = P((*patch, "x"), None)
    placed = (rows, P(patch, "x", None, None), P(patch, "x", None), P(patch, "x", None, None), P())
    return jax.shard_map(local, mesh=fine, in_specs=placed, out_specs=rows, check_vma=False)
```

```python
import jax
import jax.numpy as jnp
from jax import lax
from jax.experimental import pallas as pl
from jax.experimental.pallas import tpu as pltpu
from jax.sharding import Mesh, PartitionSpec as P

ITERS = 6
MODES = 12
SHARERS = 4
PAD = 16
CELL = ("y", "core", "x", "zl")
MESH = pl.DeviceIdType.MESH
MIB = 1 << 20


def two_pieces(value):
    high = value.astype(jnp.bfloat16).astype(jnp.float32)
    return jnp.concatenate([high, value - high], axis=0).astype(jnp.bfloat16)


def collect_kernel(
    index_ref, count_ref, taper_ref, sky_ref, gram_ref, weight_ref, column, rows, inbox, total, send_sem, recv_sem
):
    y, c, x, zl = (lax.axis_index(name) for name in CELL)
    capacity, patches = index_ref.shape
    pixels, channels = sky_ref.shape

    def peer(r):
        o = lax.rem(r * 37, patches)
        to = {
            "x": lax.rem(x + lax.rem(o, 4), 4),
            "y": lax.rem(y + lax.rem(lax.div(o, 4), 4), 4),
            "core": lax.rem(c + lax.rem(lax.div(o, 16), 2), 2),
            "zl": lax.rem(zl + lax.div(o, 32), 2),
        }
        return to, ((to["y"] * 2 + to["core"]) * 4 + to["x"]) * 2 + to["zl"]

    def copy(r):
        return pltpu.make_async_remote_copy(
            src_ref=rows.at[r],
            dst_ref=inbox.at[r],
            send_sem=send_sem.at[r],
            recv_sem=recv_sem.at[r],
            device_id=peer(r)[0],
            device_id_type=MESH,
        )

    def each(first, last, step):
        def body(i, carry):
            step(i)
            return carry

        lax.fori_loop(first, last, body, 0)

    barrier = pltpu.get_barrier_semaphore()
    each(1, patches, lambda r: pl.semaphore_signal(barrier, inc=1, device_id=peer(r)[0], device_id_type=MESH))

    slot = lax.broadcasted_iota(jnp.int32, (capacity, patches), 0)
    index = jnp.where(slot < count_ref[...], index_ref[...], -1)
    for d in range(patches):
        column[d] = jnp.broadcast_to(index[:, d : d + 1], (capacity, 128))
    lane = lax.broadcasted_iota(jnp.int32, (4 * capacity, 128), 1)

    def pick(block):
        near = jnp.concatenate([column[peer(4 * block + j)[1]] for j in range(4)], axis=0)
        hot = [jnp.where(near == lane + 128 * t, 1.0, 0.0) for t in range(pixels // 128)]
        hot = jnp.concatenate(hot, axis=1).astype(jnp.bfloat16)
        found = jnp.dot(hot, sky_ref[...], preferred_element_type=jnp.float32).astype(jnp.bfloat16)
        for j in range(4):
            rows[4 * block + j] = found[capacity * j : capacity * (j + 1)]

    pick(0)
    pl.semaphore_wait(barrier, patches - 1)
    for j in range(1, 4):
        copy(j).start()

    def send(block):
        pick(block)
        for j in range(4):
            copy(4 * block + j).start()

    each(1, patches // 4, send)
    inbox[0] = rows[0]

    for part in range(pixels // 128):
        pixel = 128 * part + lax.broadcasted_iota(jnp.int32, (128, patches), 0)
        weights = jnp.zeros((128, patches), jnp.float32)
        for j in range(capacity):
            weights = weights + jnp.where(index[j : j + 1, :] == pixel, taper_ref[j : j + 1, :], 0.0)
        whole = jnp.sum(weights, axis=1, keepdims=True)
        weights = weights / jnp.where(whole > 0, whole, 1.0)
        high = weights.astype(jnp.bfloat16).astype(jnp.float32)
        weight_ref[128 * part : 128 * (part + 1), :] = jnp.concatenate([high, weights - high], axis=1).astype(
            jnp.bfloat16
        )

    total[...] = jnp.zeros_like(total)
    width = 256

    def add(group):
        each(jnp.maximum(8 * group, 1), 8 * group + 8, lambda r: copy(r).wait_recv())
        block = inbox[pl.ds(8 * group, 8)].reshape(8 * capacity, channels)
        for t in range(channels // width):
            part = slice(width * t, width * (t + 1))
            total[part, :] += lax.dot_general(
                block[:, part], block, (((0,), (0,)), ((), ())), preferred_element_type=jnp.float32
            )

    each(0, patches // 8, add)
    for t in range(channels // width):
        part = slice(width * t, width * (t + 1))
        high = total[part, :].astype(jnp.bfloat16)
        gram_ref[part, :] = high
        gram_ref[channels + width * t : channels + width * (t + 1), :] = (
            total[part, :] - high.astype(jnp.float32)
        ).astype(jnp.bfloat16)
    each(1, patches, lambda r: copy(r).wait_send())


def collect(index, count, taper, sky):
    capacity, patches = index.shape
    pixels, channels = sky.shape
    vmem = pl.BlockSpec(memory_space=pltpu.VMEM)
    return pl.pallas_call(
        collect_kernel,
        out_shape=(
            jax.ShapeDtypeStruct((2 * channels, channels), jnp.bfloat16),
            jax.ShapeDtypeStruct((pixels, 2 * patches), jnp.bfloat16),
        ),
        in_specs=[vmem] * 4,
        out_specs=(vmem, vmem),
        scratch_shapes=[
            pltpu.VMEM((patches, capacity, 128), jnp.int32),
            pltpu.VMEM((patches, capacity, channels), jnp.bfloat16),
            pltpu.VMEM((patches, capacity, channels), jnp.bfloat16),
            pltpu.VMEM((channels, channels), jnp.float32),
            pltpu.SemaphoreType.DMA((patches,)),
            pltpu.SemaphoreType.DMA((patches,)),
        ],
        compiler_params=pltpu.CompilerParams(
            collective_id=1, has_side_effects=True, vmem_limit_bytes=40 * MIB
        ),
    )(index, count, taper, sky)


def orthonormal_rows(v):
    row = lax.broadcasted_iota(jnp.int32, (MODES, 1), 0)
    norms = jnp.zeros((MODES, 1), jnp.float32)
    for k in range(MODES):
        lead = v[k : k + 1]
        dots = jnp.sum(v * lead, axis=1, keepdims=True)
        norms = jnp.where(row == k, dots, norms)
        if k + 1 < MODES:
            v = v - jnp.where(row > k, dots / (dots[k : k + 1] + 1e-12), 0.0) * lead
    return v / jnp.sqrt(norms + 1e-12)


def stacked(z, folds):
    width = z.shape[1] // folds
    return jnp.concatenate([z[:, width * f : width * (f + 1)] for f in range(folds)], axis=0)


def unstacked(z, folds):
    return jnp.concatenate([z[MODES * f : MODES * (f + 1)] for f in range(folds)], axis=1)


def sweep_kernel(
    gram_ref, q0_ref, out_ref, q_ref, exact, short,
    x_send, x_recv, s_send, s_recv, n_send, n_recv, f_send, f_recv, c_send, c_recv,
):
    me = lax.axis_index("zp")
    y, c, x, zl = (lax.axis_index(name) for name in CELL)
    barrier = pltpu.get_barrier_semaphore()
    ring = lambda at, o: lax.rem(at + o, 4)
    for o in range(1, 4):
        for to in ({"zp": ring(me, o)}, {"x": ring(x, o)}, {"y": ring(y, o)}):
            pl.semaphore_signal(barrier, inc=1, device_id=to, device_id_type=MESH)
    for to in ({"core": 1 - c}, {"zl": 1 - zl}):
        pl.semaphore_signal(barrier, inc=1, device_id=to, device_id_type=MESH)
    pl.semaphore_wait(barrier, 11)

    q_ref[...] = q0_ref[...]

    def partial():
        lhs = two_pieces(q_ref[...])
        z = jnp.dot(jnp.concatenate([lhs, lhs], axis=1), gram_ref[...], preferred_element_type=jnp.float32)
        return z[:MODES] + z[MODES:]

    def exchange(box, send_sem, recv_sem):
        copies = [
            pltpu.make_async_remote_copy(
                src_ref=box.at[me],
                dst_ref=box.at[me],
                send_sem=send_sem.at[o],
                recv_sem=recv_sem.at[o],
                device_id={"zp": lax.rem(me + o, SHARERS)},
                device_id_type=MESH,
            )
            for o in range(1, SHARERS)
        ]
        for each in copies:
            each.start()
        for each in copies:
            each.wait()
        total = box[0].astype(jnp.float32)
        for k in range(1, SHARERS):
            total = total + box[k].astype(jnp.float32)
        return total

    def sweep(step, wide):
        folds, box, sems = (2, exact, (x_send, x_recv)) if wide else (4, short, (s_send, s_recv))
        slot = lax.rem(step, 2)
        box = box.at[slot]
        box[me] = stacked(partial(), folds).astype(box.dtype)
        total = exchange(box, sems[0].at[slot], sems[1].at[slot])
        q_ref[...] = orthonormal_rows(unstacked(total, folds))

    def loop(first, last, wide):
        def body(step, carry):
            sweep(step, wide)
            return carry

        lax.fori_loop(first, last, body, 0)

    loop(0, 2, True)
    loop(2, ITERS - 1, False)
    loop(ITERS - 1, ITERS, True)
    q = q_ref[...]
    channels = q.shape[1]
    width = channels // 2
    q = jnp.concatenate([q, jnp.zeros((PAD - MODES, channels), jnp.float32)], axis=0).astype(jnp.bfloat16)

    def copy(src, dst, sems, at, to):
        return pltpu.make_async_remote_copy(
            src_ref=src, dst_ref=dst, send_sem=sems[0].at[at], recv_sem=sems[1].at[at],
            device_id=to, device_id_type=MESH,
        )

    near, far, across = (n_send, n_recv), (f_send, f_recv), (c_send, c_recv)
    pair = []
    for h in range(2):
        out_ref[h, y, c, x, zl] = q[:, width * h : width * (h + 1)]
        block = out_ref.at[h, y, c, x, zl]
        pair.append(copy(block, block, near, 6 + h, {"zl": 1 - zl}))
        pair[h].start()
    blocks = [out_ref.at[h, y, c, x] for h in range(2)]
    own = [
        [copy(blocks[0], blocks[0], near, o - 1, {"x": ring(x, o)}) for o in range(1, 4)],
        [copy(blocks[1], blocks[1], near, 2 + o, {"y": ring(y, o)}) for o in range(1, 4)],
    ]
    for h in range(2):
        pair[h].wait_recv()
        for each in own[h]:
            each.start()
    lines = [out_ref.at[0, y, c], out_ref.at[1, :, c, x]]
    sibling = {"core": 1 - c}
    started = pair + own[0] + own[1]
    passed = [[], []]
    crossed = []
    for h, axis in ((0, "y"), (1, "x")):
        at = y if h == 0 else x
        for o in range(3):
            own[h][o].wait_recv()
        for o in range(1, 4):
            passed[h].append(copy(lines[h], lines[h], far, 3 * h + o, {axis: ring(at, o)}))
            passed[h][-1].start()
        crossed.append(copy(lines[h], lines[h], across, 4 * h, sibling))
        crossed[-1].start()
    for o in range(1, 4):
        for h in range(2):
            passed[h][o - 1].wait_recv()
            line = out_ref.at[0, ring(y, 4 - o), c] if h == 0 else out_ref.at[1, :, c, ring(x, 4 - o)]
            crossed.append(copy(line, line, across, 4 * h + o, sibling))
            crossed[-1].start()
    for each in crossed:
        each.wait_recv()
    for each in started + passed[0] + passed[1] + crossed:
        each.wait_send()


def sweeps(gram, q0):
    channels = q0.shape[1]
    vmem = pl.BlockSpec(memory_space=pltpu.VMEM)
    return pl.pallas_call(
        sweep_kernel,
        out_shape=jax.ShapeDtypeStruct((2, 4, 2, 4, 2, PAD, channels // 2), jnp.bfloat16),
        in_specs=[vmem, vmem],
        out_specs=vmem,
        scratch_shapes=[
            pltpu.VMEM((MODES, channels), jnp.float32),
            pltpu.VMEM((2, SHARERS, 2 * MODES, channels // 2), jnp.float32),
            pltpu.VMEM((2, SHARERS, 4 * MODES, channels // 4), jnp.bfloat16),
            *[pltpu.SemaphoreType.DMA((2, SHARERS))] * 4,
            *[pltpu.SemaphoreType.DMA((8,))] * 6,
        ],
        compiler_params=pltpu.CompilerParams(
            collective_id=0, has_side_effects=True, vmem_limit_bytes=40 * MIB
        ),
    )(gram, q0)


def blend_kernel(weight_ref, sky_ref, basis_ref, out_ref):
    rows = sky_ref.shape[0]
    pieces = weight_ref.shape[1]
    halves, columns, width = basis_ref.shape
    patch = lax.rem(lax.broadcasted_iota(jnp.int32, (pieces, columns), 0), pieces // 2)
    spread = patch == lax.div(lax.broadcasted_iota(jnp.int32, (pieces, columns), 1), PAD)
    spread = jnp.where(spread, 1.0, 0.0).astype(jnp.bfloat16)
    spread = jnp.dot(weight_ref[...], spread, preferred_element_type=jnp.float32)
    coefficients = sum(
        lax.dot_general(
            sky_ref[:, width * h : width * (h + 1)],
            basis_ref[h],
            (((1,), (1,)), ((), ())),
            preferred_element_type=jnp.float32,
        )
        for h in range(halves)
    )
    amounts = two_pieces(spread * coefficients)
    for h in range(halves):
        taken = jnp.dot(amounts, basis_ref[h], preferred_element_type=jnp.float32)
        part = slice(width * h, width * (h + 1))
        out_ref[:, part] = sky_ref[:, part].astype(jnp.float32) - (taken[:rows] + taken[rows:])


def blend(weight, sky, basis):
    pixels, channels = sky.shape
    rows = 256
    return pl.pallas_call(
        blend_kernel,
        grid=(pixels // rows,),
        out_shape=jax.ShapeDtypeStruct((pixels, channels), jnp.float32),
        in_specs=[
            pl.BlockSpec((rows, weight.shape[1]), lambda i: (i, 0)),
            pl.BlockSpec((rows, channels), lambda i: (i, 0)),
            pl.BlockSpec(basis.shape, lambda i: (0, 0, 0)),
        ],
        out_specs=pl.BlockSpec((rows, channels), lambda i: (i, 0)),
        compiler_params=pltpu.CompilerParams(vmem_limit_bytes=32 * MIB),
    )(weight, sky, basis)


def local(sky, send_index, send_count, taper, start_basis):
    patches, capacity = send_index.shape[2:]
    channels = sky.shape[1]
    index = send_index.reshape(patches, capacity).T
    count = send_count.reshape(1, patches)
    gram, weight = collect(index, count, taper.reshape(patches, capacity).T, sky)
    bases = sweeps(gram, start_basis.T)
    return blend(weight, sky, bases.reshape(2, patches * PAD, channels // 2))


def solution(mesh):
    fine = Mesh(mesh.devices.reshape(4, SHARERS, 2, 2, 4), ("y", "zp", "zl", "core", "x"))
    patch = ("y", "zp", "zl", "core")
    rows = P((*patch, "x"), None)
    placed = (rows, P(patch, "x", None, None), P(patch, "x", None), P(patch, "x", None, None), P())
    return jax.shard_map(local, mesh=fine, in_specs=placed, out_specs=rows, check_vma=False)
```

```python
import jax
import jax.numpy as jnp
from jax import lax
from jax.experimental import pallas as pl
from jax.experimental.pallas import tpu as pltpu
from jax.sharding import Mesh, PartitionSpec as P

ITERS = 6
MODES = 12
SHARERS = 4
PAD = 16
CELL = ("y", "core", "x", "zl")
MESH = pl.DeviceIdType.MESH
MIB = 1 << 20
VMEM_MIB = 56


def two_pieces(value):
    high = value.astype(jnp.bfloat16).astype(jnp.float32)
    return jnp.concatenate([high, value - high], axis=0).astype(jnp.bfloat16)


def orthonormal_rows(v):
    row = lax.broadcasted_iota(jnp.int32, (MODES, 1), 0)
    norms = jnp.zeros((MODES, 1), jnp.float32)
    for k in range(MODES):
        lead = v[k : k + 1]
        dots = jnp.sum(v * lead, axis=1, keepdims=True)
        norms = jnp.where(row == k, dots, norms)
        if k + 1 < MODES:
            v = v - jnp.where(row > k, dots / (dots[k : k + 1] + 1e-12), 0.0) * lead
    return v / jnp.sqrt(norms + 1e-12)


def stacked(z, folds):
    width = z.shape[1] // folds
    return jnp.concatenate([z[:, width * f : width * (f + 1)] for f in range(folds)], axis=0)


def unstacked(z, folds):
    return jnp.concatenate([z[MODES * f : MODES * (f + 1)] for f in range(folds)], axis=1)


def each(first, last, step):
    def body(i, carry):
        step(i)
        return carry

    lax.fori_loop(first, last, body, 0)


def ring(at, o):
    return lax.rem(at + o, 4)


def send_to(src, dst, send_sem, recv_sem, to):
    return pltpu.make_async_remote_copy(
        src_ref=src, dst_ref=dst, send_sem=send_sem, recv_sem=recv_sem, device_id=to, device_id_type=MESH
    )


def taken_kernel(
    index_hbm, count_hbm, taper_hbm, sky_hbm, q0_hbm, taken_ref,
    index_ref, count_ref, taper_ref, sky_ref, q_ref, bases, weight_ref, column, rows, inbox, total, gram_ref, exact, short,
    in_sem, row_send, row_recv, x_send, x_recv, s_send, s_recv,
    p_send, p_recv, a_send, a_recv, b_send, b_recv, c_send, c_recv,
):
    me = lax.axis_index("zp")
    y, c, x, zl = (lax.axis_index(name) for name in CELL)
    capacity, patches = index_ref.shape
    pixels, channels = sky_ref.shape

    sources = (index_hbm, count_hbm, sky_hbm, taper_hbm, q0_hbm)
    places = (index_ref, count_ref, sky_ref, taper_ref, q_ref)
    loads = [pltpu.make_async_copy(f, t, in_sem.at[i]) for i, (f, t) in enumerate(zip(sources, places))]
    for load in loads:
        load.start()

    def peer(r):
        o = lax.rem(r * 37, patches)
        to = {
            "x": ring(x, lax.rem(o, 4)),
            "y": ring(y, lax.rem(lax.div(o, 4), 4)),
            "core": lax.rem(c + lax.rem(lax.div(o, 16), 2), 2),
            "zl": lax.rem(zl + lax.div(o, 32), 2),
        }
        return to, ((to["y"] * 2 + to["core"]) * 4 + to["x"]) * 2 + to["zl"]

    def row_copy(r):
        return send_to(rows.at[r], inbox.at[r], row_send.at[r], row_recv.at[r], peer(r)[0])

    barrier = pltpu.get_barrier_semaphore()
    each(1, patches, lambda r: pl.semaphore_signal(barrier, inc=1, device_id=peer(r)[0], device_id_type=MESH))
    for o in range(1, SHARERS):
        pl.semaphore_signal(barrier, inc=1, device_id={"zp": ring(me, o)}, device_id_type=MESH)

    loads[0].wait()
    loads[1].wait()
    slot = lax.broadcasted_iota(jnp.int32, (capacity, patches), 0)
    index = jnp.where(slot < count_ref[...], index_ref[...], -1)
    for d in range(patches):
        column[d] = jnp.broadcast_to(index[:, d : d + 1], (capacity, 128))
    lane = lax.broadcasted_iota(jnp.int32, (4 * capacity, 128), 1)
    loads[2].wait()

    def pick(block):
        near = jnp.concatenate([column[peer(4 * block + j)[1]] for j in range(4)], axis=0)
        hot = [jnp.where(near == lane + 128 * t, 1.0, 0.0) for t in range(pixels // 128)]
        hot = jnp.concatenate(hot, axis=1).astype(jnp.bfloat16)
        found = jnp.dot(hot, sky_ref[...], preferred_element_type=jnp.float32).astype(jnp.bfloat16)
        for j in range(4):
            rows[4 * block + j] = found[capacity * j : capacity * (j + 1)]

    pick(0)
    pl.semaphore_wait(barrier, patches - 1 + SHARERS - 1)
    for j in range(1, 4):
        row_copy(j).start()

    def send(block):
        pick(block)
        for j in range(4):
            row_copy(4 * block + j).start()

    each(1, patches // 4, send)
    inbox[0] = rows[0]

    loads[3].wait()
    loads[4].wait()
    for part in range(pixels // 128):
        pixel = 128 * part + lax.broadcasted_iota(jnp.int32, (128, patches), 0)
        weights = jnp.zeros((128, patches), jnp.float32)
        for j in range(capacity):
            weights = weights + jnp.where(index[j : j + 1, :] == pixel, taper_ref[j : j + 1, :], 0.0)
        whole = jnp.sum(weights, axis=1, keepdims=True)
        weights = weights / jnp.where(whole > 0, whole, 1.0)
        high = weights.astype(jnp.bfloat16).astype(jnp.float32)
        weight_ref[128 * part : 128 * (part + 1), :] = jnp.concatenate([high, weights - high], axis=1).astype(
            jnp.bfloat16
        )

    total[...] = jnp.zeros_like(total)
    tile = 256

    def add(group):
        each(jnp.maximum(8 * group, 1), 8 * group + 8, lambda r: row_copy(r).wait_recv())
        block = inbox[pl.ds(8 * group, 8)].reshape(8 * capacity, channels)
        for t in range(channels // tile):
            part = slice(tile * t, tile * (t + 1))
            total[part, :] += lax.dot_general(
                block[:, part], block, (((0,), (0,)), ((), ())), preferred_element_type=jnp.float32
            )

    each(0, patches // 8, add)
    for t in range(channels // tile):
        part = slice(tile * t, tile * (t + 1))
        high = total[part, :].astype(jnp.bfloat16)
        gram_ref[part, :] = high
        gram_ref[channels + tile * t : channels + tile * (t + 1), :] = (
            total[part, :] - high.astype(jnp.float32)
        ).astype(jnp.bfloat16)

    width = channels // 2

    def sweep(step, wide):
        folds, box, sems = (2, exact, (x_send, x_recv)) if wide else (4, short, (s_send, s_recv))
        at = lax.rem(step, 2)
        box = box.at[at]
        lhs = two_pieces(q_ref[...])
        lhs = jnp.concatenate([lhs, lhs], axis=1)
        copies = []
        for h in range(2):
            z = jnp.dot(lhs, gram_ref[:, width * h : width * (h + 1)], preferred_element_type=jnp.float32)
            box[me, h] = stacked(z[:MODES] + z[MODES:], folds).astype(box.dtype)
            for o in (2, 1, 3):
                mine = box.at[me, h]
                copies.append(
                    send_to(mine, mine, sems[0].at[at, 4 * h + o], sems[1].at[at, 4 * h + o], {"zp": ring(me, o)})
                )
                copies[-1].start()
        for one in copies:
            one.wait_recv()
        halves = []
        for h in range(2):
            whole = box[0, h].astype(jnp.float32)
            for k in range(1, SHARERS):
                whole = whole + box[k, h].astype(jnp.float32)
            halves.append(unstacked(whole, folds))
        q_ref[...] = orthonormal_rows(jnp.concatenate(halves, axis=1))
        for one in copies:
            one.wait_send()

    each(0, 2, lambda step: sweep(step, True))
    each(2, ITERS - 1, lambda step: sweep(step, False))
    each(ITERS - 1, ITERS, lambda step: sweep(step, True))

    q = jnp.concatenate([q_ref[...], jnp.zeros((PAD - MODES, channels), jnp.float32)], axis=0)
    q = q.astype(jnp.bfloat16)
    first, second = ("x", "y"), ("y", "x")
    place = {"x": x, "y": y}

    def pair_at(h, i, o):
        back = {first[h]: ring(place[first[h]], 4 - i), second[h]: ring(place[second[h]], 4 - o)}
        return bases.at[h, back["y"], c, back["x"]]

    def line_at(h, o):
        if h == 0:
            return bases.at[0, ring(y, 4 - o), c]
        return bases.at[1, :, c, ring(x, 4 - o)]

    started = []

    def go(src, sems, at, to):
        one = send_to(src, src, sems[0].at[at], sems[1].at[at], to)
        one.start()
        started.append(one)
        return one

    near = [[[None] * 4, [None] * 4] for _ in range(2)]
    far = [[[None] * 4 for _ in range(4)] for _ in range(2)]
    pair = []

    def to_first(h, b):
        block = bases.at[h, y, c, x, zl if b == 0 else 1 - zl]
        for o in (2, 1, 3):
            to = {first[h]: ring(place[first[h]], o)}
            near[h][b][o] = go(block, (a_send, a_recv), 8 * h + 4 * b + o, to)

    def to_second(h, i):
        for o in (2, 1, 3):
            to = {second[h]: ring(place[second[h]], o)}
            far[h][i][o] = go(pair_at(h, i, 0), (b_send, b_recv), 16 * h + 4 * i + o, to)

    def across(h, o):
        return go(line_at(h, o), (c_send, c_recv), 4 * h + o, {"core": 1 - c})

    for h in range(2):
        bases[h, y, c, x, zl] = q[:, width * h : width * (h + 1)]
        pair.append(go(bases.at[h, y, c, x, zl], (p_send, p_recv), h, {"zl": 1 - zl}))
        to_first(h, 0)
    for h in range(2):
        pair[h].wait_recv()
        to_first(h, 1)
        to_second(h, 0)
    for i in (1, 3, 2):
        for h in range(2):
            near[h][0][i].wait_recv()
            near[h][1][i].wait_recv()
            to_second(h, i)
    crossed = [across(0, 0), across(1, 0)]
    for o in (1, 3, 2):
        for h in range(2):
            for i in range(4):
                far[h][i][o].wait_recv()
            crossed.append(across(h, o))
    for one in crossed:
        one.wait_recv()
    for one in started:
        one.wait_send()
    each(1, patches, lambda r: row_copy(r).wait_send())

    columns = patches * PAD
    pieces = 2 * patches
    patch = lax.rem(lax.broadcasted_iota(jnp.int32, (pieces, columns), 0), patches)
    spread = patch == lax.div(lax.broadcasted_iota(jnp.int32, (pieces, columns), 1), PAD)
    spread = jnp.where(spread, 1.0, 0.0).astype(jnp.bfloat16)
    count = 256

    def project(i):
        at = pl.ds(pl.multiple_of(count * i, count), count)
        coefficients = sum(
            lax.dot_general(
                sky_ref[at, width * h : width * (h + 1)],
                bases[h].reshape(columns, width),
                (((1,), (1,)), ((), ())),
                preferred_element_type=jnp.float32,
            )
            for h in range(2)
        )
        amounts = two_pieces(
            jnp.dot(weight_ref[at, :], spread, preferred_element_type=jnp.float32) * coefficients
        )
        for h in range(2):
            taken = jnp.dot(amounts, bases[h].reshape(columns, width), preferred_element_type=jnp.float32)
            taken_ref[at, width * h : width * (h + 1)] = taken[:count] + taken[count:]

    each(0, pixels // count, project)


def taken_from(index, count, taper, sky, q0):
    capacity, patches = index.shape
    pixels, channels = sky.shape
    sems = lambda *shape: pltpu.SemaphoreType.DMA(shape)
    return pl.pallas_call(
        taken_kernel,
        out_shape=jax.ShapeDtypeStruct((pixels, channels), jnp.float32),
        in_specs=[pl.BlockSpec(memory_space=pl.ANY)] * 5,
        out_specs=pl.BlockSpec(memory_space=pltpu.VMEM),
        scratch_shapes=[
            pltpu.VMEM(index.shape, index.dtype),
            pltpu.VMEM(count.shape, count.dtype),
            pltpu.VMEM(taper.shape, taper.dtype),
            pltpu.VMEM(sky.shape, sky.dtype),
            pltpu.VMEM(q0.shape, q0.dtype),
            pltpu.VMEM((2, 4, 2, 4, 2, PAD, channels // 2), jnp.bfloat16),
            pltpu.VMEM((pixels, 2 * patches), jnp.bfloat16),
            pltpu.VMEM((patches, capacity, 128), jnp.int32),
            pltpu.VMEM((patches, capacity, channels), jnp.bfloat16),
            pltpu.VMEM((patches, capacity, channels), jnp.bfloat16),
            pltpu.VMEM((channels, channels), jnp.float32),
            pltpu.VMEM((2 * channels, channels), jnp.bfloat16),
            pltpu.VMEM((2, SHARERS, 2, 2 * MODES, channels // 4), jnp.float32),
            pltpu.VMEM((2, SHARERS, 2, 4 * MODES, channels // 8), jnp.bfloat16),
            sems(5),
            sems(patches), sems(patches),
            sems(2, 8), sems(2, 8), sems(2, 8), sems(2, 8),
            sems(2), sems(2), sems(16), sems(16), sems(32), sems(32), sems(8), sems(8),
        ],
        compiler_params=pltpu.CompilerParams(
            collective_id=0, has_side_effects=True, vmem_limit_bytes=VMEM_MIB * MIB
        ),
    )(index, count, taper, sky, q0)


def local(sky, send_index, send_count, taper, start_basis):
    patches, capacity = send_index.shape[2:]
    index = send_index.reshape(patches, capacity).T
    count = send_count.reshape(1, patches)
    taken = taken_from(index, count, taper.reshape(patches, capacity).T, sky, start_basis.T)
    return sky.astype(jnp.float32) - taken


def solution(mesh):
    fine = Mesh(mesh.devices.reshape(4, SHARERS, 2, 2, 4), ("y", "zp", "zl", "core", "x"))
    patch = ("y", "zp", "zl", "core")
    rows = P((*patch, "x"), None)
    placed = (rows, P(patch, "x", None, None), P(patch, "x", None), P(patch, "x", None, None), P())
    return jax.shard_map(local, mesh=fine, in_specs=placed, out_specs=rows, check_vma=False)
```

```python
import jax
import jax.numpy as jnp
from jax import lax
from jax.experimental import pallas as pl
from jax.experimental.pallas import tpu as pltpu
from jax.sharding import Mesh, PartitionSpec as P

ITERS = 6
MODES = 12
SHARERS = 4
CELL = ("y", "core", "x", "zl")
MESH = pl.DeviceIdType.MESH
MIB = 1 << 20
VMEM_MIB = 56


def two_pieces(value):
    high = value.astype(jnp.bfloat16).astype(jnp.float32)
    return jnp.concatenate([high, value - high], axis=0).astype(jnp.bfloat16)


def orthonormal_rows(v):
    row = lax.broadcasted_iota(jnp.int32, (MODES, 1), 0)
    norms = jnp.zeros((MODES, 1), jnp.float32)
    for k in range(MODES):
        lead = v[k : k + 1]
        dots = jnp.sum(v * lead, axis=1, keepdims=True)
        norms = jnp.where(row == k, dots, norms)
        if k + 1 < MODES:
            v = v - jnp.where(row > k, dots / (dots[k : k + 1] + 1e-12), 0.0) * lead
    return v / jnp.sqrt(norms + 1e-12)


def stacked(z, folds):
    width = z.shape[1] // folds
    return jnp.concatenate([z[:, width * f : width * (f + 1)] for f in range(folds)], axis=0)


def unstacked(z, folds):
    return jnp.concatenate([z[MODES * f : MODES * (f + 1)] for f in range(folds)], axis=1)


def each(first, last, step):
    def body(i, carry):
        step(i)
        return carry

    lax.fori_loop(first, last, body, 0)


def ring(at, o):
    return lax.rem(at + o, 4)


def send_to(src, dst, send_sem, recv_sem, to):
    return pltpu.make_async_remote_copy(
        src_ref=src, dst_ref=dst, send_sem=send_sem, recv_sem=recv_sem, device_id=to, device_id_type=MESH
    )


def clean_kernel(
    index_hbm, count_hbm, taper_hbm, sky_hbm, q0_hbm, clean_ref,
    index_ref, count_ref, taper_ref, sky_ref, q_ref, duo, bases, basis, weight_ref, column, rows, inbox, total, gram_ref, exact, short,
    in_sem, row_send, row_recv, x_send, x_recv, s_send, s_recv,
    p_send, p_recv, a_send, a_recv, b_send, b_recv, c_send, c_recv,
):
    me = lax.axis_index("zp")
    y, c, x, zl = (lax.axis_index(name) for name in CELL)
    capacity, patches = index_ref.shape
    pixels, channels = sky_ref.shape

    sources = (index_hbm, count_hbm, sky_hbm, taper_hbm, q0_hbm)
    places = (index_ref, count_ref, sky_ref, taper_ref, q_ref)
    loads = [pltpu.make_async_copy(f, t, in_sem.at[i]) for i, (f, t) in enumerate(zip(sources, places))]
    for load in loads:
        load.start()

    def peer(r):
        o = lax.rem(r * 37, patches)
        to = {
            "x": ring(x, lax.rem(o, 4)),
            "y": ring(y, lax.rem(lax.div(o, 4), 4)),
            "core": lax.rem(c + lax.rem(lax.div(o, 16), 2), 2),
            "zl": lax.rem(zl + lax.div(o, 32), 2),
        }
        return to, ((to["y"] * 2 + to["core"]) * 4 + to["x"]) * 2 + to["zl"]

    def row_copy(r):
        return send_to(rows.at[r], inbox.at[r], row_send.at[r], row_recv.at[r], peer(r)[0])

    barrier = pltpu.get_barrier_semaphore()
    each(1, patches, lambda r: pl.semaphore_signal(barrier, inc=1, device_id=peer(r)[0], device_id_type=MESH))
    for o in range(1, SHARERS):
        pl.semaphore_signal(barrier, inc=1, device_id={"zp": ring(me, o)}, device_id_type=MESH)

    loads[0].wait()
    loads[1].wait()
    slot = lax.broadcasted_iota(jnp.int32, (capacity, patches), 0)
    index = jnp.where(slot < count_ref[...], index_ref[...], -1)
    for d in range(patches):
        column[d] = jnp.broadcast_to(index[:, d : d + 1], (capacity, 128))
    lane = lax.broadcasted_iota(jnp.int32, (4 * capacity, 128), 1)
    loads[2].wait()

    def pick(block):
        near = jnp.concatenate([column[peer(4 * block + j)[1]] for j in range(4)], axis=0)
        hot = [jnp.where(near == lane + 128 * t, 1.0, 0.0) for t in range(pixels // 128)]
        hot = jnp.concatenate(hot, axis=1).astype(jnp.bfloat16)
        found = jnp.dot(hot, sky_ref[...], preferred_element_type=jnp.float32).astype(jnp.bfloat16)
        for j in range(4):
            rows[4 * block + j] = found[capacity * j : capacity * (j + 1)]

    pick(0)
    pl.semaphore_wait(barrier, patches - 1 + SHARERS - 1)
    for j in range(1, 4):
        row_copy(j).start()

    def send(block):
        pick(block)
        for j in range(4):
            row_copy(4 * block + j).start()

    each(1, patches // 4, send)
    inbox[0] = rows[0]

    loads[3].wait()
    loads[4].wait()
    for part in range(pixels // 128):
        pixel = 128 * part + lax.broadcasted_iota(jnp.int32, (128, patches), 0)
        weights = jnp.zeros((128, patches), jnp.float32)
        for j in range(capacity):
            weights = weights + jnp.where(index[j : j + 1, :] == pixel, taper_ref[j : j + 1, :], 0.0)
        whole = jnp.sum(weights, axis=1, keepdims=True)
        weights = weights / jnp.where(whole > 0, whole, 1.0)
        high = weights.astype(jnp.bfloat16).astype(jnp.float32)
        weight_ref[128 * part : 128 * (part + 1), :] = jnp.concatenate([high, weights - high], axis=1).astype(
            jnp.bfloat16
        )

    total[...] = jnp.zeros_like(total)
    tile = 256

    def add(group):
        each(jnp.maximum(8 * group, 1), 8 * group + 8, lambda r: row_copy(r).wait_recv())
        block = inbox[pl.ds(8 * group, 8)].reshape(8 * capacity, channels)
        for t in range(channels // tile):
            part = slice(tile * t, tile * (t + 1))
            total[part, :] += lax.dot_general(
                block[:, part], block, (((0,), (0,)), ((), ())), preferred_element_type=jnp.float32
            )

    def settle(t, value):
        high = value.astype(jnp.bfloat16)
        gram_ref[tile * t : tile * (t + 1), :] = high
        gram_ref[channels + tile * t : channels + tile * (t + 1), :] = (value - high.astype(jnp.float32)).astype(
            jnp.bfloat16
        )

    last = patches // 8 - 1
    each(0, last, add)
    for t in range(channels // tile):
        settle(t, total[tile * t : tile * (t + 1), :])
    each(8 * last, patches, lambda r: row_copy(r).wait_recv())

    def late_rows():
        return inbox[8 * last :].reshape(8 * capacity, channels)

    def settle_late():
        block = late_rows()
        for t in range(channels // tile):
            part = slice(tile * t, tile * (t + 1))
            settle(
                t,
                total[part, :]
                + lax.dot_general(
                    block[:, part], block, (((0,), (0,)), ((), ())), preferred_element_type=jnp.float32
                ),
            )

    width = channels // 2

    def sweep(step, wide, late=False):
        folds, box, sems = (2, exact, (x_send, x_recv)) if wide else (4, short, (s_send, s_recv))
        at = step % 2 if isinstance(step, int) else lax.rem(step, 2)
        box = box.at[at]
        pieces = two_pieces(q_ref[...])
        lhs = jnp.concatenate([pieces, pieces], axis=1)
        if late:
            y = lax.dot_general(
                pieces, late_rows(), (((1,), (1,)), ((), ())), preferred_element_type=jnp.float32
            )
            y = two_pieces(y[:MODES] + y[MODES:])
        copies = []
        for h in range(2):
            z = jnp.dot(lhs, gram_ref[:, width * h : width * (h + 1)], preferred_element_type=jnp.float32)
            if late:
                z = z + jnp.dot(
                    y, late_rows()[:, width * h : width * (h + 1)], preferred_element_type=jnp.float32
                )
            box[me, h] = stacked(z[:MODES] + z[MODES:], folds).astype(box.dtype)
            for o in (2, 1, 3):
                mine = box.at[me, h]
                copies.append(
                    send_to(mine, mine, sems[0].at[at, 4 * h + o], sems[1].at[at, 4 * h + o], {"zp": ring(me, o)})
                )
                copies[-1].start()
        if late:
            settle_late()
        for one in copies:
            one.wait_recv()
        halves = []
        for h in range(2):
            whole = box[0, h].astype(jnp.float32)
            for k in range(1, SHARERS):
                whole = whole + box[k, h].astype(jnp.float32)
            halves.append(unstacked(whole, folds))
        q_ref[...] = orthonormal_rows(jnp.concatenate(halves, axis=1))
        for one in copies:
            one.wait_send()

    sweep(0, True, late=True)
    each(1, ITERS - 1, lambda step: sweep(step, False))
    sweep(ITERS - 1, True)

    blank = jnp.zeros((16 - MODES, channels), jnp.float32)
    own = jnp.concatenate([q_ref[...], blank], axis=0).astype(jnp.bfloat16)
    first, second = ("x", "y"), ("y", "x")
    place = {"x": x, "y": y}

    def pair_at(h, i, o):
        back = {first[h]: ring(place[first[h]], 4 - i), second[h]: ring(place[second[h]], 4 - o)}
        return bases.at[h, back["y"], c, back["x"]]

    def line_at(h, o):
        if h == 0:
            return bases.at[0, ring(y, 4 - o), c]
        return bases.at[1, :, c, ring(x, 4 - o)]

    started = []

    def go(src, sems, at, to):
        one = send_to(src, src, sems[0].at[at], sems[1].at[at], to)
        one.start()
        started.append(one)
        return one

    near = [[None] * 4 for _ in range(2)]
    far = [[[None] * 4 for _ in range(4)] for _ in range(2)]
    pair = []

    def to_first(h):
        for o in (2, 1, 3):
            to = {first[h]: ring(place[first[h]], o)}
            near[h][o] = go(pair_at(h, 0, 0), (a_send, a_recv), 4 * h + o, to)

    def to_second(h, i):
        for o in (2, 1, 3):
            to = {second[h]: ring(place[second[h]], o)}
            far[h][i][o] = go(pair_at(h, i, 0), (b_send, b_recv), 16 * h + 4 * i + o, to)

    def across(h, o):
        return go(line_at(h, o), (c_send, c_recv), 4 * h + o, {"core": 1 - c})

    for h in range(2):
        duo[zl, h] = own[:, width * h : width * (h + 1)]
        pair.append(go(duo.at[zl, h], (p_send, p_recv), h, {"zl": 1 - zl}))
    for h in range(2):
        pair[h].wait_recv()
        one, two = (duo[k, h].astype(jnp.float32) for k in range(2))
        rest = jnp.concatenate([one[8:MODES], two[8:MODES]], axis=0)
        fold = width // 2
        block = jnp.concatenate(
            [
                jnp.concatenate([one[:8], two[:8]], axis=0),
                jnp.concatenate([rest[:, :fold], rest[:, fold:]], axis=0),
            ],
            axis=1,
        )
        bases[h, y, c, x] = block.astype(jnp.bfloat16)
        to_first(h)
        to_second(h, 0)
    for i in (1, 3, 2):
        for h in range(2):
            near[h][i].wait_recv()
            to_second(h, i)
    crossed = [across(0, 0), across(1, 0)]
    for o in (1, 3, 2):
        for h in range(2):
            for i in range(4):
                far[h][i][o].wait_recv()
            crossed.append(across(h, o))
    for one in crossed:
        one.wait_recv()
    for one in started:
        one.wait_send()
    each(1, patches, lambda r: row_copy(r).wait_send())

    plain = patches // 2 * 16
    columns = patches * MODES
    for h in range(2):
        block = bases[h].reshape(patches // 2, 16, width + width // 2)
        basis[h, :plain] = block[:, :, :width].reshape(plain, width)
        rest = block[:, :, width:].astype(jnp.float32)
        rest = jnp.concatenate([rest[:, :8], rest[:, 8:]], axis=2)
        basis[h, plain:] = rest.reshape(columns - plain, width).astype(jnp.bfloat16)
    pieces = 2 * patches
    patch = lax.rem(lax.broadcasted_iota(jnp.int32, (pieces, columns), 0), patches)
    at = lax.broadcasted_iota(jnp.int32, (pieces, columns), 1)
    owner = jnp.where(at < plain, lax.div(at, 8), lax.div(at - plain, 4))
    spread = jnp.where(patch == owner, 1.0, 0.0).astype(jnp.bfloat16)
    count = 256

    def project(i):
        at = pl.ds(pl.multiple_of(count * i, count), count)
        coefficients = sum(
            lax.dot_general(
                sky_ref[at, width * h : width * (h + 1)],
                basis[h],
                (((1,), (1,)), ((), ())),
                preferred_element_type=jnp.float32,
            )
            for h in range(2)
        )
        amounts = two_pieces(
            jnp.dot(weight_ref[at, :], spread, preferred_element_type=jnp.float32) * coefficients
        )
        for h in range(2):
            taken = jnp.dot(amounts, basis[h], preferred_element_type=jnp.float32)
            part = slice(width * h, width * (h + 1))
            clean_ref[at, part] = sky_ref[at, part].astype(jnp.float32) - (taken[:count] + taken[count:])

    each(0, pixels // count, project)


def cleaned(index, count, taper, sky, q0):
    capacity, patches = index.shape
    pixels, channels = sky.shape
    sems = lambda *shape: pltpu.SemaphoreType.DMA(shape)
    return pl.pallas_call(
        clean_kernel,
        out_shape=jax.ShapeDtypeStruct((pixels, channels), jnp.float32),
        in_specs=[pl.BlockSpec(memory_space=pl.ANY)] * 5,
        out_specs=pl.BlockSpec(memory_space=pltpu.VMEM),
        scratch_shapes=[
            pltpu.VMEM(index.shape, index.dtype),
            pltpu.VMEM(count.shape, count.dtype),
            pltpu.VMEM(taper.shape, taper.dtype),
            pltpu.VMEM(sky.shape, sky.dtype),
            pltpu.VMEM(q0.shape, q0.dtype),
            pltpu.VMEM((2, 2, 16, channels // 2), jnp.bfloat16),
            pltpu.VMEM((2, 4, 2, 4, 16, channels * 3 // 4), jnp.bfloat16),
            pltpu.VMEM((2, patches * MODES, channels // 2), jnp.bfloat16),
            pltpu.VMEM((pixels, 2 * patches), jnp.bfloat16),
            pltpu.VMEM((patches, capacity, 128), jnp.int32),
            pltpu.VMEM((patches, capacity, channels), jnp.bfloat16),
            pltpu.VMEM((patches, capacity, channels), jnp.bfloat16),
            pltpu.VMEM((channels, channels), jnp.float32),
            pltpu.VMEM((2 * channels, channels), jnp.bfloat16),
            pltpu.VMEM((2, SHARERS, 2, 2 * MODES, channels // 4), jnp.float32),
            pltpu.VMEM((2, SHARERS, 2, 4 * MODES, channels // 8), jnp.bfloat16),
            sems(5),
            sems(patches), sems(patches),
            sems(2, 8), sems(2, 8), sems(2, 8), sems(2, 8),
            sems(2), sems(2), sems(8), sems(8), sems(32), sems(32), sems(8), sems(8),
        ],
        compiler_params=pltpu.CompilerParams(
            collective_id=0, has_side_effects=True, vmem_limit_bytes=VMEM_MIB * MIB
        ),
    )(index, count, taper, sky, q0)


def local(sky, send_index, send_count, taper, start_basis):
    patches, capacity = send_index.shape[2:]
    index = send_index.reshape(patches, capacity).T
    count = send_count.reshape(1, patches)
    return cleaned(index, count, taper.reshape(patches, capacity).T, sky, start_basis.T)


def solution(mesh):
    fine = Mesh(mesh.devices.reshape(4, SHARERS, 2, 2, 4), ("y", "zp", "zl", "core", "x"))
    patch = ("y", "zp", "zl", "core")
    rows = P((*patch, "x"), None)
    placed = (rows, P(patch, "x", None, None), P(patch, "x", None), P(patch, "x", None, None), P())
    return jax.shard_map(local, mesh=fine, in_specs=placed, out_specs=rows, check_vma=False)
```

```python
import jax
import jax.numpy as jnp
from jax import lax
from jax.experimental import pallas as pl
from jax.experimental.pallas import tpu as pltpu
from jax.sharding import Mesh, PartitionSpec as P

ITERS = 6
MODES = 12
SHARERS = 4
CELL = ("y", "core", "x", "zl")
MESH = pl.DeviceIdType.MESH
MIB = 1 << 20
VMEM_MIB = 56
WINDOW = 4


def two_pieces(value):
    high = value.astype(jnp.bfloat16).astype(jnp.float32)
    return jnp.concatenate([high, value - high], axis=0).astype(jnp.bfloat16)


def orthonormal_rows(v):
    row = lax.broadcasted_iota(jnp.int32, (MODES, 1), 0)
    norms = jnp.zeros((MODES, 1), jnp.float32)
    for k in range(MODES):
        lead = v[k : k + 1]
        dots = jnp.sum(v * lead, axis=1, keepdims=True)
        norms = jnp.where(row == k, dots, norms)
        if k + 1 < MODES:
            v = v - jnp.where(row > k, dots / (dots[k : k + 1] + 1e-12), 0.0) * lead
    return v * (1.0 / jnp.sqrt(norms + 1e-12))


def orthonormal_pairs(v):
    row = lax.broadcasted_iota(jnp.int32, (MODES, 1), 0)
    norms = jnp.ones((MODES, 1), jnp.float32)
    for k in range(0, MODES, 2):
        a, b = v[k : k + 1], v[k + 1 : k + 2]
        on_a = jnp.sum(v * a, axis=1, keepdims=True)
        on_b = jnp.sum(v * b, axis=1, keepdims=True)
        aa, ab, bb = on_a[k : k + 1], on_a[k + 1 : k + 2], on_b[k + 1 : k + 2]
        by_a = on_a / (aa + 1e-12)
        c = by_a[k + 1 : k + 2]
        rest = jnp.maximum(bb - 2.0 * c * ab + c * c * aa, 1e-6 * bb)
        on_rest = on_b - c * on_a - by_a * ab + by_a * (c * aa)
        by_rest = jnp.where(row > k + 1, on_rest / (rest + 1e-12), 0.0)
        v = v - (jnp.where(row > k, by_a, 0.0) - by_rest * c) * a - by_rest * b
        norms = jnp.where(row == k, aa, jnp.where(row == k + 1, rest, norms))
    return v * (1.0 / jnp.sqrt(norms + 1e-12))


def stacked(z, folds):
    width = z.shape[1] // folds
    return jnp.concatenate([z[:, width * f : width * (f + 1)] for f in range(folds)], axis=0)


def unstacked(z, folds):
    return jnp.concatenate([z[MODES * f : MODES * (f + 1)] for f in range(folds)], axis=1)


def each(first, last, step):
    def body(i, carry):
        step(i)
        return carry

    lax.fori_loop(first, last, body, 0)


def ring(at, o):
    return lax.rem(at + o, 4)


def send_to(src, dst, send_sem, recv_sem, to):
    return pltpu.make_async_remote_copy(
        src_ref=src, dst_ref=dst, send_sem=send_sem, recv_sem=recv_sem, device_id=to, device_id_type=MESH
    )


def clean_kernel(
    index_hbm, count_hbm, taper_hbm, sky_hbm, q0_hbm, clean_hbm,
    clean_ref, index_ref, count_ref, taper_ref, sky_ref, q_ref, duo, bases, basis, weight_ref, column, rows, inbox, total, gram_ref, exact, short,
    in_sem, out_sem, row_send, row_recv, x_send, x_recv, s_send, s_recv,
    p_send, p_recv, a_send, a_recv, b_send, b_recv, c_send, c_recv,
):
    me = lax.axis_index("zp")
    y, c, x, zl = (lax.axis_index(name) for name in CELL)
    capacity, patches = index_ref.shape
    pixels, channels = sky_ref.shape

    sources = (index_hbm, count_hbm, sky_hbm, taper_hbm, q0_hbm)
    places = (index_ref, count_ref, sky_ref, taper_ref, q_ref)
    loads = [pltpu.make_async_copy(f, t, in_sem.at[i]) for i, (f, t) in enumerate(zip(sources, places))]
    for load in loads:
        load.start()

    def peer(r):
        o = lax.rem(r * 37, patches)
        to = {
            "x": ring(x, lax.rem(o, 4)),
            "y": ring(y, lax.rem(lax.div(o, 4), 4)),
            "core": lax.rem(c + lax.rem(lax.div(o, 16), 2), 2),
            "zl": lax.rem(zl + lax.div(o, 32), 2),
        }
        return to, ((to["y"] * 2 + to["core"]) * 4 + to["x"]) * 2 + to["zl"]

    def row_copy(r):
        return send_to(rows.at[r], inbox.at[r], row_send.at[r], row_recv.at[r], peer(r)[0])

    barrier = pltpu.get_barrier_semaphore()
    at_x, at_y = [ring(x, o) for o in range(4)], [ring(y, o) for o in range(4)]
    for o in range(1, patches):
        to = {
            "x": at_x[o % 4],
            "y": at_y[o // 4 % 4],
            "core": 1 - c if o // 16 % 2 else c,
            "zl": 1 - zl if o // 32 else zl,
        }
        pl.semaphore_signal(barrier, inc=1, device_id=to, device_id_type=MESH)
    for o in range(1, SHARERS):
        pl.semaphore_signal(barrier, inc=1, device_id={"zp": ring(me, o)}, device_id_type=MESH)

    loads[0].wait()
    loads[1].wait()
    slot = lax.broadcasted_iota(jnp.int32, (capacity, patches), 0)
    index = jnp.where(slot < count_ref[...], index_ref[...], -1)
    for d in range(patches):
        column[d] = jnp.broadcast_to(index[:, d : d + 1], (capacity, 128))
    lane = lax.broadcasted_iota(jnp.int32, (4 * capacity, 128), 1)
    loads[2].wait()

    def pick(block):
        near = jnp.concatenate([column[peer(4 * block + j)[1]] for j in range(4)], axis=0)
        hot = [jnp.where(near == lane + 128 * t, 1.0, 0.0) for t in range(pixels // 128)]
        hot = jnp.concatenate(hot, axis=1).astype(jnp.bfloat16)
        found = jnp.dot(hot, sky_ref[...], preferred_element_type=jnp.float32).astype(jnp.bfloat16)
        for j in range(4):
            rows[4 * block + j] = found[capacity * j : capacity * (j + 1)]

    pick(0)
    pl.semaphore_wait(barrier, patches - 1 + SHARERS - 1)
    for j in range(1, 4):
        row_copy(j).start()

    def send(block):
        pick(block)
        for j in range(4):
            row_copy(4 * block + j).start()

    each(1, WINDOW, send)
    inbox[0] = rows[0]

    loads[3].wait()
    loads[4].wait()
    for part in range(pixels // 128):
        pixel = 128 * part + lax.broadcasted_iota(jnp.int32, (128, patches), 0)
        weights = jnp.zeros((128, patches), jnp.float32)
        for j in range(capacity):
            weights = weights + jnp.where(index[j : j + 1, :] == pixel, taper_ref[j : j + 1, :], 0.0)
        whole = jnp.sum(weights, axis=1, keepdims=True)
        weights = weights / jnp.where(whole > 0, whole, 1.0)
        high = weights.astype(jnp.bfloat16).astype(jnp.float32)
        weight_ref[128 * part : 128 * (part + 1), :] = jnp.concatenate([high, weights - high], axis=1).astype(
            jnp.bfloat16
        )

    total[...] = jnp.zeros_like(total)
    tile = 256

    def add(group):
        each(jnp.maximum(8 * group, 1), 8 * group + 8, lambda r: row_copy(r).wait_recv())
        block = inbox[pl.ds(8 * group, 8)].reshape(8 * capacity, channels)
        for t in range(channels // tile):
            part = slice(tile * t, tile * (t + 1))
            total[part, :] += lax.dot_general(
                block[:, part], block, (((0,), (0,)), ((), ())), preferred_element_type=jnp.float32
            )

    def settle(t, value):
        high = value.astype(jnp.bfloat16)
        gram_ref[tile * t : tile * (t + 1), :] = high
        gram_ref[channels + tile * t : channels + tile * (t + 1), :] = (value - high.astype(jnp.float32)).astype(
            jnp.bfloat16
        )

    last = patches // 8 - 1

    def send_on(block):
        first = 4 * (block - WINDOW)
        each(jnp.maximum(first, 1), first + 4, lambda r: row_copy(r).wait_send())
        send(block)

    def send_and_add(group):
        send_on(2 * group + WINDOW)
        send_on(2 * group + WINDOW + 1)
        add(group)

    paired = (patches // 4 - WINDOW) // 2
    each(0, paired, send_and_add)
    each(paired, last, add)
    for t in range(channels // tile):
        settle(t, total[tile * t : tile * (t + 1), :])
    each(8 * last, patches, lambda r: row_copy(r).wait_recv())

    def late_rows():
        return inbox[8 * last :].reshape(8 * capacity, channels)

    def settle_late():
        block = late_rows()
        for t in range(channels // tile):
            part = slice(tile * t, tile * (t + 1))
            settle(
                t,
                total[part, :]
                + lax.dot_general(
                    block[:, part], block, (((0,), (0,)), ((), ())), preferred_element_type=jnp.float32
                ),
            )

    width = channels // 2

    def sweep(step, wide, late=False, final=False):
        folds, box, sems = (2, exact, (x_send, x_recv)) if wide else (4, short, (s_send, s_recv))
        at = step % 2 if isinstance(step, int) else lax.rem(step, 2)
        box = box.at[at]
        pieces = two_pieces(q_ref[...])
        lhs = jnp.concatenate([pieces, pieces], axis=1)
        if late:
            y = lax.dot_general(
                pieces, late_rows(), (((1,), (1,)), ((), ())), preferred_element_type=jnp.float32
            )
            y = two_pieces(y[:MODES] + y[MODES:])
        copies = []
        for h in range(2):
            z = jnp.dot(lhs, gram_ref[:, width * h : width * (h + 1)], preferred_element_type=jnp.float32)
            if late:
                z = z + jnp.dot(
                    y, late_rows()[:, width * h : width * (h + 1)], preferred_element_type=jnp.float32
                )
            box[me, h] = stacked(z[:MODES] + z[MODES:], folds).astype(box.dtype)
            for o in (2, 1, 3):
                mine = box.at[me, h]
                copies.append(
                    send_to(mine, mine, sems[0].at[at, 4 * h + o], sems[1].at[at, 4 * h + o], {"zp": ring(me, o)})
                )
                copies[-1].start()
        if late:
            settle_late()
            each(patches - 4 * WINDOW, patches, lambda r: row_copy(r).wait_send())
        for one in copies:
            one.wait_recv()
        halves = []
        for h in range(2):
            whole = box[0, h].astype(jnp.float32)
            for k in range(1, SHARERS):
                whole = whole + box[k, h].astype(jnp.float32)
            halves.append(unstacked(whole, folds))
        whole = jnp.concatenate(halves, axis=1)
        q_ref[...] = orthonormal_rows(whole) if final else orthonormal_pairs(whole)
        for one in copies:
            one.wait_send()

    sweep(0, True, late=True)
    each(1, ITERS - 1, lambda step: sweep(step, False))
    sweep(ITERS - 1, True, final=True)

    blank = jnp.zeros((16 - MODES, channels), jnp.float32)
    own = jnp.concatenate([q_ref[...], blank], axis=0).astype(jnp.bfloat16)
    first, second = ("x", "y"), ("y", "x")
    place = {"x": x, "y": y}

    def pair_at(h, i, o):
        back = {first[h]: ring(place[first[h]], 4 - i), second[h]: ring(place[second[h]], 4 - o)}
        return bases.at[h, back["y"], c, back["x"]]

    def line_at(h, o):
        if h == 0:
            return bases.at[0, ring(y, 4 - o), c]
        return bases.at[1, :, c, ring(x, 4 - o)]

    started = []

    def go(src, sems, at, to):
        one = send_to(src, src, sems[0].at[at], sems[1].at[at], to)
        one.start()
        started.append(one)
        return one

    near = [[None] * 4 for _ in range(2)]
    far = [[[None] * 4 for _ in range(4)] for _ in range(2)]
    pair = []

    def to_first(h):
        for o in (2, 1, 3):
            to = {first[h]: ring(place[first[h]], o)}
            near[h][o] = go(pair_at(h, 0, 0), (a_send, a_recv), 4 * h + o, to)

    def to_second(h, i):
        for o in (2, 1, 3):
            to = {second[h]: ring(place[second[h]], o)}
            far[h][i][o] = go(pair_at(h, i, 0), (b_send, b_recv), 16 * h + 4 * i + o, to)

    def across(h, o):
        return go(line_at(h, o), (c_send, c_recv), 4 * h + o, {"core": 1 - c})

    for h in range(2):
        duo[zl, h] = own[:, width * h : width * (h + 1)]
        pair.append(go(duo.at[zl, h], (p_send, p_recv), h, {"zl": 1 - zl}))
    for h in range(2):
        pair[h].wait_recv()
        one, two = (duo[k, h].astype(jnp.float32) for k in range(2))
        rest = jnp.concatenate([one[8:MODES], two[8:MODES]], axis=0)
        fold = width // 2
        block = jnp.concatenate(
            [
                jnp.concatenate([one[:8], two[:8]], axis=0),
                jnp.concatenate([rest[:, :fold], rest[:, fold:]], axis=0),
            ],
            axis=1,
        )
        bases[h, y, c, x] = block.astype(jnp.bfloat16)
        to_first(h)
        to_second(h, 0)
    for i in (1, 3, 2):
        for h in range(2):
            near[h][i].wait_recv()
            to_second(h, i)
    crossed = [across(0, 0), across(1, 0)]
    for o in (1, 3, 2):
        for h in range(2):
            for i in range(4):
                far[h][i][o].wait_recv()
            crossed.append(across(h, o))
    for one in crossed:
        one.wait_recv()

    plain = patches // 2 * 16
    columns = patches * MODES
    for h in range(2):
        block = bases[h].reshape(patches // 2, 16, width + width // 2)
        basis[h, :plain] = block[:, :, :width].reshape(plain, width)
        rest = block[:, :, width:].astype(jnp.float32)
        rest = jnp.concatenate([rest[:, :8], rest[:, 8:]], axis=2)
        basis[h, plain:] = rest.reshape(columns - plain, width).astype(jnp.bfloat16)
    pieces = 2 * patches
    patch = lax.rem(lax.broadcasted_iota(jnp.int32, (pieces, columns), 0), patches)
    at = lax.broadcasted_iota(jnp.int32, (pieces, columns), 1)
    owner = jnp.where(at < plain, lax.div(at, 8), lax.div(at - plain, 4))
    spread = jnp.where(patch == owner, 1.0, 0.0).astype(jnp.bfloat16)
    count = 256

    def project(i):
        at = pl.ds(count * i, count)
        coefficients = sum(
            lax.dot_general(
                sky_ref[at, width * h : width * (h + 1)],
                basis[h],
                (((1,), (1,)), ((), ())),
                preferred_element_type=jnp.float32,
            )
            for h in range(2)
        )
        amounts = two_pieces(
            jnp.dot(weight_ref[at, :], spread, preferred_element_type=jnp.float32) * coefficients
        )
        for h in range(2):
            taken = jnp.dot(amounts, basis[h], preferred_element_type=jnp.float32)
            part = slice(width * h, width * (h + 1))
            clean_ref[at, part] = sky_ref[at, part].astype(jnp.float32) - (taken[:count] + taken[count:])

    stores = []
    for i in range(pixels // count):
        project(i)
        at = pl.ds(count * i, count)
        stores.append(pltpu.make_async_copy(clean_ref.at[at], clean_hbm.at[at], out_sem.at[i]))
        stores[i].start()
    for one in started:
        one.wait_send()
    for store in stores:
        store.wait()


def cleaned(index, count, taper, sky, q0):
    capacity, patches = index.shape
    pixels, channels = sky.shape
    sems = lambda *shape: pltpu.SemaphoreType.DMA(shape)
    return pl.pallas_call(
        clean_kernel,
        out_shape=jax.ShapeDtypeStruct((pixels, channels), jnp.float32),
        in_specs=[pl.BlockSpec(memory_space=pl.ANY)] * 5,
        out_specs=pl.BlockSpec(memory_space=pl.ANY),
        scratch_shapes=[
            pltpu.VMEM((pixels, channels), jnp.float32),
            pltpu.VMEM(index.shape, index.dtype),
            pltpu.VMEM(count.shape, count.dtype),
            pltpu.VMEM(taper.shape, taper.dtype),
            pltpu.VMEM(sky.shape, sky.dtype),
            pltpu.VMEM(q0.shape, q0.dtype),
            pltpu.VMEM((2, 2, 16, channels // 2), jnp.bfloat16),
            pltpu.VMEM((2, 4, 2, 4, 16, channels * 3 // 4), jnp.bfloat16),
            pltpu.VMEM((2, patches * MODES, channels // 2), jnp.bfloat16),
            pltpu.VMEM((pixels, 2 * patches), jnp.bfloat16),
            pltpu.VMEM((patches, capacity, 128), jnp.int32),
            pltpu.VMEM((patches, capacity, channels), jnp.bfloat16),
            pltpu.VMEM((patches, capacity, channels), jnp.bfloat16),
            pltpu.VMEM((channels, channels), jnp.float32),
            pltpu.VMEM((2 * channels, channels), jnp.bfloat16),
            pltpu.VMEM((2, SHARERS, 2, 2 * MODES, channels // 4), jnp.float32),
            pltpu.VMEM((2, SHARERS, 2, 4 * MODES, channels // 8), jnp.bfloat16),
            sems(5),
            sems(2),
            sems(patches), sems(patches),
            sems(2, 8), sems(2, 8), sems(2, 8), sems(2, 8),
            sems(2), sems(2), sems(8), sems(8), sems(32), sems(32), sems(8), sems(8),
        ],
        compiler_params=pltpu.CompilerParams(
            collective_id=0, has_side_effects=True, vmem_limit_bytes=VMEM_MIB * MIB
        ),
    )(index, count, taper, sky, q0)


def copy_kernel(from_ref, to_ref, held, in_sem, out_sem):
    chunks = in_sem.shape[0]
    count = held.shape[0] // chunks
    parts = [pl.ds(count * i, count) for i in range(chunks)]
    loads = [pltpu.make_async_copy(from_ref.at[p], held.at[p], in_sem.at[i]) for i, p in enumerate(parts)]
    stores = [pltpu.make_async_copy(held.at[p], to_ref.at[p], out_sem.at[i]) for i, p in enumerate(parts)]
    for load in loads:
        load.start()
    for load, store in zip(loads, stores):
        load.wait()
        store.start()
    for store in stores:
        store.wait()


def copied(array):
    anywhere = pl.BlockSpec(memory_space=pl.ANY)
    return pl.pallas_call(
        copy_kernel,
        out_shape=jax.ShapeDtypeStruct(array.shape, array.dtype),
        in_specs=[anywhere],
        out_specs=anywhere,
        scratch_shapes=[
            pltpu.VMEM(array.shape, array.dtype),
            pltpu.SemaphoreType.DMA((8,)),
            pltpu.SemaphoreType.DMA((8,)),
        ],
        compiler_params=pltpu.CompilerParams(vmem_limit_bytes=VMEM_MIB * MIB),
    )(array)


def local(sky, send_index, send_count, taper, start_basis):
    patches, capacity = send_index.shape[2:]
    index = send_index.reshape(patches, capacity).T
    count = send_count.reshape(1, patches)
    return copied(cleaned(index, count, taper.reshape(patches, capacity).T, sky, start_basis.T))


def solution(mesh):
    fine = Mesh(mesh.devices.reshape(4, SHARERS, 2, 2, 4), ("y", "zp", "zl", "core", "x"))
    patch = ("y", "zp", "zl", "core")
    rows = P((*patch, "x"), None)
    placed = (rows, P(patch, "x", None, None), P(patch, "x", None), P(patch, "x", None, None), P())
    return jax.shard_map(local, mesh=fine, in_specs=placed, out_specs=rows, check_vma=False)
```

```python
import jax
import jax.numpy as jnp
from jax import lax
from jax.experimental import pallas as pl
from jax.experimental.pallas import tpu as pltpu
from jax.sharding import Mesh, PartitionSpec as P

ITERS = 6
MODES = 12
SHARERS = 4
CELL = ("y", "core", "x", "zl")
MESH = pl.DeviceIdType.MESH
MIB = 1 << 20
VMEM_MIB = 56
WINDOW = 8


def two_pieces(value):
    high = value.astype(jnp.bfloat16).astype(jnp.float32)
    return jnp.concatenate([high, value - high], axis=0).astype(jnp.bfloat16)


def orthonormal_rows(v):
    row = lax.broadcasted_iota(jnp.int32, (MODES, 1), 0)
    norms = jnp.zeros((MODES, 1), jnp.float32)
    for k in range(MODES):
        lead = v[k : k + 1]
        dots = jnp.sum(v * lead, axis=1, keepdims=True)
        norms = jnp.where(row == k, dots, norms)
        if k + 1 < MODES:
            v = v - jnp.where(row > k, dots / (dots[k : k + 1] + 1e-12), 0.0) * lead
    return v * (1.0 / jnp.sqrt(norms + 1e-12))


def orthonormal_pairs(v):
    row = lax.broadcasted_iota(jnp.int32, (MODES, 1), 0)
    norms = jnp.ones((MODES, 1), jnp.float32)
    for k in range(0, MODES, 2):
        a, b = v[k : k + 1], v[k + 1 : k + 2]
        on_a = jnp.sum(v * a, axis=1, keepdims=True)
        on_b = jnp.sum(v * b, axis=1, keepdims=True)
        aa, ab, bb = on_a[k : k + 1], on_a[k + 1 : k + 2], on_b[k + 1 : k + 2]
        by_a = on_a / (aa + 1e-12)
        c = by_a[k + 1 : k + 2]
        rest = jnp.maximum(bb - 2.0 * c * ab + c * c * aa, 1e-6 * bb)
        on_rest = on_b - c * on_a - by_a * ab + by_a * (c * aa)
        by_rest = jnp.where(row > k + 1, on_rest / (rest + 1e-12), 0.0)
        v = v - (jnp.where(row > k, by_a, 0.0) - by_rest * c) * a - by_rest * b
        norms = jnp.where(row == k, aa, jnp.where(row == k + 1, rest, norms))
    return v * (1.0 / jnp.sqrt(norms + 1e-12))


def stacked(z, folds):
    width = z.shape[1] // folds
    return jnp.concatenate([z[:, width * f : width * (f + 1)] for f in range(folds)], axis=0)


def unstacked(z, folds):
    return jnp.concatenate([z[MODES * f : MODES * (f + 1)] for f in range(folds)], axis=1)


def each(first, last, step):
    def body(i, carry):
        step(i)
        return carry

    lax.fori_loop(first, last, body, 0)


def ring(at, o):
    return lax.rem(at + o, 4)


def send_to(src, dst, send_sem, recv_sem, to):
    return pltpu.make_async_remote_copy(
        src_ref=src, dst_ref=dst, send_sem=send_sem, recv_sem=recv_sem, device_id=to, device_id_type=MESH
    )


def clean_kernel(
    index_hbm, count_hbm, taper_hbm, sky_hbm, q0_hbm, clean_hbm,
    clean_ref, index_ref, count_ref, taper_ref, sky_ref, q_ref, duo, bases, basis, weight_ref, spread, column, rows, inbox, total, gram_ref, exact, short,
    in_sem, out_sem, row_send, row_recv, x_send, x_recv, s_send, s_recv,
    p_send, p_recv, a_send, a_recv, b_send, b_recv, c_send, c_recv,
):
    me = lax.axis_index("zp")
    y, c, x, zl = (lax.axis_index(name) for name in CELL)
    capacity, patches = index_ref.shape
    pixels, channels = sky_ref.shape

    sources = (index_hbm, count_hbm, sky_hbm, taper_hbm, q0_hbm)
    places = (index_ref, count_ref, sky_ref, taper_ref, q_ref)
    loads = [pltpu.make_async_copy(f, t, in_sem.at[i]) for i, (f, t) in enumerate(zip(sources, places))]
    for load in loads:
        load.start()

    def peer(r):
        o = lax.rem(r * 37, patches)
        to = {
            "x": ring(x, lax.rem(o, 4)),
            "y": ring(y, lax.rem(lax.div(o, 4), 4)),
            "core": lax.rem(c + lax.rem(lax.div(o, 16), 2), 2),
            "zl": lax.rem(zl + lax.div(o, 32), 2),
        }
        return to, ((to["y"] * 2 + to["core"]) * 4 + to["x"]) * 2 + to["zl"]

    def row_copy(r):
        return send_to(rows.at[r], inbox.at[r], row_send.at[r], row_recv.at[r], peer(r)[0])

    barrier = pltpu.get_barrier_semaphore()
    at_x, at_y = [ring(x, o) for o in range(4)], [ring(y, o) for o in range(4)]
    for o in range(1, patches):
        to = {
            "x": at_x[o % 4],
            "y": at_y[o // 4 % 4],
            "core": 1 - c if o // 16 % 2 else c,
            "zl": 1 - zl if o // 32 else zl,
        }
        pl.semaphore_signal(barrier, inc=1, device_id=to, device_id_type=MESH)
    for o in range(1, SHARERS):
        pl.semaphore_signal(barrier, inc=1, device_id={"zp": ring(me, o)}, device_id_type=MESH)

    loads[0].wait()
    loads[1].wait()
    slot = lax.broadcasted_iota(jnp.int32, (capacity, patches), 0)
    index = jnp.where(slot < count_ref[...], index_ref[...], -1)
    for d in range(patches):
        column[d] = jnp.broadcast_to(index[:, d : d + 1], (capacity, 128))
    lane = lax.broadcasted_iota(jnp.int32, (4 * capacity, 128), 1)
    loads[2].wait()

    def pick(block):
        near = jnp.concatenate([column[peer(4 * block + j)[1]] for j in range(4)], axis=0)
        hot = [jnp.where(near == lane + 128 * t, 1.0, 0.0) for t in range(pixels // 128)]
        hot = jnp.concatenate(hot, axis=1).astype(jnp.bfloat16)
        found = jnp.dot(hot, sky_ref[...], preferred_element_type=jnp.float32).astype(jnp.bfloat16)
        for j in range(4):
            rows[4 * block + j] = found[capacity * j : capacity * (j + 1)]

    pick(0)
    pl.semaphore_wait(barrier, patches - 1 + SHARERS - 1)
    for j in range(1, 4):
        row_copy(j).start()

    def send(block):
        pick(block)
        for j in range(4):
            row_copy(4 * block + j).start()

    each(1, WINDOW, send)
    inbox[0] = rows[0]

    loads[3].wait()
    loads[4].wait()
    for part in range(pixels // 128):
        pixel = 128 * part + lax.broadcasted_iota(jnp.int32, (128, patches), 0)
        weights = jnp.zeros((128, patches), jnp.float32)
        for j in range(capacity):
            weights = weights + jnp.where(index[j : j + 1, :] == pixel, taper_ref[j : j + 1, :], 0.0)
        whole = jnp.sum(weights, axis=1, keepdims=True)
        weights = weights / jnp.where(whole > 0, whole, 1.0)
        high = weights.astype(jnp.bfloat16).astype(jnp.float32)
        weight_ref[128 * part : 128 * (part + 1), :] = jnp.concatenate([high, weights - high], axis=1).astype(
            jnp.bfloat16
        )

    plain = patches // 4 * 16
    columns = patches // 2 * MODES
    patch = lax.rem(lax.broadcasted_iota(jnp.int32, (2 * patches, columns), 0), patches)
    col = lax.broadcasted_iota(jnp.int32, (2 * patches, columns), 1)
    wide_owner = 16 * lax.div(col, 64) + lax.div(lax.rem(col, 64), 8)
    thin_owner = 16 * lax.div(col - plain, 32) + lax.div(lax.rem(col - plain, 32), 4)
    owner = jnp.where(col < plain, wide_owner, thin_owner)
    cores = (c, 1 - c)
    for k in range(2):
        hot = jnp.where(patch == owner + 8 * cores[k], 1.0, 0.0).astype(jnp.bfloat16)
        spread[k] = jnp.dot(weight_ref[...], hot, preferred_element_type=jnp.float32)

    total[...] = jnp.zeros_like(total)
    tile = 256

    def add(group):
        each(jnp.maximum(8 * group, 1), 8 * group + 8, lambda r: row_copy(r).wait_recv())
        block = inbox[pl.ds(8 * group, 8)].reshape(8 * capacity, channels)
        for t in range(channels // tile):
            part = slice(tile * t, tile * (t + 1))
            total[part, :] += lax.dot_general(
                block[:, part], block, (((0,), (0,)), ((), ())), preferred_element_type=jnp.float32
            )

    def settle(t, value):
        high = value.astype(jnp.bfloat16)
        gram_ref[tile * t : tile * (t + 1), :] = high
        gram_ref[channels + tile * t : channels + tile * (t + 1), :] = (value - high.astype(jnp.float32)).astype(
            jnp.bfloat16
        )

    last = patches // 8 - 1

    def send_on(block):
        first = 4 * (block - WINDOW)
        each(jnp.maximum(first, 1), first + 4, lambda r: row_copy(r).wait_send())
        send(block)

    def send_and_add(group):
        send_on(2 * group + WINDOW)
        send_on(2 * group + WINDOW + 1)
        add(group)

    paired = (patches // 4 - WINDOW) // 2
    each(0, paired, send_and_add)
    each(paired, last, add)
    for t in range(channels // tile):
        settle(t, total[tile * t : tile * (t + 1), :])
    each(8 * last, patches, lambda r: row_copy(r).wait_recv())

    def late_rows():
        return inbox[8 * last :].reshape(8 * capacity, channels)

    def settle_late():
        block = late_rows()
        for t in range(channels // tile):
            part = slice(tile * t, tile * (t + 1))
            settle(
                t,
                total[part, :]
                + lax.dot_general(
                    block[:, part], block, (((0,), (0,)), ((), ())), preferred_element_type=jnp.float32
                ),
            )

    width = channels // 2

    def sweep(step, wide, late=False, final=False):
        folds, box, sems = (2, exact, (x_send, x_recv)) if wide else (4, short, (s_send, s_recv))
        at = step % 2 if isinstance(step, int) else lax.rem(step, 2)
        box = box.at[at]
        pieces = two_pieces(q_ref[...])
        lhs = jnp.concatenate([pieces, pieces], axis=1)
        if late:
            y = lax.dot_general(
                pieces, late_rows(), (((1,), (1,)), ((), ())), preferred_element_type=jnp.float32
            )
            y = two_pieces(y[:MODES] + y[MODES:])
        copies = []
        for h in range(2):
            z = jnp.dot(lhs, gram_ref[:, width * h : width * (h + 1)], preferred_element_type=jnp.float32)
            if late:
                z = z + jnp.dot(
                    y, late_rows()[:, width * h : width * (h + 1)], preferred_element_type=jnp.float32
                )
            box[me, h] = stacked(z[:MODES] + z[MODES:], folds).astype(box.dtype)
            for o in (2, 1, 3):
                mine = box.at[me, h]
                copies.append(
                    send_to(mine, mine, sems[0].at[at, 4 * h + o], sems[1].at[at, 4 * h + o], {"zp": ring(me, o)})
                )
                copies[-1].start()
        if late:
            settle_late()
            each(patches - 4 * WINDOW, patches, lambda r: row_copy(r).wait_send())
        for one in copies:
            one.wait_recv()
        halves = []
        for h in range(2):
            whole = box[0, h].astype(jnp.float32)
            for k in range(1, SHARERS):
                whole = whole + box[k, h].astype(jnp.float32)
            halves.append(unstacked(whole, folds))
        whole = jnp.concatenate(halves, axis=1)
        q_ref[...] = orthonormal_rows(whole) if final else orthonormal_pairs(whole)
        for one in copies:
            one.wait_send()

    sweep(0, True, late=True)
    each(1, ITERS - 1, lambda step: sweep(step, False))
    sweep(ITERS - 1, True, final=True)

    blank = jnp.zeros((16 - MODES, channels), jnp.float32)
    own = jnp.concatenate([q_ref[...], blank], axis=0).astype(jnp.bfloat16)
    first, second = ("x", "y"), ("y", "x")
    place = {"x": x, "y": y}

    def pair_at(h, i, o):
        back = {first[h]: ring(place[first[h]], 4 - i), second[h]: ring(place[second[h]], 4 - o)}
        return bases.at[h, back["y"], c, back["x"]]

    def line_at(h, o):
        if h == 0:
            return bases.at[0, ring(y, 4 - o), c]
        return bases.at[1, :, c, ring(x, 4 - o)]

    started = []

    def go(src, sems, at, to):
        one = send_to(src, src, sems[0].at[at], sems[1].at[at], to)
        one.start()
        started.append(one)
        return one

    near = [[None] * 4 for _ in range(2)]
    far = [[[None] * 4 for _ in range(4)] for _ in range(2)]
    pair = []

    def to_first(h):
        for o in (2, 1, 3):
            to = {first[h]: ring(place[first[h]], o)}
            near[h][o] = go(pair_at(h, 0, 0), (a_send, a_recv), 4 * h + o, to)

    def to_second(h, i):
        for o in (2, 1, 3):
            to = {second[h]: ring(place[second[h]], o)}
            far[h][i][o] = go(pair_at(h, i, 0), (b_send, b_recv), 16 * h + 4 * i + o, to)

    def across(h, o):
        return go(line_at(h, o), (c_send, c_recv), 4 * h + o, {"core": 1 - c})

    for h in range(2):
        duo[zl, h] = own[:, width * h : width * (h + 1)]
        pair.append(go(duo.at[zl, h], (p_send, p_recv), h, {"zl": 1 - zl}))
    for h in range(2):
        pair[h].wait_recv()
        one, two = (duo[k, h].astype(jnp.float32) for k in range(2))
        rest = jnp.concatenate([one[8:MODES], two[8:MODES]], axis=0)
        fold = width // 2
        block = jnp.concatenate(
            [
                jnp.concatenate([one[:8], two[:8]], axis=0),
                jnp.concatenate([rest[:, :fold], rest[:, fold:]], axis=0),
            ],
            axis=1,
        )
        bases[h, y, c, x] = block.astype(jnp.bfloat16)
        to_first(h)
        to_second(h, 0)
    for i in (1, 3, 2):
        for h in range(2):
            near[h][i].wait_recv()
            to_second(h, i)
    crossed = [across(0, 0), across(1, 0)]
    for o in (1, 3, 2):
        for h in range(2):
            for i in range(4):
                far[h][i][o].wait_recv()
            crossed.append(across(h, o))

    count = 256
    stores = []

    def project(k):
        for h in range(2):
            block = bases[h, :, cores[k]].reshape(patches // 4, 16, width + width // 2)
            basis[h, :plain] = block[:, :, :width].reshape(plain, width)
            rest = block[:, :, width:].astype(jnp.float32)
            rest = jnp.concatenate([rest[:, :8], rest[:, 8:]], axis=2)
            basis[h, plain:] = rest.reshape(columns - plain, width).astype(jnp.bfloat16)
        for i in range(pixels // count):
            at = pl.ds(count * i, count)
            coefficients = sum(
                lax.dot_general(
                    sky_ref[at, width * h : width * (h + 1)],
                    basis[h],
                    (((1,), (1,)), ((), ())),
                    preferred_element_type=jnp.float32,
                )
                for h in range(2)
            )
            amounts = two_pieces(spread[k, at] * coefficients)
            for h in range(2):
                taken = jnp.dot(amounts, basis[h], preferred_element_type=jnp.float32)
                part = slice(width * h, width * (h + 1))
                left = sky_ref[at, part].astype(jnp.float32) if k == 0 else clean_ref[at, part]
                clean_ref[at, part] = left - (taken[:count] + taken[count:])
            if k == 1:
                stores.append(pltpu.make_async_copy(clean_ref.at[at], clean_hbm.at[at], out_sem.at[i]))
                stores[i].start()

    project(0)
    for one in crossed:
        one.wait_recv()
    project(1)
    for one in started:
        one.wait_send()
    for store in stores:
        store.wait()


def cleaned(index, count, taper, sky, q0):
    capacity, patches = index.shape
    pixels, channels = sky.shape
    sems = lambda *shape: pltpu.SemaphoreType.DMA(shape)
    return pl.pallas_call(
        clean_kernel,
        out_shape=jax.ShapeDtypeStruct((pixels, channels), jnp.float32),
        in_specs=[pl.BlockSpec(memory_space=pl.ANY)] * 5,
        out_specs=pl.BlockSpec(memory_space=pl.ANY),
        scratch_shapes=[
            pltpu.VMEM((pixels, channels), jnp.float32),
            pltpu.VMEM(index.shape, index.dtype),
            pltpu.VMEM(count.shape, count.dtype),
            pltpu.VMEM(taper.shape, taper.dtype),
            pltpu.VMEM(sky.shape, sky.dtype),
            pltpu.VMEM(q0.shape, q0.dtype),
            pltpu.VMEM((2, 2, 16, channels // 2), jnp.bfloat16),
            pltpu.VMEM((2, 4, 2, 4, 16, channels * 3 // 4), jnp.bfloat16),
            pltpu.VMEM((2, patches // 2 * MODES, channels // 2), jnp.bfloat16),
            pltpu.VMEM((pixels, 2 * patches), jnp.bfloat16),
            pltpu.VMEM((2, pixels, patches // 2 * MODES), jnp.float32),
            pltpu.VMEM((patches, capacity, 128), jnp.int32),
            pltpu.VMEM((patches, capacity, channels), jnp.bfloat16),
            pltpu.VMEM((patches, capacity, channels), jnp.bfloat16),
            pltpu.VMEM((channels, channels), jnp.float32),
            pltpu.VMEM((2 * channels, channels), jnp.bfloat16),
            pltpu.VMEM((2, SHARERS, 2, 2 * MODES, channels // 4), jnp.float32),
            pltpu.VMEM((2, SHARERS, 2, 4 * MODES, channels // 8), jnp.bfloat16),
            sems(5),
            sems(2),
            sems(patches), sems(patches),
            sems(2, 8), sems(2, 8), sems(2, 8), sems(2, 8),
            sems(2), sems(2), sems(8), sems(8), sems(32), sems(32), sems(8), sems(8),
        ],
        compiler_params=pltpu.CompilerParams(
            collective_id=0, has_side_effects=True, vmem_limit_bytes=VMEM_MIB * MIB
        ),
    )(index, count, taper, sky, q0)


def copy_kernel(from_ref, to_ref, held, in_sem, out_sem):
    chunks = in_sem.shape[0]
    count = held.shape[0] // chunks
    parts = [pl.ds(count * i, count) for i in range(chunks)]
    loads = [pltpu.make_async_copy(from_ref.at[p], held.at[p], in_sem.at[i]) for i, p in enumerate(parts)]
    stores = [pltpu.make_async_copy(held.at[p], to_ref.at[p], out_sem.at[i]) for i, p in enumerate(parts)]
    for load in loads:
        load.start()
    for load, store in zip(loads, stores):
        load.wait()
        store.start()
    for store in stores:
        store.wait()


def copied(array):
    anywhere = pl.BlockSpec(memory_space=pl.ANY)
    return pl.pallas_call(
        copy_kernel,
        out_shape=jax.ShapeDtypeStruct(array.shape, array.dtype),
        in_specs=[anywhere],
        out_specs=anywhere,
        scratch_shapes=[
            pltpu.VMEM(array.shape, array.dtype),
            pltpu.SemaphoreType.DMA((8,)),
            pltpu.SemaphoreType.DMA((8,)),
        ],
        compiler_params=pltpu.CompilerParams(vmem_limit_bytes=VMEM_MIB * MIB),
    )(array)


def local(sky, send_index, send_count, taper, start_basis):
    patches, capacity = send_index.shape[2:]
    index = send_index.reshape(patches, capacity).T
    count = send_count.reshape(1, patches)
    return copied(cleaned(index, count, taper.reshape(patches, capacity).T, sky, start_basis.T))


def solution(mesh):
    fine = Mesh(mesh.devices.reshape(4, SHARERS, 2, 2, 4), ("y", "zp", "zl", "core", "x"))
    patch = ("y", "zp", "zl", "core")
    rows = P((*patch, "x"), None)
    placed = (rows, P(patch, "x", None, None), P(patch, "x", None), P(patch, "x", None, None), P())
    return jax.shard_map(local, mesh=fine, in_specs=placed, out_specs=rows, check_vma=False)
```

```python
import jax
import jax.numpy as jnp
from jax import lax
from jax.experimental import pallas as pl
from jax.experimental.pallas import tpu as pltpu
from jax.sharding import Mesh, PartitionSpec as P

ITERS = 6
MODES = 12
SHARERS = 4
CELL = ("y", "core", "x", "zl")
MESH = pl.DeviceIdType.MESH
MIB = 1 << 20
VMEM_MIB = 56
WINDOW = 4


def two_pieces(value):
    high = value.astype(jnp.bfloat16).astype(jnp.float32)
    return jnp.concatenate([high, value - high], axis=0).astype(jnp.bfloat16)


def orthonormal_rows(v):
    row = lax.broadcasted_iota(jnp.int32, (MODES, 1), 0)
    norms = jnp.zeros((MODES, 1), jnp.float32)
    for k in range(MODES):
        lead = v[k : k + 1]
        dots = jnp.sum(v * lead, axis=1, keepdims=True)
        norms = jnp.where(row == k, dots, norms)
        if k + 1 < MODES:
            v = v - jnp.where(row > k, dots / (dots[k : k + 1] + 1e-12), 0.0) * lead
    return v * (1.0 / jnp.sqrt(norms + 1e-12))


def orthonormal_pairs(v):
    row = lax.broadcasted_iota(jnp.int32, (MODES, 1), 0)
    norms = jnp.ones((MODES, 1), jnp.float32)
    for k in range(0, MODES, 2):
        a, b = v[k : k + 1], v[k + 1 : k + 2]
        on_a = jnp.sum(v * a, axis=1, keepdims=True)
        on_b = jnp.sum(v * b, axis=1, keepdims=True)
        aa, ab, bb = on_a[k : k + 1], on_a[k + 1 : k + 2], on_b[k + 1 : k + 2]
        by_a = on_a / (aa + 1e-12)
        c = by_a[k + 1 : k + 2]
        rest = jnp.maximum(bb - 2.0 * c * ab + c * c * aa, 1e-6 * bb)
        on_rest = on_b - c * on_a - by_a * ab + by_a * (c * aa)
        by_rest = jnp.where(row > k + 1, on_rest / (rest + 1e-12), 0.0)
        v = v - (jnp.where(row > k, by_a, 0.0) - by_rest * c) * a - by_rest * b
        norms = jnp.where(row == k, aa, jnp.where(row == k + 1, rest, norms))
    return v * (1.0 / jnp.sqrt(norms + 1e-12))


def stacked(z, folds):
    width = z.shape[1] // folds
    return jnp.concatenate([z[:, width * f : width * (f + 1)] for f in range(folds)], axis=0)


def unstacked(z, folds):
    return jnp.concatenate([z[MODES * f : MODES * (f + 1)] for f in range(folds)], axis=1)


def each(first, last, step):
    def body(i, carry):
        step(i)
        return carry

    lax.fori_loop(first, last, body, 0)


def ring(at, o):
    return lax.rem(at + o, 4)


def send_to(src, dst, send_sem, recv_sem, to):
    return pltpu.make_async_remote_copy(
        src_ref=src, dst_ref=dst, send_sem=send_sem, recv_sem=recv_sem, device_id=to, device_id_type=MESH
    )


def clean_kernel(
    index_hbm, count_hbm, taper_hbm, sky_hbm, q0_hbm, clean_hbm,
    clean_ref, index_ref, count_ref, taper_ref, sky_ref, q_ref, duo, bases, basis, weight_ref, spread, column, rows, inbox, total, gram_ref, exact, short,
    in_sem, out_sem, row_send, row_recv, x_send, x_recv, s_send, s_recv,
    p_send, p_recv, a_send, a_recv, b_send, b_recv, c_send, c_recv,
):
    me = lax.axis_index("zp")
    y, c, x, zl = (lax.axis_index(name) for name in CELL)
    capacity, patches = index_ref.shape
    pixels, channels = sky_ref.shape

    sources = (index_hbm, count_hbm, sky_hbm, taper_hbm, q0_hbm)
    places = (index_ref, count_ref, sky_ref, taper_ref, q_ref)
    loads = [pltpu.make_async_copy(f, t, in_sem.at[i]) for i, (f, t) in enumerate(zip(sources, places))]
    for load in loads:
        load.start()

    def peer(r):
        o = lax.rem(r * 37, patches)
        to = {
            "x": ring(x, lax.rem(o, 4)),
            "y": ring(y, lax.rem(lax.div(o, 4), 4)),
            "core": lax.rem(c + lax.rem(lax.div(o, 16), 2), 2),
            "zl": lax.rem(zl + lax.div(o, 32), 2),
        }
        return to, ((to["y"] * 2 + to["core"]) * 4 + to["x"]) * 2 + to["zl"]

    def row_copy(r):
        return send_to(rows.at[r], inbox.at[r], row_send.at[r], row_recv.at[r], peer(r)[0])

    barrier = pltpu.get_barrier_semaphore()
    at_x, at_y = [ring(x, o) for o in range(4)], [ring(y, o) for o in range(4)]
    for o in range(1, patches):
        to = {
            "x": at_x[o % 4],
            "y": at_y[o // 4 % 4],
            "core": 1 - c if o // 16 % 2 else c,
            "zl": 1 - zl if o // 32 else zl,
        }
        pl.semaphore_signal(barrier, inc=1, device_id=to, device_id_type=MESH)
    for o in range(1, SHARERS):
        pl.semaphore_signal(barrier, inc=1, device_id={"zp": ring(me, o)}, device_id_type=MESH)

    loads[0].wait()
    loads[1].wait()
    slot = lax.broadcasted_iota(jnp.int32, (capacity, patches), 0)
    index = jnp.where(slot < count_ref[...], index_ref[...], -1)
    for d in range(patches):
        column[d] = jnp.broadcast_to(index[:, d : d + 1], (capacity, 128))
    lane = lax.broadcasted_iota(jnp.int32, (4 * capacity, 128), 1)
    loads[2].wait()

    def pick(block):
        near = jnp.concatenate([column[peer(4 * block + j)[1]] for j in range(4)], axis=0)
        hot = [jnp.where(near == lane + 128 * t, 1.0, 0.0) for t in range(pixels // 128)]
        hot = jnp.concatenate(hot, axis=1).astype(jnp.bfloat16)
        found = jnp.dot(hot, sky_ref[...], preferred_element_type=jnp.float32).astype(jnp.bfloat16)
        for j in range(4):
            rows[4 * block + j] = found[capacity * j : capacity * (j + 1)]

    pick(0)
    pl.semaphore_wait(barrier, patches - 1 + SHARERS - 1)
    for j in range(1, 4):
        row_copy(j).start()

    def send(block):
        pick(block)
        for j in range(4):
            row_copy(4 * block + j).start()

    each(1, WINDOW, send)
    inbox[0] = rows[0]

    loads[3].wait()
    loads[4].wait()
    for part in range(pixels // 128):
        pixel = 128 * part + lax.broadcasted_iota(jnp.int32, (128, patches), 0)
        weights = jnp.zeros((128, patches), jnp.float32)
        for j in range(capacity):
            weights = weights + jnp.where(index[j : j + 1, :] == pixel, taper_ref[j : j + 1, :], 0.0)
        whole = jnp.sum(weights, axis=1, keepdims=True)
        weights = weights / jnp.where(whole > 0, whole, 1.0)
        high = weights.astype(jnp.bfloat16).astype(jnp.float32)
        weight_ref[128 * part : 128 * (part + 1), :] = jnp.concatenate([high, weights - high], axis=1).astype(
            jnp.bfloat16
        )

    plain = patches // 4 * 16
    columns = patches // 2 * MODES
    patch = lax.rem(lax.broadcasted_iota(jnp.int32, (2 * patches, columns), 0), patches)
    col = lax.broadcasted_iota(jnp.int32, (2 * patches, columns), 1)
    wide_owner = 16 * lax.div(col, 64) + lax.div(lax.rem(col, 64), 8)
    thin_owner = 16 * lax.div(col - plain, 32) + lax.div(lax.rem(col - plain, 32), 4)
    owner = jnp.where(col < plain, wide_owner, thin_owner)
    cores = (c, 1 - c)
    for k in range(2):
        hot = jnp.where(patch == owner + 8 * cores[k], 1.0, 0.0).astype(jnp.bfloat16)
        spread[k] = jnp.dot(weight_ref[...], hot, preferred_element_type=jnp.float32)

    total[...] = jnp.zeros_like(total)
    tile = 256

    def add(group):
        each(jnp.maximum(8 * group, 1), 8 * group + 8, lambda r: row_copy(r).wait_recv())
        block = inbox[pl.ds(8 * group, 8)].reshape(8 * capacity, channels)
        for t in range(channels // tile):
            part = slice(tile * t, tile * (t + 1))
            total[part, :] += lax.dot_general(
                block[:, part], block, (((0,), (0,)), ((), ())), preferred_element_type=jnp.float32
            )

    def settle(t, value):
        high = value.astype(jnp.bfloat16)
        gram_ref[tile * t : tile * (t + 1), :] = high
        gram_ref[channels + tile * t : channels + tile * (t + 1), :] = (value - high.astype(jnp.float32)).astype(
            jnp.bfloat16
        )

    last = patches // 8 - 1

    def send_on(block):
        first = 4 * (block - WINDOW)
        each(jnp.maximum(first, 1), first + 4, lambda r: row_copy(r).wait_send())
        send(block)

    def send_and_add(group):
        send_on(2 * group + WINDOW)
        send_on(2 * group + WINDOW + 1)
        add(group)

    paired = (patches // 4 - WINDOW) // 2
    each(0, paired, send_and_add)
    each(paired, last, add)
    for t in range(channels // tile):
        settle(t, total[tile * t : tile * (t + 1), :])
    each(8 * last, patches, lambda r: row_copy(r).wait_recv())

    def late_rows():
        return inbox[8 * last :].reshape(8 * capacity, channels)

    def settle_late():
        block = late_rows()
        for t in range(channels // tile):
            part = slice(tile * t, tile * (t + 1))
            settle(
                t,
                total[part, :]
                + lax.dot_general(
                    block[:, part], block, (((0,), (0,)), ((), ())), preferred_element_type=jnp.float32
                ),
            )

    width = channels // 2

    odd = lax.rem(me, 2)
    started = []

    def product(pieces, h):
        lhs = jnp.concatenate([pieces, pieces], axis=1)
        z = jnp.dot(lhs, gram_ref[:, width * h : width * (h + 1)], preferred_element_type=jnp.float32)
        return z[:MODES] + z[MODES:]

    def swap(at, h, turn, value):
        box = exact.at[at, h, turn]
        box[0] = value
        to = ring(me, 1 + 2 * odd if (h + turn) % 2 == 0 else 3 - 2 * odd)
        sem = (2 * at + h) * 2 + turn
        one = send_to(box.at[0], box.at[1], x_send.at[sem], x_recv.at[sem], {"zp": to})
        one.start()
        started.append(one)
        return one

    def exact_sweep(at, late):
        pieces = two_pieces(q_ref[...])
        if late:
            y = lax.dot_general(
                pieces, late_rows(), (((1,), (1,)), ((), ())), preferred_element_type=jnp.float32
            )
            y = two_pieces(y[:MODES] + y[MODES:])
        copies = []
        for h in range(2):
            z = product(pieces, h)
            if late:
                part = late_rows()[:, width * h : width * (h + 1)]
                rest = jnp.dot(y, part, preferred_element_type=jnp.float32)
                z = z + rest[:MODES] + rest[MODES:]
            copies.append(swap(at, h, 0, stacked(z, 2)))
        if late:
            settle_late()
            each(patches - 4 * WINDOW, patches, lambda r: row_copy(r).wait_send())
        for turn in range(2):
            sums = []
            for h in range(2):
                copies[h].wait_recv()
                sums.append(exact[at, h, turn, 0] + exact[at, h, turn, 1])
                if turn == 0:
                    copies[h] = swap(at, h, 1, sums[h])
        return jnp.concatenate([unstacked(one, 2) for one in sums], axis=1)

    def short_sweep(step):
        at = lax.rem(step, 2)
        box = short.at[at]
        pieces = two_pieces(q_ref[...])
        copies = []
        for h in range(2):
            box[me, h] = stacked(product(pieces, h), 4).astype(box.dtype)
            for o in (2, 1, 3):
                mine = box.at[me, h]
                copies.append(
                    send_to(mine, mine, s_send.at[at, 4 * h + o], s_recv.at[at, 4 * h + o], {"zp": ring(me, o)})
                )
                copies[-1].start()
        for one in copies:
            one.wait_recv()
        halves = []
        for h in range(2):
            whole = box[0, h].astype(jnp.float32)
            for k in range(1, SHARERS):
                whole = whole + box[k, h].astype(jnp.float32)
            halves.append(unstacked(whole, 4))
        q_ref[...] = orthonormal_pairs(jnp.concatenate(halves, axis=1))
        for one in copies:
            one.wait_send()

    q_ref[...] = orthonormal_pairs(exact_sweep(0, True))
    each(1, ITERS - 1, short_sweep)
    q_ref[...] = orthonormal_rows(exact_sweep(1, False))

    blank = jnp.zeros((16 - MODES, channels), jnp.float32)
    own = jnp.concatenate([q_ref[...], blank], axis=0).astype(jnp.bfloat16)
    first, second = ("x", "y"), ("y", "x")
    place = {"x": x, "y": y}

    def pair_at(h, i, o):
        back = {first[h]: ring(place[first[h]], 4 - i), second[h]: ring(place[second[h]], 4 - o)}
        return bases.at[h, back["y"], c, back["x"]]

    def line_at(h, o):
        if h == 0:
            return bases.at[0, ring(y, 4 - o), c]
        return bases.at[1, :, c, ring(x, 4 - o)]

    def go(src, sems, at, to):
        one = send_to(src, src, sems[0].at[at], sems[1].at[at], to)
        one.start()
        started.append(one)
        return one

    near = [[None] * 4 for _ in range(2)]
    far = [[[None] * 4 for _ in range(4)] for _ in range(2)]
    pair = []

    def to_first(h):
        for o in (2, 1, 3):
            to = {first[h]: ring(place[first[h]], o)}
            near[h][o] = go(pair_at(h, 0, 0), (a_send, a_recv), 4 * h + o, to)

    def to_second(h, i):
        for o in (2, 1, 3):
            to = {second[h]: ring(place[second[h]], o)}
            far[h][i][o] = go(pair_at(h, i, 0), (b_send, b_recv), 16 * h + 4 * i + o, to)

    def across(h, o):
        return go(line_at(h, o), (c_send, c_recv), 4 * h + o, {"core": 1 - c})

    for h in range(2):
        duo[zl, h] = own[:, width * h : width * (h + 1)]
        pair.append(go(duo.at[zl, h], (p_send, p_recv), h, {"zl": 1 - zl}))
    for h in range(2):
        pair[h].wait_recv()
        one, two = (duo[k, h].astype(jnp.float32) for k in range(2))
        rest = jnp.concatenate([one[8:MODES], two[8:MODES]], axis=0)
        fold = width // 2
        block = jnp.concatenate(
            [
                jnp.concatenate([one[:8], two[:8]], axis=0),
                jnp.concatenate([rest[:, :fold], rest[:, fold:]], axis=0),
            ],
            axis=1,
        )
        bases[h, y, c, x] = block.astype(jnp.bfloat16)
        to_first(h)
        to_second(h, 0)
    for i in (1, 3, 2):
        for h in range(2):
            near[h][i].wait_recv()
            to_second(h, i)
    crossed = [across(0, 0), across(1, 0)]
    for o in (1, 3, 2):
        for h in range(2):
            for i in range(4):
                far[h][i][o].wait_recv()
            crossed.append(across(h, o))

    count = 256
    stores = []

    def project(k):
        for h in range(2):
            block = bases[h, :, cores[k]].reshape(patches // 4, 16, width + width // 2)
            basis[h, :plain] = block[:, :, :width].reshape(plain, width)
            rest = block[:, :, width:].astype(jnp.float32)
            rest = jnp.concatenate([rest[:, :8], rest[:, 8:]], axis=2)
            basis[h, plain:] = rest.reshape(columns - plain, width).astype(jnp.bfloat16)
        for i in range(pixels // count):
            at = pl.ds(count * i, count)
            coefficients = sum(
                lax.dot_general(
                    sky_ref[at, width * h : width * (h + 1)],
                    basis[h],
                    (((1,), (1,)), ((), ())),
                    preferred_element_type=jnp.float32,
                )
                for h in range(2)
            )
            amounts = two_pieces(spread[k, at] * coefficients)
            for h in range(2):
                taken = jnp.dot(amounts, basis[h], preferred_element_type=jnp.float32)
                part = slice(width * h, width * (h + 1))
                left = sky_ref[at, part].astype(jnp.float32) if k == 0 else clean_ref[at, part]
                clean_ref[at, part] = left - (taken[:count] + taken[count:])
            if k == 1:
                stores.append(pltpu.make_async_copy(clean_ref.at[at], clean_hbm.at[at], out_sem.at[i]))
                stores[i].start()

    project(0)
    for one in crossed:
        one.wait_recv()
    project(1)
    for one in started:
        one.wait_send()
    for store in stores:
        store.wait()


def cleaned(index, count, taper, sky, q0):
    capacity, patches = index.shape
    pixels, channels = sky.shape
    sems = lambda *shape: pltpu.SemaphoreType.DMA(shape)
    return pl.pallas_call(
        clean_kernel,
        out_shape=jax.ShapeDtypeStruct((pixels, channels), jnp.float32),
        in_specs=[pl.BlockSpec(memory_space=pl.ANY)] * 5,
        out_specs=pl.BlockSpec(memory_space=pl.ANY),
        scratch_shapes=[
            pltpu.VMEM((pixels, channels), jnp.float32),
            pltpu.VMEM(index.shape, index.dtype),
            pltpu.VMEM(count.shape, count.dtype),
            pltpu.VMEM(taper.shape, taper.dtype),
            pltpu.VMEM(sky.shape, sky.dtype),
            pltpu.VMEM(q0.shape, q0.dtype),
            pltpu.VMEM((2, 2, 16, channels // 2), jnp.bfloat16),
            pltpu.VMEM((2, 4, 2, 4, 16, channels * 3 // 4), jnp.bfloat16),
            pltpu.VMEM((2, patches // 2 * MODES, channels // 2), jnp.bfloat16),
            pltpu.VMEM((pixels, 2 * patches), jnp.bfloat16),
            pltpu.VMEM((2, pixels, patches // 2 * MODES), jnp.float32),
            pltpu.VMEM((patches, capacity, 128), jnp.int32),
            pltpu.VMEM((patches, capacity, channels), jnp.bfloat16),
            pltpu.VMEM((patches, capacity, channels), jnp.bfloat16),
            pltpu.VMEM((channels, channels), jnp.float32),
            pltpu.VMEM((2 * channels, channels), jnp.bfloat16),
            pltpu.VMEM((2, 2, 2, 2, 2 * MODES, channels // 4), jnp.float32),
            pltpu.VMEM((2, SHARERS, 2, 4 * MODES, channels // 8), jnp.bfloat16),
            sems(5),
            sems(2),
            sems(patches), sems(patches),
            sems(8), sems(8), sems(2, 8), sems(2, 8),
            sems(2), sems(2), sems(8), sems(8), sems(32), sems(32), sems(8), sems(8),
        ],
        compiler_params=pltpu.CompilerParams(
            collective_id=0, has_side_effects=True, vmem_limit_bytes=VMEM_MIB * MIB
        ),
    )(index, count, taper, sky, q0)


def copy_kernel(from_ref, to_ref, held, in_sem, out_sem):
    chunks = in_sem.shape[0]
    count = held.shape[0] // chunks
    parts = [pl.ds(count * i, count) for i in range(chunks)]
    loads = [pltpu.make_async_copy(from_ref.at[p], held.at[p], in_sem.at[i]) for i, p in enumerate(parts)]
    stores = [pltpu.make_async_copy(held.at[p], to_ref.at[p], out_sem.at[i]) for i, p in enumerate(parts)]
    for load in loads:
        load.start()
    for load, store in zip(loads, stores):
        load.wait()
        store.start()
    for store in stores:
        store.wait()


def copied(array):
    anywhere = pl.BlockSpec(memory_space=pl.ANY)
    return pl.pallas_call(
        copy_kernel,
        out_shape=jax.ShapeDtypeStruct(array.shape, array.dtype),
        in_specs=[anywhere],
        out_specs=anywhere,
        scratch_shapes=[
            pltpu.VMEM(array.shape, array.dtype),
            pltpu.SemaphoreType.DMA((8,)),
            pltpu.SemaphoreType.DMA((8,)),
        ],
        compiler_params=pltpu.CompilerParams(vmem_limit_bytes=VMEM_MIB * MIB),
    )(array)


def local(sky, send_index, send_count, taper, start_basis):
    patches, capacity = send_index.shape[2:]
    index = send_index.reshape(patches, capacity).T
    count = send_count.reshape(1, patches)
    return copied(cleaned(index, count, taper.reshape(patches, capacity).T, sky, start_basis.T))


def solution(mesh):
    fine = Mesh(mesh.devices.reshape(4, SHARERS, 2, 2, 4), ("y", "zp", "zl", "core", "x"))
    patch = ("y", "zp", "zl", "core")
    rows = P((*patch, "x"), None)
    placed = (rows, P(patch, "x", None, None), P(patch, "x", None), P(patch, "x", None, None), P())
    return jax.shard_map(local, mesh=fine, in_specs=placed, out_specs=rows, check_vma=False)
```

```python
import jax
import jax.numpy as jnp
from jax import lax
from jax.experimental import pallas as pl
from jax.experimental.pallas import tpu as pltpu
from jax.sharding import Mesh, PartitionSpec as P

ITERS = 6
MODES = 12
SHARERS = 4
CELL = ("y", "core", "x", "zl")
MESH = pl.DeviceIdType.MESH
MIB = 1 << 20
VMEM_MIB = 56
WINDOW = 4


def two_pieces(value):
    high = value.astype(jnp.bfloat16).astype(jnp.float32)
    return jnp.concatenate([high, value - high], axis=0).astype(jnp.bfloat16)


def orthonormal_rows(v):
    row = lax.broadcasted_iota(jnp.int32, (MODES, 1), 0)
    norms = jnp.zeros((MODES, 1), jnp.float32)
    for k in range(MODES):
        lead = v[k : k + 1]
        dots = jnp.sum(v * lead, axis=1, keepdims=True)
        norms = jnp.where(row == k, dots, norms)
        if k + 1 < MODES:
            v = v - jnp.where(row > k, dots / (dots[k : k + 1] + 1e-12), 0.0) * lead
    return v * (1.0 / jnp.sqrt(norms + 1e-12))


def orthonormal_pairs(v):
    row = lax.broadcasted_iota(jnp.int32, (MODES, 1), 0)
    norms = jnp.ones((MODES, 1), jnp.float32)
    for k in range(0, MODES, 2):
        a, b = v[k : k + 1], v[k + 1 : k + 2]
        on_a = jnp.sum(v * a, axis=1, keepdims=True)
        on_b = jnp.sum(v * b, axis=1, keepdims=True)
        aa, ab, bb = on_a[k : k + 1], on_a[k + 1 : k + 2], on_b[k + 1 : k + 2]
        by_a = on_a / (aa + 1e-12)
        c = by_a[k + 1 : k + 2]
        rest = jnp.maximum(bb - 2.0 * c * ab + c * c * aa, 1e-6 * bb)
        on_rest = on_b - c * on_a - by_a * ab + by_a * (c * aa)
        by_rest = jnp.where(row > k + 1, on_rest / (rest + 1e-12), 0.0)
        v = v - (jnp.where(row > k, by_a, 0.0) - by_rest * c) * a - by_rest * b
        norms = jnp.where(row == k, aa, jnp.where(row == k + 1, rest, norms))
    return v * (1.0 / jnp.sqrt(norms + 1e-12))


def stacked(z, folds):
    width = z.shape[1] // folds
    return jnp.concatenate([z[:, width * f : width * (f + 1)] for f in range(folds)], axis=0)


def unstacked(z, folds):
    return jnp.concatenate([z[MODES * f : MODES * (f + 1)] for f in range(folds)], axis=1)


def each(first, last, step):
    def body(i, carry):
        step(i)
        return carry

    lax.fori_loop(first, last, body, 0)


def ring(at, o):
    return lax.rem(at + o, 4)


def send_to(src, dst, send_sem, recv_sem, to):
    return pltpu.make_async_remote_copy(
        src_ref=src, dst_ref=dst, send_sem=send_sem, recv_sem=recv_sem, device_id=to, device_id_type=MESH
    )


def clean_kernel(
    index_hbm, count_hbm, taper_hbm, sky_hbm, q0_hbm, clean_hbm,
    clean_ref, index_ref, count_ref, taper_ref, sky_ref, q_ref, bases, basis, weight_ref, spread, column, rows, inbox, total, gram_ref, exact, short,
    in_sem, out_sem, row_send, row_recv, x_send, x_recv, s_send, s_recv,
    a_send, a_recv, b_send, b_recv, c_send, c_recv,
):
    me = lax.axis_index("zp")
    y, c, x, zl = (lax.axis_index(name) for name in CELL)
    capacity, patches = index_ref.shape
    pixels, channels = sky_ref.shape

    sources = (index_hbm, count_hbm, sky_hbm, taper_hbm, q0_hbm)
    places = (index_ref, count_ref, sky_ref, taper_ref, q_ref)
    loads = [pltpu.make_async_copy(f, t, in_sem.at[i]) for i, (f, t) in enumerate(zip(sources, places))]
    for load in loads:
        load.start()

    def peer(r):
        o = lax.rem(r * 37, patches)
        to = {
            "x": ring(x, lax.rem(o, 4)),
            "y": ring(y, lax.rem(lax.div(o, 4), 4)),
            "core": lax.rem(c + lax.rem(lax.div(o, 16), 2), 2),
            "zl": lax.rem(zl + lax.div(o, 32), 2),
        }
        return to, ((to["y"] * 2 + to["core"]) * 4 + to["x"]) * 2 + to["zl"]

    def row_copy(r):
        return send_to(rows.at[r], inbox.at[r], row_send.at[r], row_recv.at[r], peer(r)[0])

    barrier = pltpu.get_barrier_semaphore()
    at_x, at_y = [ring(x, o) for o in range(4)], [ring(y, o) for o in range(4)]
    for o in range(1, patches):
        to = {
            "x": at_x[o % 4],
            "y": at_y[o // 4 % 4],
            "core": 1 - c if o // 16 % 2 else c,
            "zl": 1 - zl if o // 32 else zl,
        }
        pl.semaphore_signal(barrier, inc=1, device_id=to, device_id_type=MESH)
    for o in range(1, SHARERS):
        pl.semaphore_signal(barrier, inc=1, device_id={"zp": ring(me, o)}, device_id_type=MESH)

    loads[0].wait()
    loads[1].wait()
    slot = lax.broadcasted_iota(jnp.int32, (capacity, patches), 0)
    index = jnp.where(slot < count_ref[...], index_ref[...], -1)
    for d in range(patches):
        column[d] = jnp.broadcast_to(index[:, d : d + 1], (capacity, 128))
    lane = lax.broadcasted_iota(jnp.int32, (4 * capacity, 128), 1)
    loads[2].wait()

    def pick(block):
        near = jnp.concatenate([column[peer(4 * block + j)[1]] for j in range(4)], axis=0)
        hot = [jnp.where(near == lane + 128 * t, 1.0, 0.0) for t in range(pixels // 128)]
        hot = jnp.concatenate(hot, axis=1).astype(jnp.bfloat16)
        found = jnp.dot(hot, sky_ref[...], preferred_element_type=jnp.float32).astype(jnp.bfloat16)
        for j in range(4):
            rows[4 * block + j] = found[capacity * j : capacity * (j + 1)]

    pick(0)
    pl.semaphore_wait(barrier, patches - 1 + SHARERS - 1)
    for j in range(1, 4):
        row_copy(j).start()

    def send(block):
        pick(block)
        for j in range(4):
            row_copy(4 * block + j).start()

    each(1, WINDOW, send)
    inbox[0] = rows[0]

    loads[3].wait()
    loads[4].wait()
    for part in range(pixels // 128):
        pixel = 128 * part + lax.broadcasted_iota(jnp.int32, (128, patches), 0)
        weights = jnp.zeros((128, patches), jnp.float32)
        for j in range(capacity):
            weights = weights + jnp.where(index[j : j + 1, :] == pixel, taper_ref[j : j + 1, :], 0.0)
        whole = jnp.sum(weights, axis=1, keepdims=True)
        weights = weights / jnp.where(whole > 0, whole, 1.0)
        high = weights.astype(jnp.bfloat16).astype(jnp.float32)
        weight_ref[128 * part : 128 * (part + 1), :] = jnp.concatenate([high, weights - high], axis=1).astype(
            jnp.bfloat16
        )

    plain = patches // 4 * 16
    columns = patches // 2 * MODES
    patch = lax.rem(lax.broadcasted_iota(jnp.int32, (2 * patches, columns), 0), patches)
    col = lax.broadcasted_iota(jnp.int32, (2 * patches, columns), 1)
    wide_owner = 16 * lax.div(col, 64) + lax.div(lax.rem(col, 64), 8)
    thin_owner = 16 * lax.div(col - plain, 32) + lax.div(lax.rem(col - plain, 32), 4)
    owner = jnp.where(col < plain, wide_owner, thin_owner)
    cores = (c, 1 - c)
    for k in range(2):
        hot = jnp.where(patch == owner + 8 * cores[k], 1.0, 0.0).astype(jnp.bfloat16)
        spread[k] = jnp.dot(weight_ref[...], hot, preferred_element_type=jnp.float32)

    total[...] = jnp.zeros_like(total)
    tile = 256

    def add(group):
        each(jnp.maximum(8 * group, 1), 8 * group + 8, lambda r: row_copy(r).wait_recv())
        block = inbox[pl.ds(8 * group, 8)].reshape(8 * capacity, channels)
        for t in range(channels // tile):
            part = slice(tile * t, tile * (t + 1))
            total[part, :] += lax.dot_general(
                block[:, part], block, (((0,), (0,)), ((), ())), preferred_element_type=jnp.float32
            )

    def settle(t, value):
        high = value.astype(jnp.bfloat16)
        gram_ref[tile * t : tile * (t + 1), :] = high
        gram_ref[channels + tile * t : channels + tile * (t + 1), :] = (value - high.astype(jnp.float32)).astype(
            jnp.bfloat16
        )

    last = patches // 8 - 1

    def send_on(block):
        first = 4 * (block - WINDOW)
        each(jnp.maximum(first, 1), first + 4, lambda r: row_copy(r).wait_send())
        send(block)

    def send_and_add(group):
        send_on(2 * group + WINDOW)
        send_on(2 * group + WINDOW + 1)
        add(group)

    paired = (patches // 4 - WINDOW) // 2
    each(0, paired, send_and_add)
    each(paired, last, add)
    for t in range(channels // tile):
        settle(t, total[tile * t : tile * (t + 1), :])
    each(8 * last, patches, lambda r: row_copy(r).wait_recv())

    def late_rows():
        return inbox[8 * last :].reshape(8 * capacity, channels)

    def settle_late():
        block = late_rows()
        for t in range(channels // tile):
            part = slice(tile * t, tile * (t + 1))
            settle(
                t,
                total[part, :]
                + lax.dot_general(
                    block[:, part], block, (((0,), (0,)), ((), ())), preferred_element_type=jnp.float32
                ),
            )

    width = channels // 2

    def sweep(step, wide, late=False, final=False):
        folds, box, sems = (2, exact, (x_send, x_recv)) if wide else (4, short, (s_send, s_recv))
        at = step % 2 if isinstance(step, int) else lax.rem(step, 2)
        box = box.at[at]
        pieces = two_pieces(q_ref[...])
        lhs = jnp.concatenate([pieces, pieces], axis=1)
        if late:
            y = lax.dot_general(
                pieces, late_rows(), (((1,), (1,)), ((), ())), preferred_element_type=jnp.float32
            )
            y = two_pieces(y[:MODES] + y[MODES:])
        copies = []
        for h in range(2):
            z = jnp.dot(lhs, gram_ref[:, width * h : width * (h + 1)], preferred_element_type=jnp.float32)
            if late:
                z = z + jnp.dot(
                    y, late_rows()[:, width * h : width * (h + 1)], preferred_element_type=jnp.float32
                )
            box[me, h] = stacked(z[:MODES] + z[MODES:], folds).astype(box.dtype)
            for o in (2, 1, 3):
                mine = box.at[me, h]
                copies.append(
                    send_to(mine, mine, sems[0].at[at, 4 * h + o], sems[1].at[at, 4 * h + o], {"zp": ring(me, o)})
                )
                copies[-1].start()
        if late:
            settle_late()
            each(patches - 4 * WINDOW, patches, lambda r: row_copy(r).wait_send())
        for one in copies:
            one.wait_recv()
        halves = []
        for h in range(2):
            whole = box[0, h].astype(jnp.float32)
            for k in range(1, SHARERS):
                whole = whole + box[k, h].astype(jnp.float32)
            halves.append(unstacked(whole, folds))
        whole = jnp.concatenate(halves, axis=1)
        q_ref[...] = orthonormal_rows(whole) if final else orthonormal_pairs(whole)
        for one in copies:
            one.wait_send()

    sweep(0, True, late=True)
    each(1, ITERS - 1, lambda step: sweep(step, False))
    sweep(ITERS - 1, True, final=True)

    fold, thin = width // 2, width // 4
    first, second = ("x", "y"), ("y", "x")
    place = {"x": x, "y": y}

    def pair_at(h, i, o):
        back = {first[h]: ring(place[first[h]], 4 - i), second[h]: ring(place[second[h]], 4 - o)}
        return bases.at[h, back["y"], c, back["x"]]

    def block_of(q):
        wide, rest = q[:8], q[8:]
        return jnp.concatenate(
            [
                jnp.concatenate([wide[:, :fold], wide[:, fold:]], axis=0),
                jnp.concatenate([rest[:, thin * j : thin * (j + 1)] for j in range(4)], axis=0),
            ],
            axis=1,
        )

    def line_at(h, o):
        if h == 0:
            return bases.at[0, ring(y, 4 - o), c]
        return bases.at[1, :, c, ring(x, 4 - o)]

    started = []

    def go(src, sems, at, to):
        one = send_to(src, src, sems[0].at[at], sems[1].at[at], to)
        one.start()
        started.append(one)
        return one

    near = [[[None] * 2 for _ in range(4)] for _ in range(2)]
    far = [[[None] * 4 for _ in range(4)] for _ in range(2)]

    def to_first(h):
        mine = bases.at[h, y, c, x, zl]
        for o in (2, 1, 3, 0):
            for j in range(2):
                if o + j:
                    to = {first[h]: ring(place[first[h]], o), "zl": 1 - zl if j else zl}
                    near[h][o][j] = go(mine, (a_send, a_recv), 8 * h + 2 * o + j, to)

    def to_second(h, i):
        for o in (2, 1, 3):
            to = {second[h]: ring(place[second[h]], o)}
            far[h][i][o] = go(pair_at(h, i, 0), (b_send, b_recv), 16 * h + 4 * i + o, to)

    def across(h, o):
        return go(line_at(h, o), (c_send, c_recv), 4 * h + o, {"core": 1 - c})

    for h in range(2):
        bases[h, y, c, x, zl] = block_of(q_ref[:, width * h : width * (h + 1)]).astype(jnp.bfloat16)
        to_first(h)
    for i in (0, 1, 3, 2):
        for h in range(2):
            for j in range(2):
                if i + j:
                    near[h][i][j].wait_recv()
            to_second(h, i)
    crossed = [across(0, 0), across(1, 0)]
    for o in (1, 3, 2):
        for h in range(2):
            for i in range(4):
                far[h][i][o].wait_recv()
            crossed.append(across(h, o))

    count = 256
    stores = []

    def project(k):
        for h in range(2):
            block = bases[h, :, cores[k]].reshape(patches // 4, 2, 16, fold + thin)
            wide = block[:, :, :, :fold].astype(jnp.float32)
            wide = jnp.concatenate([wide[:, :, :8], wide[:, :, 8:]], axis=3)
            basis[h, :plain] = wide.reshape(plain, width).astype(jnp.bfloat16)
            rest = block[:, :, :, fold:].astype(jnp.float32)
            rest = [
                jnp.concatenate([rest[:, z, 4 * j : 4 * j + 4] for z in range(2)], axis=1) for j in range(4)
            ]
            rest = jnp.concatenate(rest, axis=2)
            basis[h, plain:] = rest.reshape(columns - plain, width).astype(jnp.bfloat16)
        for i in range(pixels // count):
            at = pl.ds(count * i, count)
            coefficients = sum(
                lax.dot_general(
                    sky_ref[at, width * h : width * (h + 1)],
                    basis[h],
                    (((1,), (1,)), ((), ())),
                    preferred_element_type=jnp.float32,
                )
                for h in range(2)
            )
            amounts = two_pieces(spread[k, at] * coefficients)
            for h in range(2):
                taken = jnp.dot(amounts, basis[h], preferred_element_type=jnp.float32)
                part = slice(width * h, width * (h + 1))
                left = sky_ref[at, part].astype(jnp.float32) if k == 0 else clean_ref[at, part]
                clean_ref[at, part] = left - (taken[:count] + taken[count:])
            if k == 1:
                stores.append(pltpu.make_async_copy(clean_ref.at[at], clean_hbm.at[at], out_sem.at[i]))
                stores[i].start()

    project(0)
    for one in crossed:
        one.wait_recv()
    project(1)
    for one in started:
        one.wait_send()
    for store in stores:
        store.wait()


def cleaned(index, count, taper, sky, q0):
    capacity, patches = index.shape
    pixels, channels = sky.shape
    sems = lambda *shape: pltpu.SemaphoreType.DMA(shape)
    return pl.pallas_call(
        clean_kernel,
        out_shape=jax.ShapeDtypeStruct((pixels, channels), jnp.float32),
        in_specs=[pl.BlockSpec(memory_space=pl.ANY)] * 5,
        out_specs=pl.BlockSpec(memory_space=pl.ANY),
        scratch_shapes=[
            pltpu.VMEM((pixels, channels), jnp.float32),
            pltpu.VMEM(index.shape, index.dtype),
            pltpu.VMEM(count.shape, count.dtype),
            pltpu.VMEM(taper.shape, taper.dtype),
            pltpu.VMEM(sky.shape, sky.dtype),
            pltpu.VMEM(q0.shape, q0.dtype),
            pltpu.VMEM((2, 4, 2, 4, 2, 16, channels * 3 // 8), jnp.bfloat16),
            pltpu.VMEM((2, patches // 2 * MODES, channels // 2), jnp.bfloat16),
            pltpu.VMEM((pixels, 2 * patches), jnp.bfloat16),
            pltpu.VMEM((2, pixels, patches // 2 * MODES), jnp.float32),
            pltpu.VMEM((patches, capacity, 128), jnp.int32),
            pltpu.VMEM((patches, capacity, channels), jnp.bfloat16),
            pltpu.VMEM((patches, capacity, channels), jnp.bfloat16),
            pltpu.VMEM((channels, channels), jnp.float32),
            pltpu.VMEM((2 * channels, channels), jnp.bfloat16),
            pltpu.VMEM((2, SHARERS, 2, 2 * MODES, channels // 4), jnp.float32),
            pltpu.VMEM((2, SHARERS, 2, 4 * MODES, channels // 8), jnp.bfloat16),
            sems(5),
            sems(2),
            sems(patches), sems(patches),
            sems(2, 8), sems(2, 8), sems(2, 8), sems(2, 8),
            sems(16), sems(16), sems(32), sems(32), sems(8), sems(8),
        ],
        compiler_params=pltpu.CompilerParams(
            collective_id=0, has_side_effects=True, vmem_limit_bytes=VMEM_MIB * MIB
        ),
    )(index, count, taper, sky, q0)


def copy_kernel(from_ref, to_ref, held, in_sem, out_sem):
    chunks = in_sem.shape[0]
    count = held.shape[0] // chunks
    parts = [pl.ds(count * i, count) for i in range(chunks)]
    loads = [pltpu.make_async_copy(from_ref.at[p], held.at[p], in_sem.at[i]) for i, p in enumerate(parts)]
    stores = [pltpu.make_async_copy(held.at[p], to_ref.at[p], out_sem.at[i]) for i, p in enumerate(parts)]
    for load in loads:
        load.start()
    for load, store in zip(loads, stores):
        load.wait()
        store.start()
    for store in stores:
        store.wait()


def copied(array):
    anywhere = pl.BlockSpec(memory_space=pl.ANY)
    return pl.pallas_call(
        copy_kernel,
        out_shape=jax.ShapeDtypeStruct(array.shape, array.dtype),
        in_specs=[anywhere],
        out_specs=anywhere,
        scratch_shapes=[
            pltpu.VMEM(array.shape, array.dtype),
            pltpu.SemaphoreType.DMA((8,)),
            pltpu.SemaphoreType.DMA((8,)),
        ],
        compiler_params=pltpu.CompilerParams(vmem_limit_bytes=VMEM_MIB * MIB),
    )(array)


def local(sky, send_index, send_count, taper, start_basis):
    patches, capacity = send_index.shape[2:]
    index = send_index.reshape(patches, capacity).T
    count = send_count.reshape(1, patches)
    return copied(cleaned(index, count, taper.reshape(patches, capacity).T, sky, start_basis.T))


def solution(mesh):
    fine = Mesh(mesh.devices.reshape(4, SHARERS, 2, 2, 4), ("y", "zp", "zl", "core", "x"))
    patch = ("y", "zp", "zl", "core")
    rows = P((*patch, "x"), None)
    placed = (rows, P(patch, "x", None, None), P(patch, "x", None), P(patch, "x", None, None), P())
    return jax.shard_map(local, mesh=fine, in_specs=placed, out_specs=rows, check_vma=False)
```

```python
import jax
import jax.numpy as jnp
from jax import lax
from jax.experimental import pallas as pl
from jax.experimental.pallas import tpu as pltpu
from jax.sharding import Mesh, PartitionSpec as P

ITERS = 6
MODES = 12
SHARERS = 4
CELL = ("y", "core", "x", "zl")
MESH = pl.DeviceIdType.MESH
MIB = 1 << 20
VMEM_MIB = 56
WINDOW = 2


def two_pieces(value):
    high = value.astype(jnp.bfloat16).astype(jnp.float32)
    return jnp.concatenate([high, value - high], axis=0).astype(jnp.bfloat16)


def orthonormal_rows(v):
    row = lax.broadcasted_iota(jnp.int32, (MODES, 1), 0)
    norms = jnp.zeros((MODES, 1), jnp.float32)
    for k in range(MODES):
        lead = v[k : k + 1]
        dots = jnp.sum(v * lead, axis=1, keepdims=True)
        norms = jnp.where(row == k, dots, norms)
        if k + 1 < MODES:
            v = v - jnp.where(row > k, dots / (dots[k : k + 1] + 1e-12), 0.0) * lead
    return v * (1.0 / jnp.sqrt(norms + 1e-12))


def orthonormal_pairs(v):
    row = lax.broadcasted_iota(jnp.int32, (MODES, 1), 0)
    norms = jnp.ones((MODES, 1), jnp.float32)
    for k in range(0, MODES, 2):
        a, b = v[k : k + 1], v[k + 1 : k + 2]
        on_a = jnp.sum(v * a, axis=1, keepdims=True)
        on_b = jnp.sum(v * b, axis=1, keepdims=True)
        aa, ab, bb = on_a[k : k + 1], on_a[k + 1 : k + 2], on_b[k + 1 : k + 2]
        by_a = on_a / (aa + 1e-12)
        c = by_a[k + 1 : k + 2]
        rest = jnp.maximum(bb - 2.0 * c * ab + c * c * aa, 1e-6 * bb)
        on_rest = on_b - c * on_a - by_a * ab + by_a * (c * aa)
        by_rest = jnp.where(row > k + 1, on_rest / (rest + 1e-12), 0.0)
        v = v - (jnp.where(row > k, by_a, 0.0) - by_rest * c) * a - by_rest * b
        norms = jnp.where(row == k, aa, jnp.where(row == k + 1, rest, norms))
    return v * (1.0 / jnp.sqrt(norms + 1e-12))


def stacked(z, folds):
    width = z.shape[1] // folds
    return jnp.concatenate([z[:, width * f : width * (f + 1)] for f in range(folds)], axis=0)


def unstacked(z, folds):
    return jnp.concatenate([z[MODES * f : MODES * (f + 1)] for f in range(folds)], axis=1)


def each(first, last, step):
    def body(i, carry):
        step(i)
        return carry

    lax.fori_loop(first, last, body, 0)


def ring(at, o):
    return lax.rem(at + o, 4)


def send_to(src, dst, send_sem, recv_sem, to):
    return pltpu.make_async_remote_copy(
        src_ref=src, dst_ref=dst, send_sem=send_sem, recv_sem=recv_sem, device_id=to, device_id_type=MESH
    )


def clean_kernel(
    index_hbm, count_hbm, taper_hbm, sky_hbm, q0_hbm, clean_hbm,
    clean_ref, index_ref, count_ref, taper_ref, sky_ref, q_ref, bases, basis, weight_ref, spread, column, rows, inbox, total, gram_ref, exact, short,
    in_sem, out_sem, row_send, row_recv, x_send, x_recv, s_send, s_recv,
    a_send, a_recv, b_send, b_recv, c_send, c_recv,
):
    me = lax.axis_index("zp")
    y, c, x, zl = (lax.axis_index(name) for name in CELL)
    capacity, patches = index_ref.shape
    pixels, channels = sky_ref.shape

    sources = (index_hbm, count_hbm, sky_hbm, taper_hbm, q0_hbm)
    places = (index_ref, count_ref, sky_ref, taper_ref, q_ref)
    loads = [pltpu.make_async_copy(f, t, in_sem.at[i]) for i, (f, t) in enumerate(zip(sources, places))]
    for load in loads:
        load.start()

    def peer(r):
        o = lax.rem(r * 37, patches)
        to = {
            "x": ring(x, lax.rem(o, 4)),
            "y": ring(y, lax.rem(lax.div(o, 4), 4)),
            "core": lax.rem(c + lax.rem(lax.div(o, 16), 2), 2),
            "zl": lax.rem(zl + lax.div(o, 32), 2),
        }
        return to, ((to["y"] * 2 + to["core"]) * 4 + to["x"]) * 2 + to["zl"]

    def row_copy(r):
        return send_to(rows.at[r], inbox.at[r], row_send.at[r], row_recv.at[r], peer(r)[0])

    barrier = pltpu.get_barrier_semaphore()
    at_x, at_y = [ring(x, o) for o in range(4)], [ring(y, o) for o in range(4)]
    for o in range(1, patches):
        to = {
            "x": at_x[o % 4],
            "y": at_y[o // 4 % 4],
            "core": 1 - c if o // 16 % 2 else c,
            "zl": 1 - zl if o // 32 else zl,
        }
        pl.semaphore_signal(barrier, inc=1, device_id=to, device_id_type=MESH)
    for o in range(1, SHARERS):
        pl.semaphore_signal(barrier, inc=1, device_id={"zp": ring(me, o)}, device_id_type=MESH)

    loads[0].wait()
    loads[1].wait()
    slot = lax.broadcasted_iota(jnp.int32, (capacity, patches), 0)
    index = jnp.where(slot < count_ref[...], index_ref[...], -1)
    for d in range(patches):
        column[d] = jnp.broadcast_to(index[:, d : d + 1], (capacity, 128))
    lane = lax.broadcasted_iota(jnp.int32, (4 * capacity, 128), 1)
    loads[2].wait()

    def pick(block):
        near = jnp.concatenate([column[peer(4 * block + j)[1]] for j in range(4)], axis=0)
        hot = [jnp.where(near == lane + 128 * t, 1.0, 0.0) for t in range(pixels // 128)]
        hot = jnp.concatenate(hot, axis=1).astype(jnp.bfloat16)
        found = jnp.dot(hot, sky_ref[...], preferred_element_type=jnp.float32).astype(jnp.bfloat16)
        for j in range(4):
            rows[4 * block + j] = found[capacity * j : capacity * (j + 1)]

    pick(0)
    pl.semaphore_wait(barrier, patches - 1 + SHARERS - 1)
    for j in range(1, 4):
        row_copy(j).start()

    def send(block):
        pick(block)
        for j in range(4):
            row_copy(4 * block + j).start()

    each(1, WINDOW, send)
    inbox[0] = rows[0]

    loads[3].wait()
    loads[4].wait()
    for part in range(pixels // 128):
        pixel = 128 * part + lax.broadcasted_iota(jnp.int32, (128, patches), 0)
        weights = jnp.zeros((128, patches), jnp.float32)
        for j in range(capacity):
            weights = weights + jnp.where(index[j : j + 1, :] == pixel, taper_ref[j : j + 1, :], 0.0)
        whole = jnp.sum(weights, axis=1, keepdims=True)
        weights = weights / jnp.where(whole > 0, whole, 1.0)
        high = weights.astype(jnp.bfloat16).astype(jnp.float32)
        weight_ref[128 * part : 128 * (part + 1), :] = jnp.concatenate([high, weights - high], axis=1).astype(
            jnp.bfloat16
        )

    plain = patches // 4 * 16
    columns = patches // 2 * MODES
    patch = lax.rem(lax.broadcasted_iota(jnp.int32, (2 * patches, columns), 0), patches)
    col = lax.broadcasted_iota(jnp.int32, (2 * patches, columns), 1)
    wide_owner = 16 * lax.div(col, 64) + lax.div(lax.rem(col, 64), 8)
    thin_owner = 16 * lax.div(col - plain, 32) + lax.div(lax.rem(col - plain, 32), 4)
    owner = jnp.where(col < plain, wide_owner, thin_owner)
    cores = (c, 1 - c)
    for k in range(2):
        hot = jnp.where(patch == owner + 8 * cores[k], 1.0, 0.0).astype(jnp.bfloat16)
        spread[k] = jnp.dot(weight_ref[...], hot, preferred_element_type=jnp.float32)

    total[...] = jnp.zeros_like(total)
    tile = 256

    def add(group):
        each(jnp.maximum(8 * group, 1), 8 * group + 8, lambda r: row_copy(r).wait_recv())
        block = inbox[pl.ds(8 * group, 8)].reshape(8 * capacity, channels)
        for t in range(channels // tile):
            part = slice(tile * t, tile * (t + 1))
            total[part, :] += lax.dot_general(
                block[:, part], block, (((0,), (0,)), ((), ())), preferred_element_type=jnp.float32
            )

    def settle(t, value):
        high = value.astype(jnp.bfloat16)
        gram_ref[tile * t : tile * (t + 1), :] = high
        gram_ref[channels + tile * t : channels + tile * (t + 1), :] = (value - high.astype(jnp.float32)).astype(
            jnp.bfloat16
        )

    last = patches // 8 - 1

    def send_on(block):
        first = 4 * (block - WINDOW)
        each(jnp.maximum(first, 1), first + 4, lambda r: row_copy(r).wait_send())
        send(block)

    def send_and_add(group):
        send_on(2 * group + WINDOW)
        send_on(2 * group + WINDOW + 1)
        add(group)

    paired = (patches // 4 - WINDOW) // 2
    each(0, paired, send_and_add)
    each(paired, last, add)
    for t in range(channels // tile):
        settle(t, total[tile * t : tile * (t + 1), :])
    each(8 * last, patches, lambda r: row_copy(r).wait_recv())

    def late_rows():
        return inbox[8 * last :].reshape(8 * capacity, channels)

    def settle_late():
        block = late_rows()
        for t in range(channels // tile):
            part = slice(tile * t, tile * (t + 1))
            settle(
                t,
                total[part, :]
                + lax.dot_general(
                    block[:, part], block, (((0,), (0,)), ((), ())), preferred_element_type=jnp.float32
                ),
            )

    width = channels // 2

    def sweep(step, wide, late=False, final=False):
        folds, box, sems = (2, exact, (x_send, x_recv)) if wide else (4, short, (s_send, s_recv))
        at = step % 2 if isinstance(step, int) else lax.rem(step, 2)
        box = box.at[at]
        pieces = two_pieces(q_ref[...])
        lhs = jnp.concatenate([pieces, pieces], axis=1)
        if late:
            y = lax.dot_general(
                pieces, late_rows(), (((1,), (1,)), ((), ())), preferred_element_type=jnp.float32
            )
            y = two_pieces(y[:MODES] + y[MODES:])
        copies = []
        for h in range(2):
            z = jnp.dot(lhs, gram_ref[:, width * h : width * (h + 1)], preferred_element_type=jnp.float32)
            if late:
                z = z + jnp.dot(
                    y, late_rows()[:, width * h : width * (h + 1)], preferred_element_type=jnp.float32
                )
            box[me, h] = stacked(z[:MODES] + z[MODES:], folds).astype(box.dtype)
            for o in (2, 1, 3):
                mine = box.at[me, h]
                copies.append(
                    send_to(mine, mine, sems[0].at[at, 4 * h + o], sems[1].at[at, 4 * h + o], {"zp": ring(me, o)})
                )
                copies[-1].start()
        if late:
            settle_late()
            each(patches - 4 * WINDOW, patches, lambda r: row_copy(r).wait_send())
        for one in copies:
            one.wait_recv()
        halves = []
        for h in range(2):
            whole = box[0, h].astype(jnp.float32)
            for k in range(1, SHARERS):
                whole = whole + box[k, h].astype(jnp.float32)
            halves.append(unstacked(whole, folds))
        whole = jnp.concatenate(halves, axis=1)
        q_ref[...] = orthonormal_rows(whole) if final else orthonormal_pairs(whole)
        for one in copies:
            one.wait_send()

    sweep(0, True, late=True)
    each(1, ITERS - 1, lambda step: sweep(step, False))
    sweep(ITERS - 1, True, final=True)

    fold, thin = width // 2, width // 4
    first, second = ("x", "y"), ("y", "x")
    place = {"x": x, "y": y}

    def pair_at(h, i, o):
        back = {first[h]: ring(place[first[h]], 4 - i), second[h]: ring(place[second[h]], 4 - o)}
        return bases.at[h, back["y"], c, back["x"]]

    def block_of(q):
        wide, rest = q[:8], q[8:]
        return jnp.concatenate(
            [
                jnp.concatenate([wide[:, :fold], wide[:, fold:]], axis=0),
                jnp.concatenate([rest[:, thin * j : thin * (j + 1)] for j in range(4)], axis=0),
            ],
            axis=1,
        )

    def line_at(h, o):
        if h == 0:
            return bases.at[0, ring(y, 4 - o), c]
        return bases.at[1, :, c, ring(x, 4 - o)]

    started = []

    def go(src, sems, at, to):
        one = send_to(src, src, sems[0].at[at], sems[1].at[at], to)
        one.start()
        started.append(one)
        return one

    near = [[[None] * 2 for _ in range(4)] for _ in range(2)]
    far = [[[None] * 4 for _ in range(4)] for _ in range(2)]

    def to_first(h):
        mine = bases.at[h, y, c, x, zl]
        for o in (2, 1, 3, 0):
            for j in range(2):
                if o + j:
                    to = {first[h]: ring(place[first[h]], o), "zl": 1 - zl if j else zl}
                    near[h][o][j] = go(mine, (a_send, a_recv), 8 * h + 2 * o + j, to)

    def to_second(h, i):
        for o in (2, 1, 3):
            to = {second[h]: ring(place[second[h]], o)}
            far[h][i][o] = go(pair_at(h, i, 0), (b_send, b_recv), 16 * h + 4 * i + o, to)

    def across(h, o):
        return go(line_at(h, o), (c_send, c_recv), 4 * h + o, {"core": 1 - c})

    for h in range(2):
        bases[h, y, c, x, zl] = block_of(q_ref[:, width * h : width * (h + 1)]).astype(jnp.bfloat16)
        to_first(h)
    for i in (0, 1, 3, 2):
        for h in range(2):
            for j in range(2):
                if i + j:
                    near[h][i][j].wait_recv()
            to_second(h, i)
    crossed = [across(0, 0), across(1, 0)]
    for o in (1, 3, 2):
        for h in range(2):
            for i in range(4):
                far[h][i][o].wait_recv()
            crossed.append(across(h, o))

    count = 256
    stores = []

    def project(k):
        for h in range(2):
            block = bases[h, :, cores[k]].reshape(patches // 4, 2, 16, fold + thin)
            wide = block[:, :, :, :fold].astype(jnp.float32)
            wide = jnp.concatenate([wide[:, :, :8], wide[:, :, 8:]], axis=3)
            basis[h, :plain] = wide.reshape(plain, width).astype(jnp.bfloat16)
            rest = block[:, :, :, fold:].astype(jnp.float32)
            rest = [
                jnp.concatenate([rest[:, z, 4 * j : 4 * j + 4] for z in range(2)], axis=1) for j in range(4)
            ]
            rest = jnp.concatenate(rest, axis=2)
            basis[h, plain:] = rest.reshape(columns - plain, width).astype(jnp.bfloat16)
        for i in range(pixels // count):
            at = pl.ds(count * i, count)
            coefficients = sum(
                lax.dot_general(
                    sky_ref[at, width * h : width * (h + 1)],
                    basis[h],
                    (((1,), (1,)), ((), ())),
                    preferred_element_type=jnp.float32,
                )
                for h in range(2)
            )
            amounts = two_pieces(spread[k, at] * coefficients)
            for h in range(2):
                taken = jnp.dot(amounts, basis[h], preferred_element_type=jnp.float32)
                part = slice(width * h, width * (h + 1))
                left = sky_ref[at, part].astype(jnp.float32) if k == 0 else clean_ref[at, part]
                clean_ref[at, part] = left - (taken[:count] + taken[count:])
            if k == 1:
                stores.append(pltpu.make_async_copy(clean_ref.at[at], clean_hbm.at[at], out_sem.at[i]))
                stores[i].start()

    project(0)
    for one in crossed:
        one.wait_recv()
    project(1)
    for one in started:
        one.wait_send()
    for store in stores:
        store.wait()


def cleaned(index, count, taper, sky, q0):
    capacity, patches = index.shape
    pixels, channels = sky.shape
    sems = lambda *shape: pltpu.SemaphoreType.DMA(shape)
    return pl.pallas_call(
        clean_kernel,
        out_shape=jax.ShapeDtypeStruct((pixels, channels), jnp.float32),
        in_specs=[pl.BlockSpec(memory_space=pl.ANY)] * 5,
        out_specs=pl.BlockSpec(memory_space=pl.ANY),
        scratch_shapes=[
            pltpu.VMEM((pixels, channels), jnp.float32),
            pltpu.VMEM(index.shape, index.dtype),
            pltpu.VMEM(count.shape, count.dtype),
            pltpu.VMEM(taper.shape, taper.dtype),
            pltpu.VMEM(sky.shape, sky.dtype),
            pltpu.VMEM(q0.shape, q0.dtype),
            pltpu.VMEM((2, 4, 2, 4, 2, 16, channels * 3 // 8), jnp.bfloat16),
            pltpu.VMEM((2, patches // 2 * MODES, channels // 2), jnp.bfloat16),
            pltpu.VMEM((pixels, 2 * patches), jnp.bfloat16),
            pltpu.VMEM((2, pixels, patches // 2 * MODES), jnp.float32),
            pltpu.VMEM((patches, capacity, 128), jnp.int32),
            pltpu.VMEM((patches, capacity, channels), jnp.bfloat16),
            pltpu.VMEM((patches, capacity, channels), jnp.bfloat16),
            pltpu.VMEM((channels, channels), jnp.float32),
            pltpu.VMEM((2 * channels, channels), jnp.bfloat16),
            pltpu.VMEM((2, SHARERS, 2, 2 * MODES, channels // 4), jnp.float32),
            pltpu.VMEM((2, SHARERS, 2, 4 * MODES, channels // 8), jnp.bfloat16),
            sems(5),
            sems(2),
            sems(patches), sems(patches),
            sems(2, 8), sems(2, 8), sems(2, 8), sems(2, 8),
            sems(16), sems(16), sems(32), sems(32), sems(8), sems(8),
        ],
        compiler_params=pltpu.CompilerParams(
            collective_id=0, has_side_effects=True, vmem_limit_bytes=VMEM_MIB * MIB
        ),
    )(index, count, taper, sky, q0)


def copy_kernel(from_ref, to_ref, held, in_sem, out_sem):
    chunks = in_sem.shape[0]
    count = held.shape[0] // chunks
    parts = [pl.ds(count * i, count) for i in range(chunks)]
    loads = [pltpu.make_async_copy(from_ref.at[p], held.at[p], in_sem.at[i]) for i, p in enumerate(parts)]
    stores = [pltpu.make_async_copy(held.at[p], to_ref.at[p], out_sem.at[i]) for i, p in enumerate(parts)]
    for load in loads:
        load.start()
    for load, store in zip(loads, stores):
        load.wait()
        store.start()
    for store in stores:
        store.wait()


def copied(array):
    anywhere = pl.BlockSpec(memory_space=pl.ANY)
    return pl.pallas_call(
        copy_kernel,
        out_shape=jax.ShapeDtypeStruct(array.shape, array.dtype),
        in_specs=[anywhere],
        out_specs=anywhere,
        scratch_shapes=[
            pltpu.VMEM(array.shape, array.dtype),
            pltpu.SemaphoreType.DMA((8,)),
            pltpu.SemaphoreType.DMA((8,)),
        ],
        compiler_params=pltpu.CompilerParams(vmem_limit_bytes=VMEM_MIB * MIB),
    )(array)


def local(sky, send_index, send_count, taper, start_basis):
    patches, capacity = send_index.shape[2:]
    index = send_index.reshape(patches, capacity).T
    count = send_count.reshape(1, patches)
    return copied(cleaned(index, count, taper.reshape(patches, capacity).T, sky, start_basis.T))


def solution(mesh):
    fine = Mesh(mesh.devices.reshape(4, SHARERS, 2, 2, 4), ("y", "zp", "zl", "core", "x"))
    patch = ("y", "zp", "zl", "core")
    rows = P((*patch, "x"), None)
    placed = (rows, P(patch, "x", None, None), P(patch, "x", None), P(patch, "x", None, None), P())
    return jax.shard_map(local, mesh=fine, in_specs=placed, out_specs=rows, check_vma=False)
```

```python
import jax
import jax.numpy as jnp
from jax import lax
from jax.experimental import pallas as pl
from jax.experimental.pallas import tpu as pltpu
from jax.sharding import Mesh, PartitionSpec as P

ITERS = 6
MODES = 12
SHARERS = 4
CELL = ("y", "core", "x", "zl")
MESH = pl.DeviceIdType.MESH
MIB = 1 << 20
VMEM_MIB = 56
WINDOW = 4


def two_pieces(value):
    high = value.astype(jnp.bfloat16).astype(jnp.float32)
    return jnp.concatenate([high, value - high], axis=0).astype(jnp.bfloat16)


def orthonormal_rows(v):
    row = lax.broadcasted_iota(jnp.int32, (MODES, 1), 0)
    norms = jnp.ones((MODES, 1), jnp.float32)
    for k in range(0, MODES, 2):
        a, b = v[k : k + 1], v[k + 1 : k + 2]
        on_a = jnp.sum(v * a, axis=1, keepdims=True)
        on_b = jnp.sum(v * b, axis=1, keepdims=True)
        aa, ab, bb = on_a[k : k + 1], on_a[k + 1 : k + 2], on_b[k + 1 : k + 2]
        by_a = on_a / (aa + 1e-12)
        c = by_a[k + 1 : k + 2]
        rest = jnp.maximum(bb - 2.0 * c * ab + c * c * aa, 1e-6 * bb)
        on_rest = on_b - c * on_a - by_a * ab + by_a * (c * aa)
        by_rest = jnp.where(row > k + 1, on_rest / (rest + 1e-12), 0.0)
        v = v - (jnp.where(row > k, by_a, 0.0) - by_rest * c) * a - by_rest * b
        norms = jnp.where(row == k, aa, jnp.where(row == k + 1, rest, norms))
    return v * (1.0 / jnp.sqrt(norms + 1e-12))


def stacked(z, folds):
    width = z.shape[1] // folds
    return jnp.concatenate([z[:, width * f : width * (f + 1)] for f in range(folds)], axis=0)


def unstacked(z, folds):
    return jnp.concatenate([z[MODES * f : MODES * (f + 1)] for f in range(folds)], axis=1)


def each(first, last, step):
    def body(i, carry):
        step(i)
        return carry

    lax.fori_loop(first, last, body, 0)


def ring(at, o):
    return lax.rem(at + o, 4)


def send_to(src, dst, send_sem, recv_sem, to):
    return pltpu.make_async_remote_copy(
        src_ref=src, dst_ref=dst, send_sem=send_sem, recv_sem=recv_sem, device_id=to, device_id_type=MESH
    )


def clean_kernel(
    index_hbm, count_hbm, taper_hbm, sky_hbm, q0_hbm, clean_hbm,
    clean_ref, index_ref, count_ref, taper_ref, sky_ref, q_ref, bases, basis, weight_ref, spread, column, rows, inbox, total, gram_ref, exact, short,
    in_sem, out_sem, row_send, row_recv, x_send, x_recv, s_send, s_recv,
    a_send, a_recv, b_send, b_recv, c_send, c_recv,
):
    me = lax.axis_index("zp")
    y, c, x, zl = (lax.axis_index(name) for name in CELL)
    capacity, patches = index_ref.shape
    pixels, channels = sky_ref.shape

    sources = (index_hbm, count_hbm, sky_hbm, taper_hbm, q0_hbm)
    places = (index_ref, count_ref, sky_ref, taper_ref, q_ref)
    loads = [pltpu.make_async_copy(f, t, in_sem.at[i]) for i, (f, t) in enumerate(zip(sources, places))]
    for load in loads:
        load.start()

    def peer(r):
        o = lax.rem(r * 37, patches)
        to = {
            "x": ring(x, lax.rem(o, 4)),
            "y": ring(y, lax.rem(lax.div(o, 4), 4)),
            "core": lax.rem(c + lax.rem(lax.div(o, 16), 2), 2),
            "zl": lax.rem(zl + lax.div(o, 32), 2),
        }
        return to, ((to["y"] * 2 + to["core"]) * 4 + to["x"]) * 2 + to["zl"]

    def row_copy(r):
        return send_to(rows.at[r], inbox.at[r], row_send.at[r], row_recv.at[r], peer(r)[0])

    barrier = pltpu.get_barrier_semaphore()
    at_x, at_y = [ring(x, o) for o in range(4)], [ring(y, o) for o in range(4)]
    for o in range(1, patches):
        to = {
            "x": at_x[o % 4],
            "y": at_y[o // 4 % 4],
            "core": 1 - c if o // 16 % 2 else c,
            "zl": 1 - zl if o // 32 else zl,
        }
        pl.semaphore_signal(barrier, inc=1, device_id=to, device_id_type=MESH)
    for o in range(1, SHARERS):
        pl.semaphore_signal(barrier, inc=1, device_id={"zp": ring(me, o)}, device_id_type=MESH)

    loads[0].wait()
    loads[1].wait()
    slot = lax.broadcasted_iota(jnp.int32, (capacity, patches), 0)
    index = jnp.where(slot < count_ref[...], index_ref[...], -1)
    for d in range(patches):
        column[d] = jnp.broadcast_to(index[:, d : d + 1], (capacity, 128))
    lane = lax.broadcasted_iota(jnp.int32, (4 * capacity, 128), 1)
    loads[2].wait()

    def pick(block):
        near = jnp.concatenate([column[peer(4 * block + j)[1]] for j in range(4)], axis=0)
        hot = [jnp.where(near == lane + 128 * t, 1.0, 0.0) for t in range(pixels // 128)]
        hot = jnp.concatenate(hot, axis=1).astype(jnp.bfloat16)
        found = jnp.dot(hot, sky_ref[...], preferred_element_type=jnp.float32).astype(jnp.bfloat16)
        for j in range(4):
            rows[4 * block + j] = found[capacity * j : capacity * (j + 1)]

    pick(0)
    pl.semaphore_wait(barrier, patches - 1 + SHARERS - 1)
    for j in range(1, 4):
        row_copy(j).start()

    def send(block):
        pick(block)
        for j in range(4):
            row_copy(4 * block + j).start()

    each(1, WINDOW, send)
    inbox[0] = rows[0]

    loads[3].wait()
    loads[4].wait()
    for part in range(pixels // 128):
        pixel = 128 * part + lax.broadcasted_iota(jnp.int32, (128, patches), 0)
        weights = jnp.zeros((128, patches), jnp.float32)
        for j in range(capacity):
            weights = weights + jnp.where(index[j : j + 1, :] == pixel, taper_ref[j : j + 1, :], 0.0)
        whole = jnp.sum(weights, axis=1, keepdims=True)
        weights = weights / jnp.where(whole > 0, whole, 1.0)
        high = weights.astype(jnp.bfloat16).astype(jnp.float32)
        weight_ref[128 * part : 128 * (part + 1), :] = jnp.concatenate([high, weights - high], axis=1).astype(
            jnp.bfloat16
        )

    plain = patches // 4 * 16
    columns = patches // 2 * MODES
    patch = lax.rem(lax.broadcasted_iota(jnp.int32, (2 * patches, columns), 0), patches)
    col = lax.broadcasted_iota(jnp.int32, (2 * patches, columns), 1)
    wide_owner = 16 * lax.div(col, 64) + lax.div(lax.rem(col, 64), 8)
    thin_owner = 16 * lax.div(col - plain, 32) + lax.div(lax.rem(col - plain, 32), 4)
    owner = jnp.where(col < plain, wide_owner, thin_owner)
    cores = (c, 1 - c)
    for k in range(2):
        hot = jnp.where(patch == owner + 8 * cores[k], 1.0, 0.0).astype(jnp.bfloat16)
        spread[k] = jnp.dot(weight_ref[...], hot, preferred_element_type=jnp.float32)

    total[...] = jnp.zeros_like(total)
    tile = 256

    def add(group):
        each(jnp.maximum(8 * group, 1), 8 * group + 8, lambda r: row_copy(r).wait_recv())
        block = inbox[pl.ds(8 * group, 8)].reshape(8 * capacity, channels)
        for t in range(channels // tile):
            part = slice(tile * t, tile * (t + 1))
            total[part, :] += lax.dot_general(
                block[:, part], block, (((0,), (0,)), ((), ())), preferred_element_type=jnp.float32
            )

    def settle(t, value):
        high = value.astype(jnp.bfloat16)
        gram_ref[tile * t : tile * (t + 1), :] = high
        gram_ref[channels + tile * t : channels + tile * (t + 1), :] = (value - high.astype(jnp.float32)).astype(
            jnp.bfloat16
        )

    last = patches // 8 - 2

    def send_on(block):
        first = 4 * (block - WINDOW)
        each(jnp.maximum(first, 1), first + 4, lambda r: row_copy(r).wait_send())
        send(block)

    def send_and_add(group):
        send_on(2 * group + WINDOW)
        send_on(2 * group + WINDOW + 1)
        add(group)

    paired = (patches // 4 - WINDOW) // 2
    each(0, paired, send_and_add)
    each(paired, last, add)
    for t in range(channels // tile):
        settle(t, total[tile * t : tile * (t + 1), :])
    each(8 * last, patches, lambda r: row_copy(r).wait_recv())

    def late_rows():
        return inbox[8 * last :].reshape((patches - 8 * last) * capacity, channels)

    def settle_late():
        block = late_rows()
        for t in range(channels // tile):
            part = slice(tile * t, tile * (t + 1))
            settle(
                t,
                total[part, :]
                + lax.dot_general(
                    block[:, part], block, (((0,), (0,)), ((), ())), preferred_element_type=jnp.float32
                ),
            )

    width = channels // 2

    def sweep(step, wide, late=False):
        folds, box, sems = (2, exact, (x_send, x_recv)) if wide else (4, short, (s_send, s_recv))
        at = step % 2 if isinstance(step, int) else lax.rem(step, 2)
        box = box.at[at]
        pieces = two_pieces(q_ref[...])
        lhs = jnp.concatenate([pieces, pieces], axis=1)
        if late:
            y = lax.dot_general(
                pieces, late_rows(), (((1,), (1,)), ((), ())), preferred_element_type=jnp.float32
            )
            y = two_pieces(y[:MODES] + y[MODES:])
        copies = []
        for h in range(2):
            z = jnp.dot(lhs, gram_ref[:, width * h : width * (h + 1)], preferred_element_type=jnp.float32)
            if late:
                z = z + jnp.dot(
                    y, late_rows()[:, width * h : width * (h + 1)], preferred_element_type=jnp.float32
                )
            box[me, h] = stacked(z[:MODES] + z[MODES:], folds).astype(box.dtype)
            for o in (2, 1, 3):
                mine = box.at[me, h]
                copies.append(
                    send_to(mine, mine, sems[0].at[at, 4 * h + o], sems[1].at[at, 4 * h + o], {"zp": ring(me, o)})
                )
                copies[-1].start()
        if late:
            settle_late()
            each(patches - 4 * WINDOW, patches, lambda r: row_copy(r).wait_send())
        halves = []
        for h in range(2):
            for one in copies[3 * h : 3 * h + 3]:
                one.wait_recv()
            whole = box[0, h].astype(jnp.float32)
            for k in range(1, SHARERS):
                whole = whole + box[k, h].astype(jnp.float32)
            halves.append(unstacked(whole, folds))
        whole = jnp.concatenate(halves, axis=1)
        q_ref[...] = orthonormal_rows(whole)
        for one in copies:
            one.wait_send()

    sweep(0, True, late=True)
    each(1, ITERS - 1, lambda step: sweep(step, False))
    sweep(ITERS - 1, True)

    fold, thin = width // 2, width // 4
    first, second = ("x", "y"), ("y", "x")
    place = {"x": x, "y": y}

    def pair_at(h, i, o):
        back = {first[h]: ring(place[first[h]], 4 - i), second[h]: ring(place[second[h]], 4 - o)}
        return bases.at[h, back["y"], c, back["x"]]

    def block_of(q):
        wide, rest = q[:8], q[8:]
        return jnp.concatenate(
            [
                jnp.concatenate([wide[:, :fold], wide[:, fold:]], axis=0),
                jnp.concatenate([rest[:, thin * j : thin * (j + 1)] for j in range(4)], axis=0),
            ],
            axis=1,
        )

    def line_at(h, o):
        if h == 0:
            return bases.at[0, ring(y, 4 - o), c]
        return bases.at[1, :, c, ring(x, 4 - o)]

    started = []

    def go(src, sems, at, to):
        one = send_to(src, src, sems[0].at[at], sems[1].at[at], to)
        one.start()
        started.append(one)
        return one

    near = [[[None] * 2 for _ in range(4)] for _ in range(2)]
    far = [[[None] * 4 for _ in range(4)] for _ in range(2)]

    def to_first(h):
        mine = bases.at[h, y, c, x, zl]
        for o in (2, 1, 3, 0):
            for j in range(2):
                if o + j:
                    to = {first[h]: ring(place[first[h]], o), "zl": 1 - zl if j else zl}
                    near[h][o][j] = go(mine, (a_send, a_recv), 8 * h + 2 * o + j, to)

    def to_second(h, i):
        for o in (2, 1, 3):
            to = {second[h]: ring(place[second[h]], o)}
            far[h][i][o] = go(pair_at(h, i, 0), (b_send, b_recv), 16 * h + 4 * i + o, to)

    def across(h, o):
        return go(line_at(h, o), (c_send, c_recv), 4 * h + o, {"core": 1 - c})

    for h in range(2):
        bases[h, y, c, x, zl] = block_of(q_ref[:, width * h : width * (h + 1)]).astype(jnp.bfloat16)
        to_first(h)
    for i in (0, 1, 3, 2):
        for h in range(2):
            for j in range(2):
                if i + j:
                    near[h][i][j].wait_recv()
            to_second(h, i)
    crossed = [across(0, 0), across(1, 0)]
    for o in (1, 3, 2):
        for h in range(2):
            for i in range(4):
                far[h][i][o].wait_recv()
            crossed.append(across(h, o))

    stores = []

    def project(k):
        for h in range(2):
            block = bases[h, :, cores[k]].reshape(patches // 4, 2, 16, fold + thin)
            wide = block[:, :, :, :fold].astype(jnp.float32)
            wide = jnp.concatenate([wide[:, :, :8], wide[:, :, 8:]], axis=3)
            basis[h, :plain] = wide.reshape(plain, width).astype(jnp.bfloat16)
            rest = block[:, :, :, fold:].astype(jnp.float32)
            rest = [
                jnp.concatenate([rest[:, z, 4 * j : 4 * j + 4] for z in range(2)], axis=1) for j in range(4)
            ]
            rest = jnp.concatenate(rest, axis=2)
            basis[h, plain:] = rest.reshape(columns - plain, width).astype(jnp.bfloat16)
        coefficients = sum(
            lax.dot_general(
                sky_ref[:, width * h : width * (h + 1)],
                basis[h],
                (((1,), (1,)), ((), ())),
                preferred_element_type=jnp.float32,
            )
            for h in range(2)
        )
        amounts = two_pieces(spread[k] * coefficients)
        for h in range(2):
            taken = jnp.dot(amounts, basis[h], preferred_element_type=jnp.float32)
            part = slice(width * h, width * (h + 1))
            left = sky_ref[:, part].astype(jnp.float32) if k == 0 else clean_ref[:, part]
            clean_ref[:, part] = left - (taken[:pixels] + taken[pixels:])
            if k == 1:
                stores.append(pltpu.make_async_copy(clean_ref.at[:, part], clean_hbm.at[:, part], out_sem.at[h]))
                stores[h].start()

    project(0)
    for one in crossed:
        one.wait_recv()
    project(1)
    for one in started:
        one.wait_send()
    for store in stores:
        store.wait()


def cleaned(index, count, taper, sky, q0):
    capacity, patches = index.shape
    pixels, channels = sky.shape
    sems = lambda *shape: pltpu.SemaphoreType.DMA(shape)
    return pl.pallas_call(
        clean_kernel,
        out_shape=jax.ShapeDtypeStruct((pixels, channels), jnp.float32),
        in_specs=[pl.BlockSpec(memory_space=pl.ANY)] * 5,
        out_specs=pl.BlockSpec(memory_space=pl.ANY),
        scratch_shapes=[
            pltpu.VMEM((pixels, channels), jnp.float32),
            pltpu.VMEM(index.shape, index.dtype),
            pltpu.VMEM(count.shape, count.dtype),
            pltpu.VMEM(taper.shape, taper.dtype),
            pltpu.VMEM(sky.shape, sky.dtype),
            pltpu.VMEM(q0.shape, q0.dtype),
            pltpu.VMEM((2, 4, 2, 4, 2, 16, channels * 3 // 8), jnp.bfloat16),
            pltpu.VMEM((2, patches // 2 * MODES, channels // 2), jnp.bfloat16),
            pltpu.VMEM((pixels, 2 * patches), jnp.bfloat16),
            pltpu.VMEM((2, pixels, patches // 2 * MODES), jnp.float32),
            pltpu.VMEM((patches, capacity, 128), jnp.int32),
            pltpu.VMEM((patches, capacity, channels), jnp.bfloat16),
            pltpu.VMEM((patches, capacity, channels), jnp.bfloat16),
            pltpu.VMEM((channels, channels), jnp.float32),
            pltpu.VMEM((2 * channels, channels), jnp.bfloat16),
            pltpu.VMEM((2, SHARERS, 2, 2 * MODES, channels // 4), jnp.float32),
            pltpu.VMEM((2, SHARERS, 2, 4 * MODES, channels // 8), jnp.bfloat16),
            sems(5),
            sems(2),
            sems(patches), sems(patches),
            sems(2, 8), sems(2, 8), sems(2, 8), sems(2, 8),
            sems(16), sems(16), sems(32), sems(32), sems(8), sems(8),
        ],
        compiler_params=pltpu.CompilerParams(
            collective_id=0, has_side_effects=True, vmem_limit_bytes=VMEM_MIB * MIB
        ),
    )(index, count, taper, sky, q0)


def copy_kernel(from_ref, to_ref, held, in_sem, out_sem):
    chunks = in_sem.shape[0]
    count = held.shape[0] // chunks
    parts = [pl.ds(count * i, count) for i in range(chunks)]
    loads = [pltpu.make_async_copy(from_ref.at[p], held.at[p], in_sem.at[i]) for i, p in enumerate(parts)]
    stores = [pltpu.make_async_copy(held.at[p], to_ref.at[p], out_sem.at[i]) for i, p in enumerate(parts)]
    for load in loads:
        load.start()
    for load, store in zip(loads, stores):
        load.wait()
        store.start()
    for store in stores:
        store.wait()


def copied(array):
    anywhere = pl.BlockSpec(memory_space=pl.ANY)
    return pl.pallas_call(
        copy_kernel,
        out_shape=jax.ShapeDtypeStruct(array.shape, array.dtype),
        in_specs=[anywhere],
        out_specs=anywhere,
        scratch_shapes=[
            pltpu.VMEM(array.shape, array.dtype),
            pltpu.SemaphoreType.DMA((8,)),
            pltpu.SemaphoreType.DMA((8,)),
        ],
        compiler_params=pltpu.CompilerParams(vmem_limit_bytes=VMEM_MIB * MIB),
    )(array)


def local(sky, send_index, send_count, taper, start_basis):
    patches, capacity = send_index.shape[2:]
    index = send_index.reshape(patches, capacity).T
    count = send_count.reshape(1, patches)
    return copied(cleaned(index, count, taper.reshape(patches, capacity).T, sky, start_basis.T))


def solution(mesh):
    fine = Mesh(mesh.devices.reshape(4, SHARERS, 2, 2, 4), ("y", "zp", "zl", "core", "x"))
    patch = ("y", "zp", "zl", "core")
    rows = P((*patch, "x"), None)
    placed = (rows, P(patch, "x", None, None), P(patch, "x", None), P(patch, "x", None, None), P())
    return jax.shard_map(local, mesh=fine, in_specs=placed, out_specs=rows, check_vma=False)
```

```python
import jax
import jax.numpy as jnp
from jax import lax
from jax.experimental import pallas as pl
from jax.experimental.pallas import tpu as pltpu
from jax.sharding import Mesh, PartitionSpec as P

ITERS = 6
MODES = 12
SHARERS = 4
CELL = ("y", "core", "x", "zl")
MESH = pl.DeviceIdType.MESH
MIB = 1 << 20
VMEM_MIB = 56
WINDOW = 4


def two_pieces(value):
    high = value.astype(jnp.bfloat16).astype(jnp.float32)
    return jnp.concatenate([high, value - high], axis=0).astype(jnp.bfloat16)


def orthonormal_rows(v):
    row = lax.broadcasted_iota(jnp.int32, (MODES, 1), 0)
    norms = jnp.zeros((MODES, 1), jnp.float32)
    for k in range(MODES):
        lead = v[k : k + 1]
        dots = jnp.sum(v * lead, axis=1, keepdims=True)
        norms = jnp.where(row == k, dots, norms)
        if k + 1 < MODES:
            v = v - jnp.where(row > k, dots / (dots[k : k + 1] + 1e-12), 0.0) * lead
    return v * (1.0 / jnp.sqrt(norms + 1e-12))


def orthonormal_pairs(v):
    row = lax.broadcasted_iota(jnp.int32, (MODES, 1), 0)
    norms = jnp.ones((MODES, 1), jnp.float32)
    for k in range(0, MODES, 2):
        a, b = v[k : k + 1], v[k + 1 : k + 2]
        on_a = jnp.sum(v * a, axis=1, keepdims=True)
        on_b = jnp.sum(v * b, axis=1, keepdims=True)
        aa, ab, bb = on_a[k : k + 1], on_a[k + 1 : k + 2], on_b[k + 1 : k + 2]
        by_a = on_a / (aa + 1e-12)
        c = by_a[k + 1 : k + 2]
        rest = jnp.maximum(bb - 2.0 * c * ab + c * c * aa, 1e-6 * bb)
        on_rest = on_b - c * on_a - by_a * ab + by_a * (c * aa)
        by_rest = jnp.where(row > k + 1, on_rest / (rest + 1e-12), 0.0)
        v = v - (jnp.where(row > k, by_a, 0.0) - by_rest * c) * a - by_rest * b
        norms = jnp.where(row == k, aa, jnp.where(row == k + 1, rest, norms))
    return v * (1.0 / jnp.sqrt(norms + 1e-12))


def stacked(z, folds):
    width = z.shape[1] // folds
    return jnp.concatenate([z[:, width * f : width * (f + 1)] for f in range(folds)], axis=0)


def unstacked(z, folds):
    return jnp.concatenate([z[MODES * f : MODES * (f + 1)] for f in range(folds)], axis=1)


def each(first, last, step):
    def body(i, carry):
        step(i)
        return carry

    lax.fori_loop(first, last, body, 0)


def ring(at, o):
    return lax.rem(at + o, 4)


def send_to(src, dst, send_sem, recv_sem, to):
    return pltpu.make_async_remote_copy(
        src_ref=src, dst_ref=dst, send_sem=send_sem, recv_sem=recv_sem, device_id=to, device_id_type=MESH
    )


def clean_kernel(
    index_hbm, count_hbm, taper_hbm, sky_hbm, q0_hbm, clean_hbm,
    clean_ref, index_ref, count_ref, taper_ref, sky_ref, q_ref, bases, basis, weight_ref, spread, column, rows, inbox, total, gram_ref, exact, short,
    in_sem, out_sem, row_send, row_recv, x_send, x_recv, s_send, s_recv,
    a_send, a_recv, b_send, b_recv, c_send, c_recv,
):
    me = lax.axis_index("zp")
    y, c, x, zl = (lax.axis_index(name) for name in CELL)
    capacity, patches = index_ref.shape
    pixels, channels = sky_ref.shape

    sources = (index_hbm, count_hbm, sky_hbm, taper_hbm, q0_hbm)
    places = (index_ref, count_ref, sky_ref, taper_ref, q_ref)
    loads = [pltpu.make_async_copy(f, t, in_sem.at[i]) for i, (f, t) in enumerate(zip(sources, places))]
    for load in loads:
        load.start()

    def peer(r):
        o = lax.rem(r * 37, patches)
        to = {
            "x": ring(x, lax.rem(o, 4)),
            "y": ring(y, lax.rem(lax.div(o, 4), 4)),
            "core": lax.rem(c + lax.rem(lax.div(o, 16), 2), 2),
            "zl": lax.rem(zl + lax.div(o, 32), 2),
        }
        return to, ((to["y"] * 2 + to["core"]) * 4 + to["x"]) * 2 + to["zl"]

    def row_copy(r):
        return send_to(rows.at[r], inbox.at[r], row_send.at[r], row_recv.at[r], peer(r)[0])

    barrier = pltpu.get_barrier_semaphore()
    at_x, at_y = [ring(x, o) for o in range(4)], [ring(y, o) for o in range(4)]
    steps = (0, 1, 2, 1)
    greeted = [(-steps[o % 4] - steps[o // 4 % 4] - o // 32, o) for o in range(1, patches)]
    greeted += [(-2 * steps[o], -o) for o in range(1, SHARERS)]
    for _, o in sorted(greeted):
        if o < 0:
            to = {"zp": ring(me, -o)}
        else:
            to = {
                "x": at_x[o % 4],
                "y": at_y[o // 4 % 4],
                "core": 1 - c if o // 16 % 2 else c,
                "zl": 1 - zl if o // 32 else zl,
            }
        pl.semaphore_signal(barrier, inc=1, device_id=to, device_id_type=MESH)

    loads[0].wait()
    loads[1].wait()
    slot = lax.broadcasted_iota(jnp.int32, (capacity, patches), 0)
    index = jnp.where(slot < count_ref[...], index_ref[...], -1)
    for d in range(patches):
        column[d] = jnp.broadcast_to(index[:, d : d + 1], (capacity, 128))
    lane = lax.broadcasted_iota(jnp.int32, (4 * capacity, 128), 1)
    loads[2].wait()

    def pick(block):
        near = jnp.concatenate([column[peer(4 * block + j)[1]] for j in range(4)], axis=0)
        hot = [jnp.where(near == lane + 128 * t, 1.0, 0.0) for t in range(pixels // 128)]
        hot = jnp.concatenate(hot, axis=1).astype(jnp.bfloat16)
        found = jnp.dot(hot, sky_ref[...], preferred_element_type=jnp.float32).astype(jnp.bfloat16)
        for j in range(4):
            rows[4 * block + j] = found[capacity * j : capacity * (j + 1)]

    pick(0)
    pl.semaphore_wait(barrier, patches - 1 + SHARERS - 1)
    for j in range(1, 4):
        row_copy(j).start()

    def send(block):
        pick(block)
        for j in range(4):
            row_copy(4 * block + j).start()

    each(1, WINDOW, send)
    inbox[0] = rows[0]

    loads[3].wait()
    loads[4].wait()
    for part in range(pixels // 128):
        pixel = 128 * part + lax.broadcasted_iota(jnp.int32, (128, patches), 0)
        weights = jnp.zeros((128, patches), jnp.float32)
        for j in range(capacity):
            weights = weights + jnp.where(index[j : j + 1, :] == pixel, taper_ref[j : j + 1, :], 0.0)
        whole = jnp.sum(weights, axis=1, keepdims=True)
        weights = weights / jnp.where(whole > 0, whole, 1.0)
        high = weights.astype(jnp.bfloat16).astype(jnp.float32)
        weight_ref[128 * part : 128 * (part + 1), :] = jnp.concatenate([high, weights - high], axis=1).astype(
            jnp.bfloat16
        )

    plain = patches // 4 * 16
    columns = patches // 2 * MODES
    patch = lax.rem(lax.broadcasted_iota(jnp.int32, (2 * patches, columns), 0), patches)
    col = lax.broadcasted_iota(jnp.int32, (2 * patches, columns), 1)
    wide_owner = 16 * lax.div(col, 64) + lax.div(lax.rem(col, 64), 8)
    thin_owner = 16 * lax.div(col - plain, 32) + lax.div(lax.rem(col - plain, 32), 4)
    owner = jnp.where(col < plain, wide_owner, thin_owner)
    cores = (c, 1 - c)
    for k in range(2):
        hot = jnp.where(patch == owner + 8 * cores[k], 1.0, 0.0).astype(jnp.bfloat16)
        spread[k] = jnp.dot(weight_ref[...], hot, preferred_element_type=jnp.float32)

    total[...] = jnp.zeros_like(total)
    tile = 256

    def add(group):
        each(jnp.maximum(8 * group, 1), 8 * group + 8, lambda r: row_copy(r).wait_recv())
        block = inbox[pl.ds(8 * group, 8)].reshape(8 * capacity, channels)
        for t in range(channels // tile):
            part = slice(tile * t, tile * (t + 1))
            total[part, :] += lax.dot_general(
                block[:, part], block, (((0,), (0,)), ((), ())), preferred_element_type=jnp.float32
            )

    def settle(t, value):
        high = value.astype(jnp.bfloat16)
        gram_ref[tile * t : tile * (t + 1), :] = high
        gram_ref[channels + tile * t : channels + tile * (t + 1), :] = (value - high.astype(jnp.float32)).astype(
            jnp.bfloat16
        )

    last = patches // 8 - 2

    def send_on(block):
        first = 4 * (block - WINDOW)
        each(jnp.maximum(first, 1), first + 4, lambda r: row_copy(r).wait_send())
        send(block)

    def send_and_add(group):
        send_on(2 * group + WINDOW)
        send_on(2 * group + WINDOW + 1)
        add(group)

    paired = (patches // 4 - WINDOW) // 2
    each(0, paired, send_and_add)
    each(paired, last, add)
    for t in range(channels // tile):
        settle(t, total[tile * t : tile * (t + 1), :])
    each(8 * last, patches, lambda r: row_copy(r).wait_recv())

    def late_rows():
        return inbox[8 * last :].reshape((patches - 8 * last) * capacity, channels)

    def settle_late():
        block = late_rows()
        for t in range(channels // tile):
            part = slice(tile * t, tile * (t + 1))
            settle(
                t,
                total[part, :]
                + lax.dot_general(
                    block[:, part], block, (((0,), (0,)), ((), ())), preferred_element_type=jnp.float32
                ),
            )

    width = channels // 2

    def sweep(step, wide, late=False, final=False):
        folds, box, sems = (2, exact, (x_send, x_recv)) if wide else (4, short, (s_send, s_recv))
        at = step % 2 if isinstance(step, int) else lax.rem(step, 2)
        box = box.at[at]
        pieces = two_pieces(q_ref[...])
        lhs = jnp.concatenate([pieces, pieces], axis=1)
        if late:
            y = lax.dot_general(
                pieces, late_rows(), (((1,), (1,)), ((), ())), preferred_element_type=jnp.float32
            )
            y = two_pieces(y[:MODES] + y[MODES:])
        copies = []
        for h in range(2):
            z = jnp.dot(lhs, gram_ref[:, width * h : width * (h + 1)], preferred_element_type=jnp.float32)
            if late:
                z = z + jnp.dot(
                    y, late_rows()[:, width * h : width * (h + 1)], preferred_element_type=jnp.float32
                )
            box[me, h] = stacked(z[:MODES] + z[MODES:], folds).astype(box.dtype)
            for o in (2, 1, 3):
                mine = box.at[me, h]
                copies.append(
                    send_to(mine, mine, sems[0].at[at, 4 * h + o], sems[1].at[at, 4 * h + o], {"zp": ring(me, o)})
                )
                copies[-1].start()
        if late:
            settle_late()
            each(patches - 4 * WINDOW, patches, lambda r: row_copy(r).wait_send())
        halves = []
        for h in range(2):
            for one in copies[3 * h : 3 * h + 3]:
                one.wait()
            whole = box[0, h].astype(jnp.float32)
            for k in range(1, SHARERS):
                whole = whole + box[k, h].astype(jnp.float32)
            halves.append(unstacked(whole, folds))
        whole = jnp.concatenate(halves, axis=1)
        q_ref[...] = orthonormal_rows(whole) if final else orthonormal_pairs(whole)

    sweep(0, True, late=True)
    each(1, ITERS - 1, lambda step: sweep(step, False))
    sweep(ITERS - 1, True, final=True)

    fold, thin = width // 2, width // 4
    first, second = ("x", "y"), ("y", "x")
    place = {"x": x, "y": y}

    def pair_at(h, i, o):
        back = {first[h]: ring(place[first[h]], 4 - i), second[h]: ring(place[second[h]], 4 - o)}
        return bases.at[h, back["y"], c, back["x"]]

    def block_of(q):
        wide, rest = q[:8], q[8:]
        return jnp.concatenate(
            [
                jnp.concatenate([wide[:, :fold], wide[:, fold:]], axis=0),
                jnp.concatenate([rest[:, thin * j : thin * (j + 1)] for j in range(4)], axis=0),
            ],
            axis=1,
        )

    def line_at(h, o):
        if h == 0:
            return bases.at[0, ring(y, 4 - o), c]
        return bases.at[1, :, c, ring(x, 4 - o)]

    started = []

    def go(src, sems, at, to):
        one = send_to(src, src, sems[0].at[at], sems[1].at[at], to)
        one.start()
        started.append(one)
        return one

    near = [[[None] * 2 for _ in range(4)] for _ in range(2)]
    far = [[[None] * 4 for _ in range(4)] for _ in range(2)]

    def to_first(h):
        mine = bases.at[h, y, c, x, zl]
        for o in (2, 1, 3, 0):
            for j in range(2):
                if o + j:
                    to = {first[h]: ring(place[first[h]], o), "zl": 1 - zl if j else zl}
                    near[h][o][j] = go(mine, (a_send, a_recv), 8 * h + 2 * o + j, to)

    def to_second(h, i):
        for o in (2, 1, 3):
            to = {second[h]: ring(place[second[h]], o)}
            far[h][i][o] = go(pair_at(h, i, 0), (b_send, b_recv), 16 * h + 4 * i + o, to)

    def across(h, o):
        return go(line_at(h, o), (c_send, c_recv), 4 * h + o, {"core": 1 - c})

    for h in range(2):
        bases[h, y, c, x, zl] = block_of(q_ref[:, width * h : width * (h + 1)]).astype(jnp.bfloat16)
        to_first(h)
    for i in (0, 1, 3, 2):
        for h in range(2):
            for j in range(2):
                if i + j:
                    near[h][i][j].wait_recv()
            to_second(h, i)
    crossed = [across(0, 0), across(1, 0)]
    for o in (1, 3, 2):
        for h in range(2):
            for i in range(4):
                far[h][i][o].wait_recv()
            crossed.append(across(h, o))

    stores = []

    def project(k):
        for h in range(2):
            block = bases[h, :, cores[k]].reshape(patches // 4, 2, 16, fold + thin)
            wide = block[:, :, :, :fold].astype(jnp.float32)
            wide = jnp.concatenate([wide[:, :, :8], wide[:, :, 8:]], axis=3)
            basis[h, :plain] = wide.reshape(plain, width).astype(jnp.bfloat16)
            rest = block[:, :, :, fold:].astype(jnp.float32)
            rest = [
                jnp.concatenate([rest[:, z, 4 * j : 4 * j + 4] for z in range(2)], axis=1) for j in range(4)
            ]
            rest = jnp.concatenate(rest, axis=2)
            basis[h, plain:] = rest.reshape(columns - plain, width).astype(jnp.bfloat16)
        coefficients = sum(
            lax.dot_general(
                sky_ref[:, width * h : width * (h + 1)],
                basis[h],
                (((1,), (1,)), ((), ())),
                preferred_element_type=jnp.float32,
            )
            for h in range(2)
        )
        amounts = two_pieces(spread[k] * coefficients)
        for h in range(2):
            taken = jnp.dot(amounts, basis[h], preferred_element_type=jnp.float32)
            part = slice(width * h, width * (h + 1))
            left = sky_ref[:, part].astype(jnp.float32) if k == 0 else clean_ref[:, part]
            clean_ref[:, part] = left - (taken[:pixels] + taken[pixels:])
            if k == 1:
                stores.append(pltpu.make_async_copy(clean_ref.at[:, part], clean_hbm.at[:, part], out_sem.at[h]))
                stores[h].start()

    project(0)
    for one in crossed:
        one.wait_recv()
    project(1)
    for one in started:
        one.wait_send()
    for store in stores:
        store.wait()


def cleaned(index, count, taper, sky, q0):
    capacity, patches = index.shape
    pixels, channels = sky.shape
    sems = lambda *shape: pltpu.SemaphoreType.DMA(shape)
    return pl.pallas_call(
        clean_kernel,
        out_shape=jax.ShapeDtypeStruct((pixels, channels), jnp.float32),
        in_specs=[pl.BlockSpec(memory_space=pl.ANY)] * 5,
        out_specs=pl.BlockSpec(memory_space=pl.ANY),
        scratch_shapes=[
            pltpu.VMEM((pixels, channels), jnp.float32),
            pltpu.VMEM(index.shape, index.dtype),
            pltpu.VMEM(count.shape, count.dtype),
            pltpu.VMEM(taper.shape, taper.dtype),
            pltpu.VMEM(sky.shape, sky.dtype),
            pltpu.VMEM(q0.shape, q0.dtype),
            pltpu.VMEM((2, 4, 2, 4, 2, 16, channels * 3 // 8), jnp.bfloat16),
            pltpu.VMEM((2, patches // 2 * MODES, channels // 2), jnp.bfloat16),
            pltpu.VMEM((pixels, 2 * patches), jnp.bfloat16),
            pltpu.VMEM((2, pixels, patches // 2 * MODES), jnp.float32),
            pltpu.VMEM((patches, capacity, 128), jnp.int32),
            pltpu.VMEM((patches, capacity, channels), jnp.bfloat16),
            pltpu.VMEM((patches, capacity, channels), jnp.bfloat16),
            pltpu.VMEM((channels, channels), jnp.float32),
            pltpu.VMEM((2 * channels, channels), jnp.bfloat16),
            pltpu.VMEM((2, SHARERS, 2, 2 * MODES, channels // 4), jnp.float32),
            pltpu.VMEM((2, SHARERS, 2, 4 * MODES, channels // 8), jnp.bfloat16),
            sems(5),
            sems(2),
            sems(patches), sems(patches),
            sems(2, 8), sems(2, 8), sems(2, 8), sems(2, 8),
            sems(16), sems(16), sems(32), sems(32), sems(8), sems(8),
        ],
        compiler_params=pltpu.CompilerParams(
            collective_id=0, has_side_effects=True, vmem_limit_bytes=VMEM_MIB * MIB
        ),
    )(index, count, taper, sky, q0)


def copy_kernel(from_ref, to_ref, held, in_sem, out_sem):
    chunks = in_sem.shape[0]
    count = held.shape[0] // chunks
    parts = [pl.ds(count * i, count) for i in range(chunks)]
    loads = [pltpu.make_async_copy(from_ref.at[p], held.at[p], in_sem.at[i]) for i, p in enumerate(parts)]
    stores = [pltpu.make_async_copy(held.at[p], to_ref.at[p], out_sem.at[i]) for i, p in enumerate(parts)]
    for load in loads:
        load.start()
    for load, store in zip(loads, stores):
        load.wait()
        store.start()
    for store in stores:
        store.wait()


def copied(array):
    anywhere = pl.BlockSpec(memory_space=pl.ANY)
    return pl.pallas_call(
        copy_kernel,
        out_shape=jax.ShapeDtypeStruct(array.shape, array.dtype),
        in_specs=[anywhere],
        out_specs=anywhere,
        scratch_shapes=[
            pltpu.VMEM(array.shape, array.dtype),
            pltpu.SemaphoreType.DMA((8,)),
            pltpu.SemaphoreType.DMA((8,)),
        ],
        compiler_params=pltpu.CompilerParams(vmem_limit_bytes=VMEM_MIB * MIB),
    )(array)


def local(sky, send_index, send_count, taper, start_basis):
    patches, capacity = send_index.shape[2:]
    index = send_index.reshape(patches, capacity).T
    count = send_count.reshape(1, patches)
    return copied(cleaned(index, count, taper.reshape(patches, capacity).T, sky, start_basis.T))


def solution(mesh):
    fine = Mesh(mesh.devices.reshape(4, SHARERS, 2, 2, 4), ("y", "zp", "zl", "core", "x"))
    patch = ("y", "zp", "zl", "core")
    rows = P((*patch, "x"), None)
    placed = (rows, P(patch, "x", None, None), P(patch, "x", None), P(patch, "x", None, None), P())
    return jax.shard_map(local, mesh=fine, in_specs=placed, out_specs=rows, check_vma=False)
```

```python
import jax
import jax.numpy as jnp
from jax import lax
from jax.experimental import pallas as pl
from jax.experimental.pallas import tpu as pltpu
from jax.sharding import Mesh, PartitionSpec as P

ITERS = 6
MODES = 12
SHARERS = 4
CELL = ("y", "core", "x", "zl")
MESH = pl.DeviceIdType.MESH
MIB = 1 << 20
VMEM_MIB = 56
WINDOW = 4


def two_pieces(value):
    high = value.astype(jnp.bfloat16).astype(jnp.float32)
    return jnp.concatenate([high, value - high], axis=0).astype(jnp.bfloat16)


def orthonormal_rows(v):
    row = lax.broadcasted_iota(jnp.int32, (MODES, 1), 0)
    norms = jnp.zeros((MODES, 1), jnp.float32)
    for k in range(MODES):
        lead = v[k : k + 1]
        dots = jnp.sum(v * lead, axis=1, keepdims=True)
        norms = jnp.where(row == k, dots, norms)
        if k + 1 < MODES:
            v = v - jnp.where(row > k, dots / (dots[k : k + 1] + 1e-12), 0.0) * lead
    return v * (1.0 / jnp.sqrt(norms + 1e-12))


def orthonormal_pairs(v):
    row = lax.broadcasted_iota(jnp.int32, (MODES, 1), 0)
    norms = jnp.ones((MODES, 1), jnp.float32)
    for k in range(0, MODES, 2):
        a, b = v[k : k + 1], v[k + 1 : k + 2]
        on_a = jnp.sum(v * a, axis=1, keepdims=True)
        on_b = jnp.sum(v * b, axis=1, keepdims=True)
        aa, ab, bb = on_a[k : k + 1], on_a[k + 1 : k + 2], on_b[k + 1 : k + 2]
        by_a = on_a / (aa + 1e-12)
        c = by_a[k + 1 : k + 2]
        rest = jnp.maximum(bb - 2.0 * c * ab + c * c * aa, 1e-6 * bb)
        on_rest = on_b - c * on_a - by_a * ab + by_a * (c * aa)
        by_rest = jnp.where(row > k + 1, on_rest / (rest + 1e-12), 0.0)
        v = v - (jnp.where(row > k, by_a, 0.0) - by_rest * c) * a - by_rest * b
        norms = jnp.where(row == k, aa, jnp.where(row == k + 1, rest, norms))
    return v * (1.0 / jnp.sqrt(norms + 1e-12))


def stacked(z, folds):
    width = z.shape[1] // folds
    return jnp.concatenate([z[:, width * f : width * (f + 1)] for f in range(folds)], axis=0)


def unstacked(z, folds):
    return jnp.concatenate([z[MODES * f : MODES * (f + 1)] for f in range(folds)], axis=1)


def each(first, last, step):
    def body(i, carry):
        step(i)
        return carry

    lax.fori_loop(first, last, body, 0)


def ring(at, o):
    return lax.rem(at + o, 4)


def send_to(src, dst, send_sem, recv_sem, to):
    return pltpu.make_async_remote_copy(
        src_ref=src, dst_ref=dst, send_sem=send_sem, recv_sem=recv_sem, device_id=to, device_id_type=MESH
    )


def clean_kernel(
    index_hbm, count_hbm, taper_hbm, sky_hbm, q0_hbm, clean_hbm,
    clean_ref, index_ref, count_ref, taper_ref, sky_ref, q_ref, bases, basis, weight_ref, spread, column, rows, inbox, total, gram_ref, exact, short,
    in_sem, out_sem, row_send, row_recv, x_send, x_recv, s_send, s_recv,
    a_send, a_recv, b_send, b_recv, c_send, c_recv,
):
    me = lax.axis_index("zp")
    y, c, x, zl = (lax.axis_index(name) for name in CELL)
    capacity, patches = index_ref.shape
    pixels, channels = sky_ref.shape

    sources = (index_hbm, count_hbm, sky_hbm, taper_hbm, q0_hbm)
    places = (index_ref, count_ref, sky_ref, taper_ref, q_ref)
    loads = [pltpu.make_async_copy(f, t, in_sem.at[i]) for i, (f, t) in enumerate(zip(sources, places))]
    for load in loads:
        load.start()

    def peer(r):
        o = lax.rem(r * 37, patches)
        to = {
            "x": ring(x, lax.rem(o, 4)),
            "y": ring(y, lax.rem(lax.div(o, 4), 4)),
            "core": lax.rem(c + lax.rem(lax.div(o, 16), 2), 2),
            "zl": lax.rem(zl + lax.div(o, 32), 2),
        }
        return to, ((to["y"] * 2 + to["core"]) * 4 + to["x"]) * 2 + to["zl"]

    def row_copy(r):
        return send_to(rows.at[r], inbox.at[r], row_send.at[r], row_recv.at[r], peer(r)[0])

    barrier = pltpu.get_barrier_semaphore()
    at_x, at_y = [ring(x, o) for o in range(4)], [ring(y, o) for o in range(4)]
    steps = (0, 1, 2, 1)
    greeted = [(-steps[o % 4] - steps[o // 4 % 4] - o // 32, o) for o in range(1, patches)]
    greeted += [(-2 * steps[o], -o) for o in range(1, SHARERS)]
    for _, o in sorted(greeted):
        if o < 0:
            to = {"zp": ring(me, -o)}
        else:
            to = {
                "x": at_x[o % 4],
                "y": at_y[o // 4 % 4],
                "core": 1 - c if o // 16 % 2 else c,
                "zl": 1 - zl if o // 32 else zl,
            }
        pl.semaphore_signal(barrier, inc=1, device_id=to, device_id_type=MESH)

    loads[0].wait()
    loads[1].wait()
    slot = lax.broadcasted_iota(jnp.int32, (capacity, patches), 0)
    index = jnp.where(slot < count_ref[...], index_ref[...], -1)
    for d in range(patches):
        column[d] = jnp.broadcast_to(index[:, d : d + 1], (capacity, 128))
    lane = lax.broadcasted_iota(jnp.int32, (4 * capacity, 128), 1)
    loads[2].wait()

    def pick(block):
        near = jnp.concatenate([column[peer(4 * block + j)[1]] for j in range(4)], axis=0)
        hot = [jnp.where(near == lane + 128 * t, 1.0, 0.0) for t in range(pixels // 128)]
        hot = jnp.concatenate(hot, axis=1).astype(jnp.bfloat16)
        found = jnp.dot(hot, sky_ref[...], preferred_element_type=jnp.float32).astype(jnp.bfloat16)
        for j in range(4):
            rows[4 * block + j] = found[capacity * j : capacity * (j + 1)]

    pick(0)
    pl.semaphore_wait(barrier, patches - 1 + SHARERS - 1)
    for j in range(1, 4):
        row_copy(j).start()

    def send(block):
        pick(block)
        for j in range(4):
            row_copy(4 * block + j).start()

    each(1, WINDOW, send)
    inbox[0] = rows[0]

    loads[3].wait()
    loads[4].wait()
    for part in range(pixels // 128):
        pixel = 128 * part + lax.broadcasted_iota(jnp.int32, (128, patches), 0)
        weights = jnp.zeros((128, patches), jnp.float32)
        for j in range(capacity):
            weights = weights + jnp.where(index[j : j + 1, :] == pixel, taper_ref[j : j + 1, :], 0.0)
        whole = jnp.sum(weights, axis=1, keepdims=True)
        weights = weights / jnp.where(whole > 0, whole, 1.0)
        high = weights.astype(jnp.bfloat16).astype(jnp.float32)
        weight_ref[128 * part : 128 * (part + 1), :] = jnp.concatenate([high, weights - high], axis=1).astype(
            jnp.bfloat16
        )

    plain = patches // 4 * 16
    columns = patches // 2 * MODES
    patch = lax.rem(lax.broadcasted_iota(jnp.int32, (2 * patches, columns), 0), patches)
    col = lax.broadcasted_iota(jnp.int32, (2 * patches, columns), 1)
    wide_owner = 16 * lax.div(col, 64) + lax.div(lax.rem(col, 64), 8)
    thin_owner = 16 * lax.div(col - plain, 32) + lax.div(lax.rem(col - plain, 32), 4)
    owner = jnp.where(col < plain, wide_owner, thin_owner)
    cores = (c, 1 - c)
    for k in range(2):
        hot = jnp.where(patch == owner + 8 * cores[k], 1.0, 0.0).astype(jnp.bfloat16)
        spread[k] = jnp.dot(weight_ref[...], hot, preferred_element_type=jnp.float32)

    total[...] = jnp.zeros_like(total)
    tile = 256

    def add(group):
        each(jnp.maximum(8 * group, 1), 8 * group + 8, lambda r: row_copy(r).wait_recv())
        block = inbox[pl.ds(8 * group, 8)].reshape(8 * capacity, channels)
        for t in range(channels // tile):
            part = slice(tile * t, tile * (t + 1))
            total[part, :] += lax.dot_general(
                block[:, part], block, (((0,), (0,)), ((), ())), preferred_element_type=jnp.float32
            )

    def settle(t, value):
        high = value.astype(jnp.bfloat16)
        gram_ref[tile * t : tile * (t + 1), :] = high
        gram_ref[channels + tile * t : channels + tile * (t + 1), :] = (value - high.astype(jnp.float32)).astype(
            jnp.bfloat16
        )

    last = patches // 8 - 2

    def send_on(block):
        pick(block)
        for j in range(4):
            row_copy(4 * (block - WINDOW) + j).wait_send()
            row_copy(4 * block + j).start()

    def send_and_add(group):
        send_on(2 * group + WINDOW)
        send_on(2 * group + WINDOW + 1)
        add(group - 1)

    paired = (patches // 4 - WINDOW) // 2
    pick(WINDOW)
    for j in range(4):
        if j:
            row_copy(j).wait_send()
        row_copy(4 * WINDOW + j).start()
    send_on(WINDOW + 1)
    each(1, paired, send_and_add)
    each(paired - 1, last, add)
    for t in range(channels // tile):
        settle(t, total[tile * t : tile * (t + 1), :])
    each(8 * last, patches, lambda r: row_copy(r).wait_recv())

    def late_rows():
        return inbox[8 * last :].reshape((patches - 8 * last) * capacity, channels)

    def settle_late():
        block = late_rows()
        for t in range(channels // tile):
            part = slice(tile * t, tile * (t + 1))
            settle(
                t,
                total[part, :]
                + lax.dot_general(
                    block[:, part], block, (((0,), (0,)), ((), ())), preferred_element_type=jnp.float32
                ),
            )

    width = channels // 2

    def sweep(step, wide, late=False, final=False):
        folds, box, sems = (2, exact, (x_send, x_recv)) if wide else (4, short, (s_send, s_recv))
        at = step % 2 if isinstance(step, int) else lax.rem(step, 2)
        box = box.at[at]
        pieces = two_pieces(q_ref[...])
        lhs = jnp.concatenate([pieces, pieces], axis=1)
        if late:
            y = lax.dot_general(
                pieces, late_rows(), (((1,), (1,)), ((), ())), preferred_element_type=jnp.float32
            )
            y = two_pieces(y[:MODES] + y[MODES:])
        copies = []
        for h in range(2):
            z = jnp.dot(lhs, gram_ref[:, width * h : width * (h + 1)], preferred_element_type=jnp.float32)
            if late:
                z = z + jnp.dot(
                    y, late_rows()[:, width * h : width * (h + 1)], preferred_element_type=jnp.float32
                )
            box[me, h] = stacked(z[:MODES] + z[MODES:], folds).astype(box.dtype)
            for o in (2, 1, 3):
                mine = box.at[me, h]
                copies.append(
                    send_to(mine, mine, sems[0].at[at, 4 * h + o], sems[1].at[at, 4 * h + o], {"zp": ring(me, o)})
                )
                copies[-1].start()
        if late:
            settle_late()
            each(patches - 4 * WINDOW, patches, lambda r: row_copy(r).wait_send())
        halves = []
        for h in range(2):
            for one in copies[3 * h : 3 * h + 3]:
                one.wait()
            whole = box[0, h].astype(jnp.float32)
            for k in range(1, SHARERS):
                whole = whole + box[k, h].astype(jnp.float32)
            halves.append(unstacked(whole, folds))
        whole = jnp.concatenate(halves, axis=1)
        q_ref[...] = orthonormal_rows(whole) if final else orthonormal_pairs(whole)

    sweep(0, True, late=True)
    each(1, ITERS - 1, lambda step: sweep(step, False))
    sweep(ITERS - 1, True, final=True)

    fold, thin = width // 2, width // 4
    first, second = ("x", "y"), ("y", "x")
    place = {"x": x, "y": y}

    def pair_at(h, i, o):
        back = {first[h]: ring(place[first[h]], 4 - i), second[h]: ring(place[second[h]], 4 - o)}
        return bases.at[h, back["y"], c, back["x"]]

    def block_of(q):
        wide, rest = q[:8], q[8:]
        return jnp.concatenate(
            [
                jnp.concatenate([wide[:, :fold], wide[:, fold:]], axis=0),
                jnp.concatenate([rest[:, thin * j : thin * (j + 1)] for j in range(4)], axis=0),
            ],
            axis=1,
        )

    def line_at(h, o):
        if h == 0:
            return bases.at[0, ring(y, 4 - o), c]
        return bases.at[1, :, c, ring(x, 4 - o)]

    started = []

    def go(src, sems, at, to):
        one = send_to(src, src, sems[0].at[at], sems[1].at[at], to)
        one.start()
        started.append(one)
        return one

    near = [[[None] * 2 for _ in range(4)] for _ in range(2)]
    far = [[[None] * 4 for _ in range(4)] for _ in range(2)]

    def to_first(h):
        mine = bases.at[h, y, c, x, zl]
        for o in (0, 2, 1, 3):
            for j in range(2):
                if o + j:
                    to = {first[h]: ring(place[first[h]], o), "zl": 1 - zl if j else zl}
                    near[h][o][j] = go(mine, (a_send, a_recv), 8 * h + 2 * o + j, to)

    def to_second(h, i):
        for o in (2, 1, 3):
            to = {second[h]: ring(place[second[h]], o)}
            far[h][i][o] = go(pair_at(h, i, 0), (b_send, b_recv), 16 * h + 4 * i + o, to)

    def across(h, o):
        return go(line_at(h, o), (c_send, c_recv), 4 * h + o, {"core": 1 - c})

    for h in range(2):
        bases[h, y, c, x, zl] = block_of(q_ref[:, width * h : width * (h + 1)]).astype(jnp.bfloat16)
        to_first(h)
    for i in (0, 1, 3, 2):
        for h in range(2):
            for j in range(2):
                if i + j:
                    near[h][i][j].wait_recv()
            to_second(h, i)
    crossed = [across(0, 0), across(1, 0)]
    for o in (1, 3, 2):
        for h in range(2):
            for i in range(4):
                far[h][i][o].wait_recv()
            crossed.append(across(h, o))

    stores = []

    def project(k):
        for h in range(2):
            block = bases[h, :, cores[k]].reshape(patches // 4, 2, 16, fold + thin)
            wide = block[:, :, :, :fold].astype(jnp.float32)
            wide = jnp.concatenate([wide[:, :, :8], wide[:, :, 8:]], axis=3)
            basis[h, :plain] = wide.reshape(plain, width).astype(jnp.bfloat16)
            rest = block[:, :, :, fold:].astype(jnp.float32)
            rest = [
                jnp.concatenate([rest[:, z, 4 * j : 4 * j + 4] for z in range(2)], axis=1) for j in range(4)
            ]
            rest = jnp.concatenate(rest, axis=2)
            basis[h, plain:] = rest.reshape(columns - plain, width).astype(jnp.bfloat16)
        coefficients = sum(
            lax.dot_general(
                sky_ref[:, width * h : width * (h + 1)],
                basis[h],
                (((1,), (1,)), ((), ())),
                preferred_element_type=jnp.float32,
            )
            for h in range(2)
        )
        amounts = two_pieces(spread[k] * coefficients)
        for h in range(2):
            taken = jnp.dot(amounts, basis[h], preferred_element_type=jnp.float32)
            part = slice(width * h, width * (h + 1))
            left = sky_ref[:, part].astype(jnp.float32) if k == 0 else clean_ref[:, part]
            clean_ref[:, part] = left - (taken[:pixels] + taken[pixels:])
            if k == 1:
                stores.append(pltpu.make_async_copy(clean_ref.at[:, part], clean_hbm.at[:, part], out_sem.at[h]))
                stores[h].start()

    project(0)
    for one in crossed:
        one.wait_recv()
    project(1)
    for one in started:
        one.wait_send()
    for store in stores:
        store.wait()


def cleaned(index, count, taper, sky, q0):
    capacity, patches = index.shape
    pixels, channels = sky.shape
    sems = lambda *shape: pltpu.SemaphoreType.DMA(shape)
    return pl.pallas_call(
        clean_kernel,
        out_shape=jax.ShapeDtypeStruct((pixels, channels), jnp.float32),
        in_specs=[pl.BlockSpec(memory_space=pl.ANY)] * 5,
        out_specs=pl.BlockSpec(memory_space=pl.ANY),
        scratch_shapes=[
            pltpu.VMEM((pixels, channels), jnp.float32),
            pltpu.VMEM(index.shape, index.dtype),
            pltpu.VMEM(count.shape, count.dtype),
            pltpu.VMEM(taper.shape, taper.dtype),
            pltpu.VMEM(sky.shape, sky.dtype),
            pltpu.VMEM(q0.shape, q0.dtype),
            pltpu.VMEM((2, 4, 2, 4, 2, 16, channels * 3 // 8), jnp.bfloat16),
            pltpu.VMEM((2, patches // 2 * MODES, channels // 2), jnp.bfloat16),
            pltpu.VMEM((pixels, 2 * patches), jnp.bfloat16),
            pltpu.VMEM((2, pixels, patches // 2 * MODES), jnp.float32),
            pltpu.VMEM((patches, capacity, 128), jnp.int32),
            pltpu.VMEM((patches, capacity, channels), jnp.bfloat16),
            pltpu.VMEM((patches, capacity, channels), jnp.bfloat16),
            pltpu.VMEM((channels, channels), jnp.float32),
            pltpu.VMEM((2 * channels, channels), jnp.bfloat16),
            pltpu.VMEM((2, SHARERS, 2, 2 * MODES, channels // 4), jnp.float32),
            pltpu.VMEM((2, SHARERS, 2, 4 * MODES, channels // 8), jnp.bfloat16),
            sems(5),
            sems(2),
            sems(patches), sems(patches),
            sems(2, 8), sems(2, 8), sems(2, 8), sems(2, 8),
            sems(16), sems(16), sems(32), sems(32), sems(8), sems(8),
        ],
        compiler_params=pltpu.CompilerParams(
            collective_id=0, has_side_effects=True, vmem_limit_bytes=VMEM_MIB * MIB
        ),
    )(index, count, taper, sky, q0)


def copy_kernel(from_ref, to_ref, held, in_sem, out_sem):
    chunks = in_sem.shape[0]
    count = held.shape[0] // chunks
    parts = [pl.ds(count * i, count) for i in range(chunks)]
    loads = [pltpu.make_async_copy(from_ref.at[p], held.at[p], in_sem.at[i]) for i, p in enumerate(parts)]
    stores = [pltpu.make_async_copy(held.at[p], to_ref.at[p], out_sem.at[i]) for i, p in enumerate(parts)]
    for load in loads:
        load.start()
    for load, store in zip(loads, stores):
        load.wait()
        store.start()
    for store in stores:
        store.wait()


def copied(array):
    anywhere = pl.BlockSpec(memory_space=pl.ANY)
    return pl.pallas_call(
        copy_kernel,
        out_shape=jax.ShapeDtypeStruct(array.shape, array.dtype),
        in_specs=[anywhere],
        out_specs=anywhere,
        scratch_shapes=[
            pltpu.VMEM(array.shape, array.dtype),
            pltpu.SemaphoreType.DMA((8,)),
            pltpu.SemaphoreType.DMA((8,)),
        ],
        compiler_params=pltpu.CompilerParams(vmem_limit_bytes=VMEM_MIB * MIB),
    )(array)


def local(sky, send_index, send_count, taper, start_basis):
    patches, capacity = send_index.shape[2:]
    index = send_index.reshape(patches, capacity).T
    count = send_count.reshape(1, patches)
    return copied(cleaned(index, count, taper.reshape(patches, capacity).T, sky, start_basis.T))


def solution(mesh):
    fine = Mesh(mesh.devices.reshape(4, SHARERS, 2, 2, 4), ("y", "zp", "zl", "core", "x"))
    patch = ("y", "zp", "zl", "core")
    rows = P((*patch, "x"), None)
    placed = (rows, P(patch, "x", None, None), P(patch, "x", None), P(patch, "x", None, None), P())
    return jax.shard_map(local, mesh=fine, in_specs=placed, out_specs=rows, check_vma=False)
```

```python
import jax
import jax.numpy as jnp
from jax import lax
from jax.experimental import pallas as pl
from jax.experimental.pallas import tpu as pltpu
from jax.sharding import Mesh, PartitionSpec as P

ITERS = 6
MODES = 12
SHARERS = 4
CELL = ("y", "core", "x", "zl")
MESH = pl.DeviceIdType.MESH
MIB = 1 << 20
VMEM_MIB = 56
WINDOW = 6


def two_pieces(value):
    high = value.astype(jnp.bfloat16).astype(jnp.float32)
    return jnp.concatenate([high, value - high], axis=0).astype(jnp.bfloat16)


def orthonormal_rows(v):
    row = lax.broadcasted_iota(jnp.int32, (MODES, 1), 0)
    norms = jnp.zeros((MODES, 1), jnp.float32)
    for k in range(MODES):
        lead = v[k : k + 1]
        dots = jnp.sum(v * lead, axis=1, keepdims=True)
        norms = jnp.where(row == k, dots, norms)
        if k + 1 < MODES:
            v = v - jnp.where(row > k, dots / (dots[k : k + 1] + 1e-12), 0.0) * lead
    return v * (1.0 / jnp.sqrt(norms + 1e-12))


def orthonormal_pairs(v):
    row = lax.broadcasted_iota(jnp.int32, (MODES, 1), 0)
    norms = jnp.ones((MODES, 1), jnp.float32)
    for k in range(0, MODES, 2):
        a, b = v[k : k + 1], v[k + 1 : k + 2]
        on_a = jnp.sum(v * a, axis=1, keepdims=True)
        on_b = jnp.sum(v * b, axis=1, keepdims=True)
        aa, ab, bb = on_a[k : k + 1], on_a[k + 1 : k + 2], on_b[k + 1 : k + 2]
        by_a = on_a / (aa + 1e-12)
        c = by_a[k + 1 : k + 2]
        rest = jnp.maximum(bb - 2.0 * c * ab + c * c * aa, 1e-6 * bb)
        on_rest = on_b - c * on_a - by_a * ab + by_a * (c * aa)
        by_rest = jnp.where(row > k + 1, on_rest / (rest + 1e-12), 0.0)
        v = v - (jnp.where(row > k, by_a, 0.0) - by_rest * c) * a - by_rest * b
        norms = jnp.where(row == k, aa, jnp.where(row == k + 1, rest, norms))
    return v * (1.0 / jnp.sqrt(norms + 1e-12))


def stacked(z, folds):
    width = z.shape[1] // folds
    return jnp.concatenate([z[:, width * f : width * (f + 1)] for f in range(folds)], axis=0)


def unstacked(z, folds):
    return jnp.concatenate([z[MODES * f : MODES * (f + 1)] for f in range(folds)], axis=1)


def each(first, last, step):
    def body(i, carry):
        step(i)
        return carry

    lax.fori_loop(first, last, body, 0)


def ring(at, o):
    return lax.rem(at + o, 4)


def send_to(src, dst, send_sem, recv_sem, to):
    return pltpu.make_async_remote_copy(
        src_ref=src, dst_ref=dst, send_sem=send_sem, recv_sem=recv_sem, device_id=to, device_id_type=MESH
    )


def clean_kernel(
    index_hbm, count_hbm, taper_hbm, sky_hbm, q0_hbm, clean_hbm,
    clean_ref, index_ref, count_ref, taper_ref, sky_ref, q_ref, bases, basis, weight_ref, spread, column, rows, inbox, total, gram_ref, exact, short,
    in_sem, out_sem, row_send, row_recv, x_send, x_recv, s_send, s_recv,
    a_send, a_recv, b_send, b_recv, c_send, c_recv,
):
    me = lax.axis_index("zp")
    y, c, x, zl = (lax.axis_index(name) for name in CELL)
    capacity, patches = index_ref.shape
    pixels, channels = sky_ref.shape

    sources = (index_hbm, count_hbm, sky_hbm, taper_hbm, q0_hbm)
    places = (index_ref, count_ref, sky_ref, taper_ref, q_ref)
    loads = [pltpu.make_async_copy(f, t, in_sem.at[i]) for i, (f, t) in enumerate(zip(sources, places))]
    for load in loads:
        load.start()

    def peer(r):
        o = lax.rem(r * 37, patches)
        to = {
            "x": ring(x, lax.rem(o, 4)),
            "y": ring(y, lax.rem(lax.div(o, 4), 4)),
            "core": lax.rem(c + lax.rem(lax.div(o, 16), 2), 2),
            "zl": lax.rem(zl + lax.div(o, 32), 2),
        }
        return to, ((to["y"] * 2 + to["core"]) * 4 + to["x"]) * 2 + to["zl"]

    def row_copy(r):
        return send_to(rows.at[r], inbox.at[r], row_send.at[r], row_recv.at[r], peer(r)[0])

    barrier = pltpu.get_barrier_semaphore()
    at_x, at_y = [ring(x, o) for o in range(4)], [ring(y, o) for o in range(4)]
    steps = (0, 1, 2, 1)
    greeted = [(-steps[o % 4] - steps[o // 4 % 4] - o // 32, o) for o in range(1, patches)]
    greeted += [(-2 * steps[o], -o) for o in range(1, SHARERS)]
    for _, o in sorted(greeted):
        if o < 0:
            to = {"zp": ring(me, -o)}
        else:
            to = {
                "x": at_x[o % 4],
                "y": at_y[o // 4 % 4],
                "core": 1 - c if o // 16 % 2 else c,
                "zl": 1 - zl if o // 32 else zl,
            }
        pl.semaphore_signal(barrier, inc=1, device_id=to, device_id_type=MESH)

    loads[0].wait()
    loads[1].wait()
    slot = lax.broadcasted_iota(jnp.int32, (capacity, patches), 0)
    index = jnp.where(slot < count_ref[...], index_ref[...], -1)
    for d in range(patches):
        column[d] = jnp.broadcast_to(index[:, d : d + 1], (capacity, 128))
    lane = lax.broadcasted_iota(jnp.int32, (4 * capacity, 128), 1)
    loads[2].wait()

    def pick(block):
        near = jnp.concatenate([column[peer(4 * block + j)[1]] for j in range(4)], axis=0)
        hot = [jnp.where(near == lane + 128 * t, 1.0, 0.0) for t in range(pixels // 128)]
        hot = jnp.concatenate(hot, axis=1).astype(jnp.bfloat16)
        found = jnp.dot(hot, sky_ref[...], preferred_element_type=jnp.float32).astype(jnp.bfloat16)
        for j in range(4):
            rows[4 * block + j] = found[capacity * j : capacity * (j + 1)]

    pick(0)
    pl.semaphore_wait(barrier, patches - 1 + SHARERS - 1)
    for j in range(1, 4):
        row_copy(j).start()

    def send(block):
        pick(block)
        for j in range(4):
            row_copy(4 * block + j).start()

    each(1, WINDOW, send)
    inbox[0] = rows[0]

    loads[3].wait()
    loads[4].wait()
    for part in range(pixels // 128):
        pixel = 128 * part + lax.broadcasted_iota(jnp.int32, (128, patches), 0)
        weights = jnp.zeros((128, patches), jnp.float32)
        for j in range(capacity):
            weights = weights + jnp.where(index[j : j + 1, :] == pixel, taper_ref[j : j + 1, :], 0.0)
        whole = jnp.sum(weights, axis=1, keepdims=True)
        weights = weights / jnp.where(whole > 0, whole, 1.0)
        high = weights.astype(jnp.bfloat16).astype(jnp.float32)
        weight_ref[128 * part : 128 * (part + 1), :] = jnp.concatenate([high, weights - high], axis=1).astype(
            jnp.bfloat16
        )

    plain = patches // 4 * 16
    columns = patches // 2 * MODES
    patch = lax.rem(lax.broadcasted_iota(jnp.int32, (2 * patches, columns), 0), patches)
    col = lax.broadcasted_iota(jnp.int32, (2 * patches, columns), 1)
    wide_owner = 16 * lax.div(col, 64) + lax.div(lax.rem(col, 64), 8)
    thin_owner = 16 * lax.div(col - plain, 32) + lax.div(lax.rem(col - plain, 32), 4)
    owner = jnp.where(col < plain, wide_owner, thin_owner)
    cores = (c, 1 - c)
    for k in range(2):
        hot = jnp.where(patch == owner + 8 * cores[k], 1.0, 0.0).astype(jnp.bfloat16)
        spread[k] = jnp.dot(weight_ref[...], hot, preferred_element_type=jnp.float32)

    total[...] = jnp.zeros_like(total)
    tile = 256

    def add(group):
        each(jnp.maximum(8 * group, 1), 8 * group + 8, lambda r: row_copy(r).wait_recv())
        block = inbox[pl.ds(8 * group, 8)].reshape(8 * capacity, channels)
        for t in range(channels // tile):
            part = slice(tile * t, tile * (t + 1))
            total[part, :] += lax.dot_general(
                block[:, part], block, (((0,), (0,)), ((), ())), preferred_element_type=jnp.float32
            )

    def settle(t, value):
        high = value.astype(jnp.bfloat16)
        gram_ref[tile * t : tile * (t + 1), :] = high
        gram_ref[channels + tile * t : channels + tile * (t + 1), :] = (value - high.astype(jnp.float32)).astype(
            jnp.bfloat16
        )

    last = patches // 8 - 2

    def send_on(block):
        pick(block)
        for j in range(4):
            row_copy(4 * (block - WINDOW) + j).wait_send()
            row_copy(4 * block + j).start()

    def send_and_add(group):
        send_on(2 * group + WINDOW)
        send_on(2 * group + WINDOW + 1)
        add(group - 1)

    paired = (patches // 4 - WINDOW) // 2
    pick(WINDOW)
    for j in range(4):
        if j:
            row_copy(j).wait_send()
        row_copy(4 * WINDOW + j).start()
    send_on(WINDOW + 1)
    each(1, paired, send_and_add)
    each(paired - 1, last, add)
    for t in range(channels // tile):
        settle(t, total[tile * t : tile * (t + 1), :])
    each(8 * last, patches, lambda r: row_copy(r).wait_recv())

    def late_rows():
        return inbox[8 * last :].reshape((patches - 8 * last) * capacity, channels)

    def settle_late():
        block = late_rows()
        for t in range(channels // tile):
            part = slice(tile * t, tile * (t + 1))
            settle(
                t,
                total[part, :]
                + lax.dot_general(
                    block[:, part], block, (((0,), (0,)), ((), ())), preferred_element_type=jnp.float32
                ),
            )

    width = channels // 2

    def sweep(step, wide, late=False, final=False):
        folds, box, sems = (2, exact, (x_send, x_recv)) if wide else (4, short, (s_send, s_recv))
        at = step % 2 if isinstance(step, int) else lax.rem(step, 2)
        box = box.at[at]
        pieces = two_pieces(q_ref[...])
        lhs = jnp.concatenate([pieces, pieces], axis=1)
        if late:
            y = lax.dot_general(
                pieces, late_rows(), (((1,), (1,)), ((), ())), preferred_element_type=jnp.float32
            )
            y = two_pieces(y[:MODES] + y[MODES:])
        copies = []
        for h in range(2):
            z = jnp.dot(lhs, gram_ref[:, width * h : width * (h + 1)], preferred_element_type=jnp.float32)
            if late:
                z = z + jnp.dot(
                    y, late_rows()[:, width * h : width * (h + 1)], preferred_element_type=jnp.float32
                )
            box[me, h] = stacked(z[:MODES] + z[MODES:], folds).astype(box.dtype)
            for o in (2, 1, 3):
                mine = box.at[me, h]
                copies.append(
                    send_to(mine, mine, sems[0].at[at, 4 * h + o], sems[1].at[at, 4 * h + o], {"zp": ring(me, o)})
                )
                copies[-1].start()
        if late:
            settle_late()
            each(patches - 4 * WINDOW, patches, lambda r: row_copy(r).wait_send())
        halves = []
        for h in range(2):
            for one in copies[3 * h : 3 * h + 3]:
                one.wait()
            whole = box[0, h].astype(jnp.float32)
            for k in range(1, SHARERS):
                whole = whole + box[k, h].astype(jnp.float32)
            halves.append(unstacked(whole, folds))
        whole = jnp.concatenate(halves, axis=1)
        q_ref[...] = orthonormal_rows(whole) if final else orthonormal_pairs(whole)

    sweep(0, True, late=True)
    each(1, ITERS - 1, lambda step: sweep(step, False))
    sweep(ITERS - 1, True, final=True)

    fold, thin = width // 2, width // 4
    first, second = ("x", "y"), ("y", "x")
    place = {"x": x, "y": y}

    def pair_at(h, i, o):
        back = {first[h]: ring(place[first[h]], 4 - i), second[h]: ring(place[second[h]], 4 - o)}
        return bases.at[h, back["y"], c, back["x"]]

    def block_of(q):
        wide, rest = q[:8], q[8:]
        return jnp.concatenate(
            [
                jnp.concatenate([wide[:, :fold], wide[:, fold:]], axis=0),
                jnp.concatenate([rest[:, thin * j : thin * (j + 1)] for j in range(4)], axis=0),
            ],
            axis=1,
        )

    def line_at(h, o):
        if h == 0:
            return bases.at[0, ring(y, 4 - o), c]
        return bases.at[1, :, c, ring(x, 4 - o)]

    started = []

    def go(src, sems, at, to):
        one = send_to(src, src, sems[0].at[at], sems[1].at[at], to)
        one.start()
        started.append(one)
        return one

    near = [[[None] * 2 for _ in range(4)] for _ in range(2)]
    far = [[[None] * 4 for _ in range(4)] for _ in range(2)]

    def to_first(h):
        mine = bases.at[h, y, c, x, zl]
        for o in (0, 2, 1, 3):
            for j in range(2):
                if o + j:
                    to = {first[h]: ring(place[first[h]], o), "zl": 1 - zl if j else zl}
                    near[h][o][j] = go(mine, (a_send, a_recv), 8 * h + 2 * o + j, to)

    def to_second(h, i):
        for o in (2, 1, 3):
            to = {second[h]: ring(place[second[h]], o)}
            far[h][i][o] = go(pair_at(h, i, 0), (b_send, b_recv), 16 * h + 4 * i + o, to)

    def across(h, o):
        return go(line_at(h, o), (c_send, c_recv), 4 * h + o, {"core": 1 - c})

    for h in range(2):
        bases[h, y, c, x, zl] = block_of(q_ref[:, width * h : width * (h + 1)]).astype(jnp.bfloat16)
        to_first(h)
    for i in (0, 1, 3, 2):
        for h in range(2):
            for j in range(2):
                if i + j:
                    near[h][i][j].wait_recv()
            to_second(h, i)
    crossed = [across(0, 0), across(1, 0)]
    for o in (1, 3, 2):
        for h in range(2):
            for i in range(4):
                far[h][i][o].wait_recv()
            crossed.append(across(h, o))

    stores = []

    def project(k):
        for h in range(2):
            block = bases[h, :, cores[k]].reshape(patches // 4, 2, 16, fold + thin)
            wide = block[:, :, :, :fold].astype(jnp.float32)
            wide = jnp.concatenate([wide[:, :, :8], wide[:, :, 8:]], axis=3)
            basis[h, :plain] = wide.reshape(plain, width).astype(jnp.bfloat16)
            rest = block[:, :, :, fold:].astype(jnp.float32)
            rest = [
                jnp.concatenate([rest[:, z, 4 * j : 4 * j + 4] for z in range(2)], axis=1) for j in range(4)
            ]
            rest = jnp.concatenate(rest, axis=2)
            basis[h, plain:] = rest.reshape(columns - plain, width).astype(jnp.bfloat16)
        coefficients = sum(
            lax.dot_general(
                sky_ref[:, width * h : width * (h + 1)],
                basis[h],
                (((1,), (1,)), ((), ())),
                preferred_element_type=jnp.float32,
            )
            for h in range(2)
        )
        amounts = two_pieces(spread[k] * coefficients)
        for h in range(2):
            taken = jnp.dot(amounts, basis[h], preferred_element_type=jnp.float32)
            part = slice(width * h, width * (h + 1))
            left = sky_ref[:, part].astype(jnp.float32) if k == 0 else clean_ref[:, part]
            clean_ref[:, part] = left - (taken[:pixels] + taken[pixels:])
            if k == 1:
                stores.append(pltpu.make_async_copy(clean_ref.at[:, part], clean_hbm.at[:, part], out_sem.at[h]))
                stores[h].start()

    project(0)
    for one in crossed:
        one.wait_recv()
    project(1)
    for one in started:
        one.wait_send()
    for store in stores:
        store.wait()


def cleaned(index, count, taper, sky, q0):
    capacity, patches = index.shape
    pixels, channels = sky.shape
    sems = lambda *shape: pltpu.SemaphoreType.DMA(shape)
    return pl.pallas_call(
        clean_kernel,
        out_shape=jax.ShapeDtypeStruct((pixels, channels), jnp.float32),
        in_specs=[pl.BlockSpec(memory_space=pl.ANY)] * 5,
        out_specs=pl.BlockSpec(memory_space=pl.ANY),
        scratch_shapes=[
            pltpu.VMEM((pixels, channels), jnp.float32),
            pltpu.VMEM(index.shape, index.dtype),
            pltpu.VMEM(count.shape, count.dtype),
            pltpu.VMEM(taper.shape, taper.dtype),
            pltpu.VMEM(sky.shape, sky.dtype),
            pltpu.VMEM(q0.shape, q0.dtype),
            pltpu.VMEM((2, 4, 2, 4, 2, 16, channels * 3 // 8), jnp.bfloat16),
            pltpu.VMEM((2, patches // 2 * MODES, channels // 2), jnp.bfloat16),
            pltpu.VMEM((pixels, 2 * patches), jnp.bfloat16),
            pltpu.VMEM((2, pixels, patches // 2 * MODES), jnp.float32),
            pltpu.VMEM((patches, capacity, 128), jnp.int32),
            pltpu.VMEM((patches, capacity, channels), jnp.bfloat16),
            pltpu.VMEM((patches, capacity, channels), jnp.bfloat16),
            pltpu.VMEM((channels, channels), jnp.float32),
            pltpu.VMEM((2 * channels, channels), jnp.bfloat16),
            pltpu.VMEM((2, SHARERS, 2, 2 * MODES, channels // 4), jnp.float32),
            pltpu.VMEM((2, SHARERS, 2, 4 * MODES, channels // 8), jnp.bfloat16),
            sems(5),
            sems(2),
            sems(patches), sems(patches),
            sems(2, 8), sems(2, 8), sems(2, 8), sems(2, 8),
            sems(16), sems(16), sems(32), sems(32), sems(8), sems(8),
        ],
        compiler_params=pltpu.CompilerParams(
            collective_id=0, has_side_effects=True, vmem_limit_bytes=VMEM_MIB * MIB
        ),
    )(index, count, taper, sky, q0)


def copy_kernel(from_ref, to_ref, held, in_sem, out_sem):
    chunks = in_sem.shape[0]
    count = held.shape[0] // chunks
    parts = [pl.ds(count * i, count) for i in range(chunks)]
    loads = [pltpu.make_async_copy(from_ref.at[p], held.at[p], in_sem.at[i]) for i, p in enumerate(parts)]
    stores = [pltpu.make_async_copy(held.at[p], to_ref.at[p], out_sem.at[i]) for i, p in enumerate(parts)]
    for load in loads:
        load.start()
    for load, store in zip(loads, stores):
        load.wait()
        store.start()
    for store in stores:
        store.wait()


def copied(array):
    anywhere = pl.BlockSpec(memory_space=pl.ANY)
    return pl.pallas_call(
        copy_kernel,
        out_shape=jax.ShapeDtypeStruct(array.shape, array.dtype),
        in_specs=[anywhere],
        out_specs=anywhere,
        scratch_shapes=[
            pltpu.VMEM(array.shape, array.dtype),
            pltpu.SemaphoreType.DMA((8,)),
            pltpu.SemaphoreType.DMA((8,)),
        ],
        compiler_params=pltpu.CompilerParams(vmem_limit_bytes=VMEM_MIB * MIB),
    )(array)


def local(sky, send_index, send_count, taper, start_basis):
    patches, capacity = send_index.shape[2:]
    index = send_index.reshape(patches, capacity).T
    count = send_count.reshape(1, patches)
    return copied(cleaned(index, count, taper.reshape(patches, capacity).T, sky, start_basis.T))


def solution(mesh):
    fine = Mesh(mesh.devices.reshape(4, SHARERS, 2, 2, 4), ("y", "zp", "zl", "core", "x"))
    patch = ("y", "zp", "zl", "core")
    rows = P((*patch, "x"), None)
    placed = (rows, P(patch, "x", None, None), P(patch, "x", None), P(patch, "x", None, None), P())
    return jax.shard_map(local, mesh=fine, in_specs=placed, out_specs=rows, check_vma=False)
```

```python
import jax
import jax.numpy as jnp
from jax import lax
from jax.experimental import pallas as pl
from jax.experimental.pallas import tpu as pltpu
from jax.sharding import Mesh, PartitionSpec as P

ITERS = 6
MODES = 12
SHARERS = 4
CELL = ("y", "core", "x", "zl")
MESH = pl.DeviceIdType.MESH
MIB = 1 << 20
VMEM_MIB = 56
WINDOW = 4


def two_pieces(value):
    high = value.astype(jnp.bfloat16).astype(jnp.float32)
    return jnp.concatenate([high, value - high], axis=0).astype(jnp.bfloat16)


def orthonormal_rows(v):
    row = lax.broadcasted_iota(jnp.int32, (MODES, 1), 0)
    norms = jnp.zeros((MODES, 1), jnp.float32)
    for k in range(MODES):
        lead = v[k : k + 1]
        dots = jnp.sum(v * lead, axis=1, keepdims=True)
        norms = jnp.where(row == k, dots, norms)
        if k + 1 < MODES:
            v = v - jnp.where(row > k, dots / (dots[k : k + 1] + 1e-12), 0.0) * lead
    return v * (1.0 / jnp.sqrt(norms + 1e-12))


def orthonormal_pairs(v):
    row = lax.broadcasted_iota(jnp.int32, (MODES, 1), 0)
    norms = jnp.ones((MODES, 1), jnp.float32)
    for k in range(0, MODES, 2):
        a, b = v[k : k + 1], v[k + 1 : k + 2]
        on_a = jnp.sum(v * a, axis=1, keepdims=True)
        on_b = jnp.sum(v * b, axis=1, keepdims=True)
        aa, ab, bb = on_a[k : k + 1], on_a[k + 1 : k + 2], on_b[k + 1 : k + 2]
        by_a = on_a / (aa + 1e-12)
        c = by_a[k + 1 : k + 2]
        rest = jnp.maximum(bb - 2.0 * c * ab + c * c * aa, 1e-6 * bb)
        on_rest = on_b - c * on_a - by_a * ab + by_a * (c * aa)
        by_rest = jnp.where(row > k + 1, on_rest / (rest + 1e-12), 0.0)
        v = v - (jnp.where(row > k, by_a, 0.0) - by_rest * c) * a - by_rest * b
        norms = jnp.where(row == k, aa, jnp.where(row == k + 1, rest, norms))
    return v * (1.0 / jnp.sqrt(norms + 1e-12))


def stacked(z, folds):
    width = z.shape[1] // folds
    return jnp.concatenate([z[:, width * f : width * (f + 1)] for f in range(folds)], axis=0)


def unstacked(z, folds):
    return jnp.concatenate([z[MODES * f : MODES * (f + 1)] for f in range(folds)], axis=1)


def each(first, last, step):
    def body(i, carry):
        step(i)
        return carry

    lax.fori_loop(first, last, body, 0)


def ring(at, o):
    return lax.rem(at + o, 4)


def send_to(src, dst, send_sem, recv_sem, to):
    return pltpu.make_async_remote_copy(
        src_ref=src, dst_ref=dst, send_sem=send_sem, recv_sem=recv_sem, device_id=to, device_id_type=MESH
    )


def clean_kernel(
    index_hbm, count_hbm, taper_hbm, sky_hbm, q0_hbm, clean_hbm,
    clean_ref, index_ref, count_ref, taper_ref, sky_ref, q_ref, bases, basis, weight_ref, spread, column, rows, inbox, total, gram_ref, exact, short,
    in_sem, out_sem, row_send, row_recv, x_send, x_recv, s_send, s_recv,
    a_send, a_recv, b_send, b_recv, c_send, c_recv,
):
    me = lax.axis_index("zp")
    y, c, x, zl = (lax.axis_index(name) for name in CELL)
    capacity, patches = index_ref.shape
    pixels, channels = sky_ref.shape

    sources = (index_hbm, count_hbm, sky_hbm, taper_hbm, q0_hbm)
    places = (index_ref, count_ref, sky_ref, taper_ref, q_ref)
    loads = [pltpu.make_async_copy(f, t, in_sem.at[i]) for i, (f, t) in enumerate(zip(sources, places))]
    for load in loads:
        load.start()

    def peer(r):
        o = lax.rem(r * 37, patches)
        to = {
            "x": ring(x, lax.rem(o, 4)),
            "y": ring(y, lax.rem(lax.div(o, 4), 4)),
            "core": lax.rem(c + lax.rem(lax.div(o, 16), 2), 2),
            "zl": lax.rem(zl + lax.div(o, 32), 2),
        }
        return to, ((to["y"] * 2 + to["core"]) * 4 + to["x"]) * 2 + to["zl"]

    def row_copy(r):
        return send_to(rows.at[r], inbox.at[r], row_send.at[r], row_recv.at[r], peer(r)[0])

    barrier = pltpu.get_barrier_semaphore()
    at_x, at_y = [ring(x, o) for o in range(4)], [ring(y, o) for o in range(4)]
    steps = (0, 1, 2, 1)
    greeted = [(-steps[o % 4] - steps[o // 4 % 4] - o // 32, o) for o in range(1, patches)]
    greeted += [(-2 * steps[o], -o) for o in range(1, SHARERS)]
    for _, o in sorted(greeted):
        if o < 0:
            to = {"zp": ring(me, -o)}
        else:
            to = {
                "x": at_x[o % 4],
                "y": at_y[o // 4 % 4],
                "core": 1 - c if o // 16 % 2 else c,
                "zl": 1 - zl if o // 32 else zl,
            }
        pl.semaphore_signal(barrier, inc=1, device_id=to, device_id_type=MESH)

    loads[0].wait()
    loads[1].wait()
    slot = lax.broadcasted_iota(jnp.int32, (capacity, patches), 0)
    index = jnp.where(slot < count_ref[...], index_ref[...], -1)
    for d in range(patches):
        column[d] = jnp.broadcast_to(index[:, d : d + 1], (capacity, 128))
    lane = lax.broadcasted_iota(jnp.int32, (4 * capacity, 128), 1)
    loads[2].wait()

    def pick(block):
        near = jnp.concatenate([column[peer(4 * block + j)[1]] for j in range(4)], axis=0)
        hot = [jnp.where(near == lane + 128 * t, 1.0, 0.0) for t in range(pixels // 128)]
        hot = jnp.concatenate(hot, axis=1).astype(jnp.bfloat16)
        found = jnp.dot(hot, sky_ref[...], preferred_element_type=jnp.float32).astype(jnp.bfloat16)
        for j in range(4):
            rows[4 * block + j] = found[capacity * j : capacity * (j + 1)]

    pick(0)
    pl.semaphore_wait(barrier, patches - 1 + SHARERS - 1)
    for j in range(1, 4):
        row_copy(j).start()

    def send(block):
        pick(block)
        for j in range(4):
            row_copy(4 * block + j).start()

    each(1, WINDOW, send)
    inbox[0] = rows[0]

    loads[3].wait()
    loads[4].wait()
    for part in range(pixels // 128):
        pixel = 128 * part + lax.broadcasted_iota(jnp.int32, (128, patches), 0)
        weights = jnp.zeros((128, patches), jnp.float32)
        for j in range(capacity):
            weights = weights + jnp.where(index[j : j + 1, :] == pixel, taper_ref[j : j + 1, :], 0.0)
        whole = jnp.sum(weights, axis=1, keepdims=True)
        weights = weights / jnp.where(whole > 0, whole, 1.0)
        high = weights.astype(jnp.bfloat16).astype(jnp.float32)
        weight_ref[128 * part : 128 * (part + 1), :] = jnp.concatenate([high, weights - high], axis=1).astype(
            jnp.bfloat16
        )

    plain = patches // 4 * 16
    columns = patches // 2 * MODES
    patch = lax.rem(lax.broadcasted_iota(jnp.int32, (2 * patches, columns), 0), patches)
    col = lax.broadcasted_iota(jnp.int32, (2 * patches, columns), 1)
    wide_owner = 16 * lax.div(col, 64) + lax.div(lax.rem(col, 64), 8)
    thin_owner = 16 * lax.div(col - plain, 32) + lax.div(lax.rem(col - plain, 32), 4)
    owner = jnp.where(col < plain, wide_owner, thin_owner)
    cores = (c, 1 - c)
    for k in range(2):
        hot = jnp.where(patch == owner + 8 * cores[k], 1.0, 0.0).astype(jnp.bfloat16)
        spread[k] = jnp.dot(weight_ref[...], hot, preferred_element_type=jnp.float32)

    total[...] = jnp.zeros_like(total)
    tile = 256

    def add(group):
        each(jnp.maximum(8 * group, 1), 8 * group + 8, lambda r: row_copy(r).wait_recv())
        block = inbox[pl.ds(8 * group, 8)].reshape(8 * capacity, channels)
        for t in range(channels // tile):
            part = slice(tile * t, tile * (t + 1))
            total[part, :] += lax.dot_general(
                block[:, part], block, (((0,), (0,)), ((), ())), preferred_element_type=jnp.float32
            )

    def settle(t, value):
        high = value.astype(jnp.bfloat16)
        gram_ref[tile * t : tile * (t + 1), :] = high
        gram_ref[channels + tile * t : channels + tile * (t + 1), :] = (value - high.astype(jnp.float32)).astype(
            jnp.bfloat16
        )

    last = patches // 8 - 2

    def send_on(block):
        first = 4 * (block - WINDOW)
        each(jnp.maximum(first, 1), first + 4, lambda r: row_copy(r).wait_send())
        send(block)

    def send_and_add(group):
        send_on(2 * group + WINDOW)
        send_on(2 * group + WINDOW + 1)
        add(group)

    paired = (patches // 4 - WINDOW) // 2
    each(0, paired, send_and_add)
    each(paired, last, add)
    for t in range(channels // tile):
        settle(t, total[tile * t : tile * (t + 1), :])
    each(8 * last, patches, lambda r: row_copy(r).wait_recv())

    def late_rows():
        return inbox[8 * last :].reshape((patches - 8 * last) * capacity, channels)

    def settle_late():
        block = late_rows()
        for t in range(channels // tile):
            part = slice(tile * t, tile * (t + 1))
            settle(
                t,
                total[part, :]
                + lax.dot_general(
                    block[:, part], block, (((0,), (0,)), ((), ())), preferred_element_type=jnp.float32
                ),
            )

    width = channels // 2

    def sweep(step, wide, late=False, final=False):
        folds, box, sems = (2, exact, (x_send, x_recv)) if wide else (4, short, (s_send, s_recv))
        at = step % 2 if isinstance(step, int) else lax.rem(step, 2)
        box = box.at[at]
        pieces = two_pieces(q_ref[...])
        lhs = jnp.concatenate([pieces, pieces], axis=1)
        if late:
            y = lax.dot_general(
                pieces, late_rows(), (((1,), (1,)), ((), ())), preferred_element_type=jnp.float32
            )
            y = two_pieces(y[:MODES] + y[MODES:])
        copies = []
        for h in range(2):
            z = jnp.dot(lhs, gram_ref[:, width * h : width * (h + 1)], preferred_element_type=jnp.float32)
            if late:
                z = z + jnp.dot(
                    y, late_rows()[:, width * h : width * (h + 1)], preferred_element_type=jnp.float32
                )
            box[me, h] = stacked(z[:MODES] + z[MODES:], folds).astype(box.dtype)
            for o in (2, 1, 3):
                mine = box.at[me, h]
                copies.append(
                    send_to(mine, mine, sems[0].at[at, 4 * h + o], sems[1].at[at, 4 * h + o], {"zp": ring(me, o)})
                )
                copies[-1].start()
        if late:
            settle_late()
            each(patches - 4 * WINDOW, patches, lambda r: row_copy(r).wait_send())
        halves = []
        for h in range(2):
            for one in copies[3 * h : 3 * h + 3]:
                one.wait()
            whole = box[0, h].astype(jnp.float32)
            for k in range(1, SHARERS):
                whole = whole + box[k, h].astype(jnp.float32)
            halves.append(unstacked(whole, folds))
        whole = jnp.concatenate(halves, axis=1)
        q_ref[...] = orthonormal_rows(whole) if final else orthonormal_pairs(whole)

    sweep(0, True, late=True)
    each(1, ITERS - 1, lambda step: sweep(step, False))
    sweep(ITERS - 1, True, final=True)

    fold, thin = width // 2, width // 4
    first, second = ("x", "y"), ("y", "x")
    place = {"x": x, "y": y}

    def pair_at(h, i, o):
        back = {first[h]: ring(place[first[h]], 4 - i), second[h]: ring(place[second[h]], 4 - o)}
        return bases.at[h, back["y"], c, back["x"]]

    def block_of(q):
        wide, rest = q[:8], q[8:]
        return jnp.concatenate(
            [
                jnp.concatenate([wide[:, :fold], wide[:, fold:]], axis=0),
                jnp.concatenate([rest[:, thin * j : thin * (j + 1)] for j in range(4)], axis=0),
            ],
            axis=1,
        )

    def line_at(h, o):
        if h == 0:
            return bases.at[0, ring(y, 4 - o), c]
        return bases.at[1, :, c, ring(x, 4 - o)]

    started = []

    def go(src, sems, at, to):
        one = send_to(src, src, sems[0].at[at], sems[1].at[at], to)
        one.start()
        started.append(one)
        return one

    near = [[[None] * 2 for _ in range(4)] for _ in range(2)]
    far = [[[None] * 4 for _ in range(4)] for _ in range(2)]

    def to_first(h):
        mine = bases.at[h, y, c, x, zl]
        for o in (0, 2, 1, 3):
            for j in range(2):
                if o + j:
                    to = {first[h]: ring(place[first[h]], o), "zl": 1 - zl if j else zl}
                    near[h][o][j] = go(mine, (a_send, a_recv), 8 * h + 2 * o + j, to)

    def to_second(h, i):
        for o in (2, 1, 3):
            to = {second[h]: ring(place[second[h]], o)}
            far[h][i][o] = go(pair_at(h, i, 0), (b_send, b_recv), 16 * h + 4 * i + o, to)

    def across(h, o):
        return go(line_at(h, o), (c_send, c_recv), 4 * h + o, {"core": 1 - c})

    for h in range(2):
        bases[h, y, c, x, zl] = block_of(q_ref[:, width * h : width * (h + 1)]).astype(jnp.bfloat16)
        to_first(h)
    for i in (0, 1, 3, 2):
        for h in range(2):
            for j in range(2):
                if i + j:
                    near[h][i][j].wait_recv()
            to_second(h, i)
    crossed = [across(0, 0), across(1, 0)]
    for o in (1, 3, 2):
        for h in range(2):
            for i in range(4):
                far[h][i][o].wait_recv()
            crossed.append(across(h, o))

    stores = []

    def project(k):
        for h in range(2):
            block = bases[h, :, cores[k]].reshape(patches // 4, 2, 16, fold + thin)
            wide = block[:, :, :, :fold].astype(jnp.float32)
            wide = jnp.concatenate([wide[:, :, :8], wide[:, :, 8:]], axis=3)
            basis[h, :plain] = wide.reshape(plain, width).astype(jnp.bfloat16)
            rest = block[:, :, :, fold:].astype(jnp.float32)
            rest = [
                jnp.concatenate([rest[:, z, 4 * j : 4 * j + 4] for z in range(2)], axis=1) for j in range(4)
            ]
            rest = jnp.concatenate(rest, axis=2)
            basis[h, plain:] = rest.reshape(columns - plain, width).astype(jnp.bfloat16)
        coefficients = sum(
            lax.dot_general(
                sky_ref[:, width * h : width * (h + 1)],
                basis[h],
                (((1,), (1,)), ((), ())),
                preferred_element_type=jnp.float32,
            )
            for h in range(2)
        )
        amounts = two_pieces(spread[k] * coefficients)
        for h in range(2):
            taken = jnp.dot(amounts, basis[h], preferred_element_type=jnp.float32)
            part = slice(width * h, width * (h + 1))
            left = sky_ref[:, part].astype(jnp.float32) if k == 0 else clean_ref[:, part]
            clean_ref[:, part] = left - (taken[:pixels] + taken[pixels:])
            if k == 1:
                stores.append(pltpu.make_async_copy(clean_ref.at[:, part], clean_hbm.at[:, part], out_sem.at[h]))
                stores[h].start()

    project(0)
    for one in crossed:
        one.wait_recv()
    project(1)
    for one in started:
        one.wait_send()
    for store in stores:
        store.wait()


def cleaned(index, count, taper, sky, q0):
    capacity, patches = index.shape
    pixels, channels = sky.shape
    sems = lambda *shape: pltpu.SemaphoreType.DMA(shape)
    return pl.pallas_call(
        clean_kernel,
        out_shape=jax.ShapeDtypeStruct((pixels, channels), jnp.float32),
        in_specs=[pl.BlockSpec(memory_space=pl.ANY)] * 5,
        out_specs=pl.BlockSpec(memory_space=pl.ANY),
        scratch_shapes=[
            pltpu.VMEM((pixels, channels), jnp.float32),
            pltpu.VMEM(index.shape, index.dtype),
            pltpu.VMEM(count.shape, count.dtype),
            pltpu.VMEM(taper.shape, taper.dtype),
            pltpu.VMEM(sky.shape, sky.dtype),
            pltpu.VMEM(q0.shape, q0.dtype),
            pltpu.VMEM((2, 4, 2, 4, 2, 16, channels * 3 // 8), jnp.bfloat16),
            pltpu.VMEM((2, patches // 2 * MODES, channels // 2), jnp.bfloat16),
            pltpu.VMEM((pixels, 2 * patches), jnp.bfloat16),
            pltpu.VMEM((2, pixels, patches // 2 * MODES), jnp.float32),
            pltpu.VMEM((patches, capacity, 128), jnp.int32),
            pltpu.VMEM((patches, capacity, channels), jnp.bfloat16),
            pltpu.VMEM((patches, capacity, channels), jnp.bfloat16),
            pltpu.VMEM((channels, channels), jnp.float32),
            pltpu.VMEM((2 * channels, channels), jnp.bfloat16),
            pltpu.VMEM((2, SHARERS, 2, 2 * MODES, channels // 4), jnp.float32),
            pltpu.VMEM((2, SHARERS, 2, 4 * MODES, channels // 8), jnp.bfloat16),
            sems(5),
            sems(2),
            sems(patches), sems(patches),
            sems(2, 8), sems(2, 8), sems(2, 8), sems(2, 8),
            sems(16), sems(16), sems(32), sems(32), sems(8), sems(8),
        ],
        compiler_params=pltpu.CompilerParams(
            collective_id=0, has_side_effects=True, vmem_limit_bytes=VMEM_MIB * MIB
        ),
    )(index, count, taper, sky, q0)


def copy_kernel(from_ref, to_ref, held, in_sem, out_sem):
    chunks = in_sem.shape[0]
    count = held.shape[0] // chunks
    parts = [pl.ds(count * i, count) for i in range(chunks)]
    loads = [pltpu.make_async_copy(from_ref.at[p], held.at[p], in_sem.at[i]) for i, p in enumerate(parts)]
    stores = [pltpu.make_async_copy(held.at[p], to_ref.at[p], out_sem.at[i]) for i, p in enumerate(parts)]
    for load in loads[:2]:
        load.start()
    for i in range(chunks):
        loads[i].wait()
        stores[i].start()
        if i + 2 < chunks:
            loads[i + 2].start()
    for store in stores:
        store.wait()


def copied(array):
    anywhere = pl.BlockSpec(memory_space=pl.ANY)
    return pl.pallas_call(
        copy_kernel,
        out_shape=jax.ShapeDtypeStruct(array.shape, array.dtype),
        in_specs=[anywhere],
        out_specs=anywhere,
        scratch_shapes=[
            pltpu.VMEM(array.shape, array.dtype),
            pltpu.SemaphoreType.DMA((8,)),
            pltpu.SemaphoreType.DMA((8,)),
        ],
        compiler_params=pltpu.CompilerParams(vmem_limit_bytes=VMEM_MIB * MIB),
    )(array)


def local(sky, send_index, send_count, taper, start_basis):
    patches, capacity = send_index.shape[2:]
    index = send_index.reshape(patches, capacity).T
    count = send_count.reshape(1, patches)
    return copied(cleaned(index, count, taper.reshape(patches, capacity).T, sky, start_basis.T))


def solution(mesh):
    fine = Mesh(mesh.devices.reshape(4, SHARERS, 2, 2, 4), ("y", "zp", "zl", "core", "x"))
    patch = ("y", "zp", "zl", "core")
    rows = P((*patch, "x"), None)
    placed = (rows, P(patch, "x", None, None), P(patch, "x", None), P(patch, "x", None, None), P())
    return jax.shard_map(local, mesh=fine, in_specs=placed, out_specs=rows, check_vma=False)
```
